128 devices in a mesh: band: 8 (over z, core), patch: 16 (over y, x).
Axes of the slice: x: 4, y: 4, z: 4, core: 2. Of those that a mesh axis runs over, the one named last changes fastest.
Arguments:
- grid_feats: bfloat16 [262144, 227], P(('band', 'patch')), may hold values from -6 to 6
- mesh_feats: bfloat16 [32768, 512], P(('band', 'patch')), may hold values from -6 to 6
- cotangent: bfloat16 [32768, 512], P(('band', 'patch')), may hold values from -6 to 6
- w_embed: bfloat16 [227, 512], replicated, may hold values from -0.375 to 0.375
- w_send: bfloat16 [512, 512], replicated, may hold values from -0.25 to 0.25
- w_recv: bfloat16 [512, 512], replicated, may hold values from -0.25 to 0.25
- w_out: bfloat16 [512, 512], replicated, may hold values from -0.0625 to 0.0625
- u_src: bfloat16 [256, 512], replicated, may hold values from -0.375 to 0.375
- u_dst: bfloat16 [256, 512], replicated, may hold values from -0.375 to 0.375
- u_out: bfloat16 [512, 256], replicated, may hold values from -0.09375 to 0.09375
- v_in: bfloat16 [256, 512], replicated, may hold values from -0.375 to 0.375
- v_out: bfloat16 [512, 256], replicated, may hold values from -0.25 to 0.25
- send_rows: int32 [128, 2048], P(('band', 'patch')), may hold values from 0 to 2047, as said below
- enc_src: int32 [128, 4096], P(('band', 'patch')), may hold values from 0 to 2047, as said below
- enc_dst: int32 [128, 4096], P(('band', 'patch')), may hold values from -1 to 255, as said below
- halo_send: int32 [128, 2, 2, 32], P(('band', 'patch')), may hold values from 0 to 255, as said below
- mesh_src: int32 [128, 2048], P(('band', 'patch')), may hold values from 0 to 383, as said below
- mesh_dst: int32 [128, 2048], P(('band', 'patch')), may hold values from -1 to 255, as said below
Outputs:
- grid_grad: bfloat16 [262144, 227], P(('band', 'patch'))
- mesh_grad: float32 [32768, 512], P(('band', 'patch'))
- grad_w_embed: float32 [227, 512], replicated
- grad_w_send: float32 [512, 512], replicated
- grad_w_recv: float32 [512, 512], replicated
- grad_w_out: float32 [512, 512], replicated
- grad_u_src: float32 [256, 512], replicated
- grad_u_dst: float32 [256, 512], replicated
- grad_u_out: float32 [512, 256], replicated
- grad_v_in: float32 [256, 512], replicated
- grad_v_out: float32 [512, 256], replicated
The draws below stay inside these ranges and needn't reach their ends.
Inputs may be any that keep to these rules, and one draw needn't show every extreme that they name: Each send_rows[d] names each of the device's 2048 local grid rows exactly once. `enc_src`: index into the device's received grid rows; the first 2048 slots name each received row once and are live. `enc_dst`: local mesh node of a live slot, -1 for an empty slot; empty slots follow all live ones of a device; some device has all 4096 slots live. halo_send[d, 0, 0] and [d, 0, 1] go to the band neighbour below and above, [d, 1, 0] and [d, 1, 1] to the patch neighbours below and above. `mesh_src`: row of the halo table: own 256 nodes, then the blocks from band - 1, band + 1, patch - 1, patch + 1; the first 128 slots name each received row once and are live. `mesh_dst`: local receiver of a live slot, -1 for an empty slot; empty slots follow all live ones of a device; some device has all 2048 slots live.
All inputs are finite; a program needn't handle non-finite values.
Results may differ from the reference program's by a relative error of at most 0.025.
Values may be sent and summed in bfloat16 or wider, within the bound.
No kernel may reach another device: no remote copies, remote signals or barrier semaphores. Data moves between devices by JAX's collectives and lax.ppermute only.
A program may use at most 128 MiB of HBM per device.

```python
import jax
import jax.numpy as jnp
from jax import lax

C = 227
D = 512
HALF = 256
G_DEV = 2048
M_DEV = 256
HS = 32
RIM = 128
KEEP = 1536
ENC_CAP = 4096
MESH_CAP = 2048
NG = 262144
NM = 32768
N_BAND = 8
N_PATCH = 16
DEVICES = 128


def live_counts(key, capacity):
    counts = jax.random.randint(key, (DEVICES,), capacity * 3 // 4, capacity + 1)
    fullest = jax.random.randint(jax.random.fold_in(key, 7), (), 0, DEVICES)
    return jnp.where(jnp.arange(DEVICES) == fullest, capacity, counts)


def shuffled(key, count):

    def single(subkey):
        return jax.random.permutation(subkey, count)
    return jax.vmap(single)(jax.random.split(key, DEVICES))


def draw_send_rows(key, part):
    key = jax.random.fold_in(key, 1)
    return shuffled(key, G_DEV).astype(jnp.int32)


def draw_enc_src(key, part):
    key = jax.random.fold_in(key, 2)
    first = shuffled(jax.random.fold_in(key, 1), G_DEV)
    rest = jax.random.randint(jax.random.fold_in(key, 2), (DEVICES, ENC_CAP - G_DEV), 0, G_DEV)
    return jnp.concatenate([first, rest], axis=1).astype(jnp.int32)


def draw_enc_dst(key, part):
    key = jax.random.fold_in(key, 3)
    nodes = jax.random.randint(jax.random.fold_in(key, 1), (DEVICES, ENC_CAP), 0, M_DEV)
    counts = live_counts(jax.random.fold_in(key, 2), ENC_CAP)
    return jnp.where(jnp.arange(ENC_CAP)[None, :] < counts[:, None], nodes, -1).astype(jnp.int32)


def draw_halo_send(key, part):
    key = jax.random.fold_in(key, 4)
    return jax.random.randint(key, (DEVICES, 2, 2, HS), 0, M_DEV).astype(jnp.int32)


def draw_mesh_src(key, part):
    key = jax.random.fold_in(key, 5)
    first = M_DEV + shuffled(jax.random.fold_in(key, 1), 4 * HS)
    rest = jax.random.randint(jax.random.fold_in(key, 2), (DEVICES, MESH_CAP - 4 * HS), 0, M_DEV + 4 * HS)
    return jnp.concatenate([first, rest], axis=1).astype(jnp.int32)


def draw_mesh_dst(key, part):
    key = jax.random.fold_in(key, 6)
    nodes = jax.random.randint(jax.random.fold_in(key, 1), (DEVICES, MESH_CAP), 0, M_DEV)
    counts = live_counts(jax.random.fold_in(key, 2), MESH_CAP)
    return jnp.where(jnp.arange(MESH_CAP)[None, :] < counts[:, None], nodes, -1).astype(jnp.int32)


def levels(key, shape, pieces, smallest, high):
    def one(position, blocks):
        draws = jax.random.uniform(jax.random.fold_in(jax.random.fold_in(key, 6), position), (blocks,), jnp.float32, smallest / len(pieces), high / len(pieces))
        return jnp.repeat(jnp.exp(draws), shape[position] // blocks).reshape((-1,) + (1,) * (len(shape) - position - 1))

    level = one(*pieces[0])
    for cut in pieces[1:]:
        level = level * one(*cut)
    return level


def noise(stream_key, shape, deviation, reach, pieces=(), kind=jnp.bfloat16):
    level = levels(stream_key, shape, pieces, -0.22, 0.18) if pieces else 1.0
    drawn = jax.random.normal(stream_key, shape, jnp.float32) * deviation * level
    return jnp.minimum(jnp.maximum(drawn, -reach), reach).astype(kind)


def setup_inputs(seed: int = 0) -> dict:
    streams_of = jax.random.split(jax.random.key(seed), 19)
    return {
        "grid_feats": noise(streams_of[0], (NG, C), 1.0, 6.0, ((0, 128),)),
        "mesh_feats": noise(streams_of[1], (NM, D), 1.0, 6.0, ((0, 128),)),
        "cotangent": noise(streams_of[2], (NM, D), 1.0, 6.0, ((0, 128),)),
        "w_embed": noise(streams_of[3], (C, D), C ** -0.5, 0.375),
        "w_send": noise(streams_of[4], (D, D), D ** -0.5, 0.25),
        "w_recv": noise(streams_of[5], (D, D), D ** -0.5, 0.25),
        "w_out": noise(streams_of[6], (D, D), (D * 16) ** -0.5, 0.0625),
        "u_src": noise(streams_of[7], (HALF, D), HALF ** -0.5, 0.375),
        "u_dst": noise(streams_of[8], (HALF, D), HALF ** -0.5, 0.375),
        "u_out": noise(streams_of[9], (D, HALF), (D * 8) ** -0.5, 0.09375),
        "v_in": noise(streams_of[10], (HALF, D), HALF ** -0.5, 0.375),
        "v_out": noise(streams_of[11], (D, HALF), D ** -0.5, 0.25),
        "send_rows": draw_send_rows(jax.random.fold_in(streams_of[18], 71), 0),
        "enc_src": draw_enc_src(jax.random.fold_in(streams_of[18], 71), 0),
        "enc_dst": draw_enc_dst(jax.random.fold_in(streams_of[18], 71), 0),
        "halo_send": draw_halo_send(jax.random.fold_in(streams_of[18], 71), 0),
        "mesh_src": draw_mesh_src(jax.random.fold_in(streams_of[18], 71), 0),
        "mesh_dst": draw_mesh_dst(jax.random.fold_in(streams_of[18], 71), 0),
    }


def silu_grad(value):
    sigma = jax.nn.sigmoid(value)
    return sigma * (1.0 + value * (1.0 - sigma))

def node_table(index, count):
    return (jnp.arange(count, dtype=jnp.int32)[:, None] == index[None, :]).astype(jnp.bfloat16)

def matmul(left, right):
    return jnp.dot(left, right, preferred_element_type=jnp.float32)

def inner_left(left, right):
    return lax.dot_general(left, right, (((0,), (0,)), ((), ())), preferred_element_type=jnp.float32)

def outer_right(left, right):
    return lax.dot_general(left, right, (((1,), (1,)), ((), ())), preferred_element_type=jnp.float32)

def embed_rows(grid_rows, w_embed):
    embed_pre = matmul(grid_rows, w_embed)
    return (embed_pre, jax.nn.silu(embed_pre).astype(jnp.bfloat16))

def embed_back(grid_rows, embed_pre, embedded_grad, w_embed):
    embed_grad = (embedded_grad.astype(jnp.float32) * silu_grad(embed_pre)).astype(jnp.bfloat16)
    return (inner_left(grid_rows, embed_grad), outer_right(embed_grad, w_embed).astype(jnp.bfloat16))

def encoder_edges(embedded, mesh_rows, w_send, w_recv, w_out, sources, targets):
    sender_part = matmul(embedded, w_send)
    node_part = matmul(mesh_rows, w_recv)
    active = targets >= 0
    clipped = jnp.maximum(targets, 0)
    edge_pre = jnp.take(sender_part, sources, axis=0) + jnp.take(node_part, clipped, axis=0)
    message = jnp.where(active[:, None], jax.nn.silu(edge_pre), 0.0).astype(jnp.bfloat16)
    incidence = node_table(targets, mesh_rows.shape[0])
    gathered = matmul(incidence, message).astype(jnp.bfloat16)
    latent = (mesh_rows.astype(jnp.float32) + matmul(gathered, w_out)).astype(jnp.bfloat16)
    return (edge_pre, gathered, latent, incidence, active)

def encoder_back(embedded, mesh_rows, w_send, w_recv, w_out, sources, targets, edge_pre, gathered, incidence, active, latent_grad):
    grad_out = inner_left(gathered, latent_grad)
    gathered_grad = outer_right(latent_grad, w_out)
    clipped = jnp.maximum(targets, 0)
    enc_edge_grad = jnp.where(active[:, None], jnp.take(gathered_grad, clipped, axis=0) * silu_grad(edge_pre), 0.0).astype(jnp.bfloat16)
    node_grad = matmul(incidence, enc_edge_grad).astype(jnp.bfloat16)
    sender_grad = jnp.zeros((embedded.shape[0], embedded.shape[1]), jnp.float32).at[sources].add(enc_edge_grad.astype(jnp.float32)).astype(jnp.bfloat16)
    grad_recv = inner_left(mesh_rows, node_grad)
    grad_send = inner_left(embedded, sender_grad)
    mesh_grad = latent_grad.astype(jnp.float32) + outer_right(node_grad, w_recv)
    embedded_grad = outer_right(sender_grad, w_send).astype(jnp.bfloat16)
    return (mesh_grad, embedded_grad, (grad_send, grad_recv, grad_out))

def mesh_pass(halo_table, latent, cot_rows, u_src, u_dst, u_out, v_in, v_out, sources, targets):
    half = latent.shape[1] // 2
    nodes = latent.shape[0]
    upper = latent[:, :half]
    lower = latent[:, half:]
    source_part = matmul(halo_table, u_src)
    target_part = matmul(lower, u_dst)
    active = targets >= 0
    clipped = jnp.maximum(targets, 0)
    mesh_pre = jnp.take(source_part, sources, axis=0) + jnp.take(target_part, clipped, axis=0)
    mesh_msg = jnp.where(active[:, None], jax.nn.silu(mesh_pre), 0.0).astype(jnp.bfloat16)
    incidence = node_table(targets, nodes)
    summed = matmul(incidence, mesh_msg).astype(jnp.bfloat16)
    coupled = (upper.astype(jnp.float32) + matmul(summed, u_out)).astype(jnp.bfloat16)
    hidden_pre = matmul(coupled, v_in)
    hidden_act = jax.nn.silu(hidden_pre).astype(jnp.bfloat16)
    upper_cot = cot_rows[:, :half]
    lower_cot = cot_rows[:, half:]
    hidden_grad = (outer_right(lower_cot, v_out) * silu_grad(hidden_pre)).astype(jnp.bfloat16)
    grad_v_out = inner_left(hidden_act, lower_cot)
    grad_v_in = inner_left(coupled, hidden_grad)
    coupled_grad = (upper_cot.astype(jnp.float32) + outer_right(hidden_grad, v_in)).astype(jnp.bfloat16)
    grad_u_out = inner_left(summed, coupled_grad)
    summed_grad = outer_right(coupled_grad, u_out)
    mesh_edge_grad = jnp.where(active[:, None], jnp.take(summed_grad, clipped, axis=0) * silu_grad(mesh_pre), 0.0).astype(jnp.bfloat16)
    target_grad = matmul(incidence, mesh_edge_grad).astype(jnp.bfloat16)
    source_grad = jnp.zeros((halo_table.shape[0], source_part.shape[1]), jnp.float32).at[sources].add(mesh_edge_grad.astype(jnp.float32)).astype(jnp.bfloat16)
    grad_u_dst = inner_left(lower, target_grad)
    grad_u_src = inner_left(halo_table, source_grad)
    table_grad = outer_right(source_grad, u_src)
    lower_grad = lower_cot.astype(jnp.float32) + outer_right(target_grad, u_dst) + table_grad[:nodes]
    halo_grad = table_grad[nodes:].astype(jnp.bfloat16)
    return (coupled_grad, lower_grad, halo_grad, (grad_u_src, grad_u_dst, grad_u_out, grad_v_in, grad_v_out))

def halo_index(halo_send):
    device_ids = jnp.arange(DEVICES, dtype=jnp.int32)
    band_ids = device_ids // N_PATCH
    patch_ids = device_ids % N_PATCH
    lower_band = jnp.maximum(device_ids - N_PATCH, 0)
    upper_band = jnp.minimum(device_ids + N_PATCH, DEVICES - 1)
    west_patch = band_ids * N_PATCH + (patch_ids + N_PATCH - 1) % N_PATCH
    east_patch = band_ids * N_PATCH + (patch_ids + 1) % N_PATCH
    blocks = [lower_band[:, None] * M_DEV + halo_send[lower_band, 0, 1], upper_band[:, None] * M_DEV + halo_send[upper_band, 0, 0], west_patch[:, None] * M_DEV + halo_send[west_patch, 1, 1], east_patch[:, None] * M_DEV + halo_send[east_patch, 1, 0]]
    ones = jnp.ones((DEVICES, HS), dtype=bool)
    present = [ones & (band_ids > 0)[:, None], ones & (band_ids < N_BAND - 1)[:, None], ones, ones]
    return (jnp.concatenate(blocks, axis=1).astype(jnp.int32), jnp.concatenate(present, axis=1))

def received_rows(send_rows):
    device_ids = jnp.arange(DEVICES, dtype=jnp.int32)
    band_ids = device_ids // N_PATCH
    patch_ids = device_ids % N_PATCH
    below = jnp.where(band_ids > 0, device_ids - N_PATCH, device_ids)
    above = jnp.where(band_ids < N_BAND - 1, device_ids + N_PATCH, device_ids)
    west_patch = band_ids * N_PATCH + (patch_ids + N_PATCH - 1) % N_PATCH
    east_patch = band_ids * N_PATCH + (patch_ids + 1) % N_PATCH

    def block(source, which):
        start = KEEP + which * RIM
        return source[:, None] * G_DEV + send_rows[source][:, start:start + RIM]
    from_below = jnp.where((band_ids > 0)[:, None], block(below, 1), block(device_ids, 0))
    from_above = jnp.where((band_ids < N_BAND - 1)[:, None], block(above, 0), block(device_ids, 1))
    kept = device_ids[:, None] * G_DEV + send_rows[:, :KEEP]
    return jnp.concatenate([kept, from_below, from_above, block(west_patch, 3), block(east_patch, 2)], axis=1).astype(jnp.int32)

def reference(grid_feats, mesh_feats, cotangent, w_embed, w_send, w_recv, w_out, u_src, u_dst, u_out, v_in, v_out, send_rows, enc_src, enc_dst, halo_send, mesh_src, mesh_dst):
    received = received_rows(send_rows)
    mesh_blocks = mesh_feats.reshape(DEVICES, M_DEV, D)
    cot_blocks = cotangent.reshape(DEVICES, M_DEV, D)

    def encode_one(inputs):
        rows, mesh_rows, sources, targets = inputs
        grid_rows = jnp.take(grid_feats, rows, axis=0)
        embed_pre, embedded = embed_rows(grid_rows, w_embed)
        return encoder_edges(embedded, mesh_rows, w_send, w_recv, w_out, sources, targets)[2]
    latent = lax.map(encode_one, (received, mesh_blocks, enc_src, enc_dst))
    lower_all = latent[:, :, HALF:].reshape(NM, HALF)
    index, present = halo_index(halo_send)
    halo_rows = jnp.where(present[:, :, None], jnp.take(lower_all, index, axis=0), 0.0).astype(jnp.bfloat16)
    tables = jnp.concatenate([latent[:, :, HALF:], halo_rows], axis=1)
    zero_mesh = (jnp.zeros((HALF, D), jnp.float32), jnp.zeros((HALF, D), jnp.float32), jnp.zeros((D, HALF), jnp.float32), jnp.zeros((HALF, D), jnp.float32), jnp.zeros((D, HALF), jnp.float32))

    def mesh_one(carry, inputs):
        halo_table, latent_rows, cot_rows, sources, targets = inputs
        coupled_grad, lower_grad, halo_grad, grads = mesh_pass(halo_table, latent_rows, cot_rows, u_src, u_dst, u_out, v_in, v_out, sources, targets)
        return (tuple((a + b for a, b in zip(carry, grads))), (coupled_grad, lower_grad, halo_grad))
    mesh_sums, (coupled_grads, lower_grads, halo_grads) = lax.scan(mesh_one, zero_mesh, (tables, latent, cot_blocks, mesh_src, mesh_dst))
    drop_index = jnp.where(present, index, NM).reshape(-1)
    lower_flat = lower_grads.reshape(NM, HALF).at[drop_index].add(halo_grads.reshape(-1, HALF).astype(jnp.float32), mode='drop')
    lower_blocks = lower_flat.reshape(DEVICES, M_DEV, HALF)
    zero_enc = (jnp.zeros((C, D), jnp.float32), jnp.zeros((D, D), jnp.float32), jnp.zeros((D, D), jnp.float32), jnp.zeros((D, D), jnp.float32))

    def back_one(carry, inputs):
        rows, mesh_rows, sources, targets, coupled_grad, lower_grad = inputs
        grid_rows = jnp.take(grid_feats, rows, axis=0)
        embed_pre, embedded = embed_rows(grid_rows, w_embed)
        edge_pre, gathered, latent_rows, incidence, active = encoder_edges(embedded, mesh_rows, w_send, w_recv, w_out, sources, targets)
        latent_grad = jnp.concatenate([coupled_grad.astype(jnp.float32), lower_grad], axis=1).astype(jnp.bfloat16)
        mesh_grad, embedded_grad, grads = encoder_back(embedded, mesh_rows, w_send, w_recv, w_out, sources, targets, edge_pre, gathered, incidence, active, latent_grad)
        grad_embed, row_grad = embed_back(grid_rows, embed_pre, embedded_grad, w_embed)
        carry = (carry[0] + grad_embed, carry[1] + grads[0], carry[2] + grads[1], carry[3] + grads[2])
        return (carry, (mesh_grad, row_grad))
    enc_sums, (mesh_grads, row_grads) = lax.scan(back_one, zero_enc, (received, mesh_blocks, enc_src, enc_dst, coupled_grads, lower_blocks))
    grid_grad = jnp.zeros((NG, C), jnp.bfloat16).at[received.reshape(-1)].set(row_grads.reshape(-1, C))
    mesh_grad = mesh_grads.reshape(NM, D)
    return (grid_grad, mesh_grad, enc_sums[0], enc_sums[1], enc_sums[2], enc_sums[3], mesh_sums[0], mesh_sums[1], mesh_sums[2], mesh_sums[3], mesh_sums[4])
```

```python
import jax
import jax.numpy as jnp
from jax import lax
from jax.experimental import pallas as pl
from jax.experimental.pallas import tpu as pltpu
from jax.sharding import PartitionSpec as P

BF16 = jnp.bfloat16
F32 = jnp.float32
LANES = 128
EDGE_TILE = 512
ROW_TILE = 512
VMEM_LIMIT = 56 * 1024 * 1024


def mm(left, right):
    return lax.dot_general(left, right, (((1,), (0,)), ((), ())), preferred_element_type=F32)


def mm_left(left, right):
    return lax.dot_general(left, right, (((0,), (0,)), ((), ())), preferred_element_type=F32)


def mm_right(left, right):
    return lax.dot_general(left, right, (((1,), (1,)), ((), ())), preferred_element_type=F32)


def table_by_row(index, count):
    n = index.shape[1]
    rows = lax.broadcasted_iota(jnp.int32, (count, n), 0)
    return jnp.where(rows == index, 1.0, 0.0).astype(BF16)


def table_by_column(index, count):
    n = index.shape[1]
    parts = []
    for start in range(0, n, LANES):
        width = min(LANES, n - start)
        piece = jnp.broadcast_to(index[:, start : start + width], (LANES, width))
        column = jnp.transpose(piece)
        wide = jnp.concatenate([column] * (count // LANES), axis=1)
        columns = lax.broadcasted_iota(jnp.int32, (width, count), 1)
        parts.append(jnp.where(wide == columns, 1.0, 0.0).astype(BF16))
    return parts[0] if len(parts) == 1 else jnp.concatenate(parts, axis=0)


def silu_both(value):
    sigma = 0.5 * jnp.tanh(0.5 * value) + 0.5
    act = value * sigma
    return act, sigma + act * (1.0 - sigma)


def call(kernel, out_shape, **more):
    return pl.pallas_call(
        kernel,
        out_shape=out_shape,
        compiler_params=pltpu.CompilerParams(vmem_limit_bytes=VMEM_LIMIT),
        **more,
    )


def shape(dims, kind):
    return jax.ShapeDtypeStruct(tuple(dims), kind)


def pick_rim_kernel(order_ref, grid_ref, *out_refs):
    rim = out_refs[0].shape[1]
    keep = order_ref.shape[1] - 4 * rim
    table = table_by_row(order_ref[:, keep:], grid_ref.shape[1])
    picked = mm(grid_ref[...], table).astype(BF16)
    for k in range(4):
        out_refs[k][...] = picked[:, k * rim : (k + 1) * rim]


def keep_kernel(order_ref, grid_ref, mesh_ref, embed_ref, send_ref, recv_ref, rows_ref, sender_ref, node_ref):
    keep = rows_ref.shape[1]
    node_ref[...] = mm(mesh_ref[...], recv_ref[...]).astype(BF16)

    def step(i, carry):
        start = pl.multiple_of(i * ROW_TILE, ROW_TILE)
        table = table_by_row(order_ref[:, pl.ds(start, ROW_TILE)], grid_ref.shape[1])
        rows = mm(grid_ref[...], table).astype(BF16)
        rows_ref[:, pl.ds(start, ROW_TILE)] = rows
        embedded = silu_both(mm_left(rows, embed_ref[...]))[0].astype(BF16)
        sender_ref[pl.ds(start, ROW_TILE), :] = mm(embedded, send_ref[...]).astype(BF16)
        return carry

    lax.fori_loop(0, keep // ROW_TILE, step, 0)


def encode_kernel(
    flag_ref, src_ref, dst_ref, halo_ref, sender_ref, node_ref, mesh_ref, embed_ref, send_ref, out_w_ref,
    in0, in1, in2, in3, own0, own1,
    rim_ref, slope_ref, gathered_ref, latent_ref, h00, h01, h10, h11,
    table, total,
):
    step = pl.program_id(0)
    keep = sender_ref.shape[0]
    rim = in0.shape[1]
    rows = keep + 4 * rim
    nodes = node_ref.shape[0]

    @pl.when(step == 0)
    def _():
        table[0:keep, :] = sender_ref[...]
        table[rows : rows + nodes, :] = node_ref[...]
        rim_ref[:, 0:rim] = jnp.where(flag_ref[0] > 0, in0[...], own0[...])
        rim_ref[:, rim : 2 * rim] = jnp.where(flag_ref[1] > 0, in1[...], own1[...])
        rim_ref[:, 2 * rim : 3 * rim] = in2[...]
        rim_ref[:, 3 * rim : 4 * rim] = in3[...]
        embedded = silu_both(mm_left(rim_ref[...], embed_ref[...]))[0].astype(BF16)
        table[keep:rows, :] = mm(embedded, send_ref[...]).astype(BF16)
        total[...] = jnp.zeros_like(total)

    both = jnp.concatenate([table_by_column(src_ref[...], rows), table_by_column(dst_ref[...], nodes)], axis=1)
    act, slope = silu_both(mm(both, table[...]))
    slope_ref[...] = slope.astype(BF16)
    total[...] += mm(table_by_row(dst_ref[...], nodes), act.astype(BF16))

    @pl.when(step == pl.num_programs(0) - 1)
    def _():
        gathered = total[...].astype(BF16)
        gathered_ref[...] = gathered
        latent = (mesh_ref[...].astype(F32) + mm(gathered, out_w_ref[...])).astype(BF16)
        latent_ref[...] = latent
        lower = latent[:, latent.shape[1] // 2 :]
        for a, b, ref in ((0, 0, h00), (0, 1, h01), (1, 0, h10), (1, 1, h11)):
            pick = table_by_row(halo_ref[0, a, b : b + 1, :], nodes)
            ref[...] = mm_left(pick, lower).astype(BF16)


def mesh_kernel(
    src_ref, dst_ref, latent_ref, cot_ref, b0, b1, b2, b3, u_src_ref, u_dst_ref, u_out_ref, v_in_ref, v_out_ref,
    g0, g1, g2, g3, coupled_grad_ref, lower_grad_ref, halo_table_ref, ends_ref, summed_ref, coupled_ref, hidden_ref, hidden_grad_ref,
    table, slope_s, total, ends,
):
    nodes = latent_ref.shape[0]
    half = latent_ref.shape[1] // 2
    width = b0.shape[0]
    rows = nodes + 4 * width
    upper = latent_ref[:, :half]
    lower = latent_ref[:, half:]
    halo_table_ref[0:nodes, :] = lower
    for k, ref in enumerate((b0, b1, b2, b3)):
        halo_table_ref[nodes + k * width : nodes + (k + 1) * width, :] = ref[...]
    table[0:rows, :] = mm(halo_table_ref[...], u_src_ref[...]).astype(BF16)
    table[rows : rows + nodes, :] = mm(lower, u_dst_ref[...]).astype(BF16)
    total[...] = jnp.zeros_like(total)
    ends[...] = jnp.zeros_like(ends)
    steps = src_ref.shape[1] // EDGE_TILE

    def forward(i, carry):
        start = pl.multiple_of(i * EDGE_TILE, EDGE_TILE)
        src = src_ref[:, pl.ds(start, EDGE_TILE)]
        dst = dst_ref[:, pl.ds(start, EDGE_TILE)]
        both = jnp.concatenate([table_by_column(src, rows), table_by_column(dst, nodes)], axis=1)
        act, slope = silu_both(mm(both, table[...]))
        slope_s[pl.ds(start, EDGE_TILE), :] = slope.astype(BF16)
        total[...] += mm(table_by_row(dst, nodes), act.astype(BF16))
        return carry

    lax.fori_loop(0, steps, forward, 0)
    summed = total[...].astype(BF16)
    summed_ref[...] = summed
    coupled = (upper.astype(F32) + mm(summed, u_out_ref[...])).astype(BF16)
    coupled_ref[...] = coupled
    act, slope = silu_both(mm(coupled, v_in_ref[...]))
    hidden_ref[...] = act.astype(BF16)
    upper_cot = cot_ref[:, :half]
    lower_cot = cot_ref[:, half:]
    hidden_grad = (mm_right(lower_cot, v_out_ref[...]) * slope).astype(BF16)
    hidden_grad_ref[...] = hidden_grad
    coupled_grad = (upper_cot.astype(F32) + mm_right(hidden_grad, v_in_ref[...])).astype(BF16)
    coupled_grad_ref[...] = coupled_grad
    summed_grad = mm_right(coupled_grad, u_out_ref[...]).astype(BF16)

    def backward(i, carry):
        start = pl.multiple_of(i * EDGE_TILE, EDGE_TILE)
        src = src_ref[:, pl.ds(start, EDGE_TILE)]
        dst = dst_ref[:, pl.ds(start, EDGE_TILE)]
        grad = mm(table_by_column(dst, nodes), summed_grad) * slope_s[pl.ds(start, EDGE_TILE), :].astype(F32)
        both = jnp.concatenate([table_by_row(src, rows), table_by_row(dst, nodes)], axis=0)
        ends[...] += mm(both, grad.astype(BF16))
        return carry

    lax.fori_loop(0, steps, backward, 0)
    ends_ref[...] = ends[...].astype(BF16)
    source_grad = ends_ref[0:rows, :]
    target_grad = ends_ref[rows : rows + nodes, :]
    table_grad = mm_right(source_grad, u_src_ref[...])
    lower_grad_ref[...] = lower_cot.astype(F32) + mm_right(target_grad, u_dst_ref[...]) + table_grad[0:nodes, :]
    for k, ref in enumerate((g0, g1, g2, g3)):
        ref[...] = table_grad[nodes + k * width : nodes + (k + 1) * width, :].astype(BF16)


def mesh_weight_kernel(
    halo_table_ref, ends_ref, summed_ref, coupled_ref, hidden_ref, hidden_grad_ref, coupled_grad_ref, cot_ref,
    u_src_ref, u_dst_ref, u_out_ref, v_in_ref, v_out_ref,
):
    rows = halo_table_ref.shape[0]
    nodes, half = coupled_ref.shape
    u_src_ref[...] = mm_left(halo_table_ref[...], ends_ref[0:rows, :])
    u_dst_ref[...] = mm_left(halo_table_ref[0:nodes, :], ends_ref[rows : rows + nodes, :])
    u_out_ref[...] = mm_left(summed_ref[...], coupled_grad_ref[...])
    v_in_ref[...] = mm_left(coupled_ref[...], hidden_grad_ref[...])
    v_out_ref[...] = mm_left(hidden_ref[...], cot_ref[:, half:])


def encoder_back_kernel(
    src_ref, dst_ref, halo_ref, slope_ref, keep_rows_ref, rim_rows_ref, gathered_ref, mesh_ref,
    coupled_grad_ref, lower_grad_ref, r0, r1, r2, r3, embed_ref, send_ref, recv_ref, out_w_ref,
    keep_grad_ref, g0, g1, g2, g3, mesh_grad_ref, grad_embed_ref, grad_send_ref, grad_recv_ref, grad_out_ref,
    edge_s, latent_s, nodes_s,
):
    nodes = mesh_ref.shape[0]
    keep = keep_rows_ref.shape[1]
    rim = g0.shape[1]
    lower_grad = lower_grad_ref[...]
    for a, b, ref in ((0, 0, r0), (0, 1, r1), (1, 0, r2), (1, 1, r3)):
        lower_grad += mm(table_by_row(halo_ref[0, a, b : b + 1, :], nodes), ref[...])
    half = lower_grad.shape[1]
    latent_s[:, :half] = coupled_grad_ref[...]
    latent_s[:, half:] = lower_grad.astype(BF16)
    latent_grad = latent_s[...]
    grad_out_ref[...] = mm_left(gathered_ref[...], latent_grad)
    gathered_grad = mm_right(latent_grad, out_w_ref[...]).astype(BF16)
    nodes_s[...] = jnp.zeros_like(nodes_s)

    def edges(i, carry):
        start = pl.multiple_of(i * EDGE_TILE, EDGE_TILE)
        dst = dst_ref[:, pl.ds(start, EDGE_TILE)]
        grad = mm(table_by_column(dst, nodes), gathered_grad) * slope_ref[pl.ds(start, EDGE_TILE), :].astype(F32)
        grad = grad.astype(BF16)
        edge_s[pl.ds(start, EDGE_TILE), :] = grad
        nodes_s[...] += mm(table_by_row(dst, nodes), grad)
        return carry

    lax.fori_loop(0, src_ref.shape[1] // EDGE_TILE, edges, 0)
    node_grad = nodes_s[...].astype(BF16)
    grad_recv_ref[...] = mm_left(mesh_ref[...], node_grad)
    mesh_grad_ref[...] = latent_grad.astype(F32) + mm_right(node_grad, recv_ref[...])
    grad_embed_ref[...] = jnp.zeros_like(grad_embed_ref)
    grad_send_ref[...] = jnp.zeros_like(grad_send_ref)

    def back(rows, start, count):
        ids = lax.broadcasted_iota(jnp.int32, (count, src_ref.shape[1]), 0) + start
        table = jnp.where(ids == src_ref[...], 1.0, 0.0).astype(BF16)
        sender_grad = mm(table, edge_s[...]).astype(BF16)
        act, slope = silu_both(mm_left(rows, embed_ref[...]))
        grad_send_ref[...] += mm_left(act.astype(BF16), sender_grad)
        embedded_grad = mm_right(sender_grad, send_ref[...]).astype(BF16)
        embed_grad = (embedded_grad.astype(F32) * slope).astype(BF16)
        grad_embed_ref[...] += mm(rows, embed_grad)
        return mm_right(embed_ref[...], embed_grad).astype(BF16)

    rim_grad = back(rim_rows_ref[...], keep, 4 * rim)
    for k, ref in enumerate((g0, g1, g2, g3)):
        ref[...] = rim_grad[:, k * rim : (k + 1) * rim]

    def kept(i, carry):
        start = pl.multiple_of(i * ROW_TILE, ROW_TILE)
        keep_grad_ref[:, pl.ds(start, ROW_TILE)] = back(keep_rows_ref[:, pl.ds(start, ROW_TILE)], start, ROW_TILE)
        return carry

    lax.fori_loop(0, keep // ROW_TILE, kept, 0)


def place_kernel(flag_ref, order_ref, keep_ref, in0, in1, in2, in3, own0, own1, grid_grad_ref, all_s):
    keep = keep_ref.shape[1]
    rim = in0.shape[1]
    all_s[:, 0:keep] = keep_ref[...]
    all_s[:, keep : keep + rim] = jnp.where(flag_ref[0] > 0, in0[...], own0[...])
    all_s[:, keep + rim : keep + 2 * rim] = jnp.where(flag_ref[1] > 0, in1[...], own1[...])
    all_s[:, keep + 2 * rim : keep + 3 * rim] = in2[...]
    all_s[:, keep + 3 * rim : keep + 4 * rim] = in3[...]

    def place(i, carry):
        start = pl.multiple_of(i * ROW_TILE, ROW_TILE)
        ids = lax.broadcasted_iota(jnp.int32, (ROW_TILE, order_ref.shape[1]), 0) + start
        table = jnp.where(ids == order_ref[...], 1.0, 0.0).astype(BF16)
        grid_grad_ref[:, pl.ds(start, ROW_TILE)] = mm_right(all_s[...], table).astype(BF16)
        return carry

    lax.fori_loop(0, grid_grad_ref.shape[1] // ROW_TILE, place, 0)


def trade(below, above, west, east):
    bands = lax.axis_size("band")
    patches = lax.axis_size("patch")
    up = [(i, i + 1) for i in range(bands - 1)]
    down = [(i + 1, i) for i in range(bands - 1)]
    right = [(i, (i + 1) % patches) for i in range(patches)]
    left = [((i + 1) % patches, i) for i in range(patches)]
    return (
        lax.ppermute(above, "band", up),
        lax.ppermute(below, "band", down),
        lax.ppermute(east, "patch", right),
        lax.ppermute(west, "patch", left),
    )


def body(
    grid_feats, mesh_feats, cotangent, w_embed, w_send, w_recv, w_out, u_src, u_dst, u_out, v_in, v_out,
    send_rows, enc_src, enc_dst, halo_send, mesh_src, mesh_dst,
):
    chans = grid_feats.shape[1]
    grid_rows = grid_feats.shape[0]
    nodes, dim = mesh_feats.shape
    half = dim // 2
    rim = grid_rows // 16
    keep = grid_rows - 4 * rim
    edges = enc_src.shape[1]
    width = halo_send.shape[3]
    table_rows = nodes + 4 * width
    band = lax.axis_index("band")
    flags = jnp.stack([band, lax.axis_size("band") - 1 - band]).astype(jnp.int32)
    smem = pl.BlockSpec(memory_space=pltpu.SMEM)
    vmem = pl.BlockSpec(memory_space=pltpu.VMEM)

    grid_cols = grid_feats.T
    own = call(pick_rim_kernel, [shape((chans, rim), BF16)] * 4)(send_rows, grid_cols)
    arrived = trade(*own)
    keep_rows, keep_sender, node_part = call(
        keep_kernel,
        [shape((chans, keep), BF16), shape((keep, dim), BF16), shape((nodes, dim), BF16)],
    )(send_rows, grid_cols, mesh_feats, w_embed, w_send, w_recv)

    def whole(array):
        dims = array.shape
        return pl.BlockSpec(dims, lambda i: (0,) * len(dims))

    tile = pl.BlockSpec((1, EDGE_TILE), lambda i: (0, i))
    outs = [
        shape((chans, 4 * rim), BF16), shape((edges, dim), BF16), shape((nodes, dim), BF16), shape((nodes, dim), BF16),
    ] + [shape((width, half), BF16)] * 4
    ins = (halo_send, keep_sender, node_part, mesh_feats, w_embed, w_send, w_out, *arrived, own[0], own[1])
    rim_rows, slope, gathered, latent, h00, h01, h10, h11 = call(
        encode_kernel,
        outs,
        grid=(edges // EDGE_TILE,),
        in_specs=[smem, tile, tile] + [whole(x) for x in ins],
        out_specs=[
            whole(outs[0]), pl.BlockSpec((EDGE_TILE, dim), lambda i: (i, 0)),
        ] + [whole(x) for x in outs[2:]],
        scratch_shapes=[pltpu.VMEM((grid_rows + nodes, dim), BF16), pltpu.VMEM((nodes, dim), F32)],
    )(flags, enc_src, enc_dst, *ins)

    halos = trade(h00, h01, h10, h11)
    outs = [shape((width, half), BF16)] * 4 + [
        shape((nodes, half), BF16), shape((nodes, half), F32), shape((table_rows, half), BF16),
        shape((table_rows + nodes, dim), BF16), shape((nodes, dim), BF16), shape((nodes, half), BF16),
        shape((nodes, dim), BF16), shape((nodes, dim), BF16),
    ]
    (g0, g1, g2, g3, coupled_grad, lower_grad, halo_table, ends, summed, coupled, hidden, hidden_grad) = call(
        mesh_kernel,
        outs,
        scratch_shapes=[
            pltpu.VMEM((table_rows + nodes, dim), BF16), pltpu.VMEM((mesh_src.shape[1], dim), BF16),
            pltpu.VMEM((nodes, dim), F32), pltpu.VMEM((table_rows + nodes, dim), F32),
        ],
    )(mesh_src, mesh_dst, latent, cotangent, *halos, u_src, u_dst, u_out, v_in, v_out)
    returned = trade(g0, g1, g2, g3)
    mesh_grads = call(
        mesh_weight_kernel,
        [shape((half, dim), F32), shape((half, dim), F32), shape((dim, half), F32), shape((half, dim), F32), shape((dim, half), F32)],
    )(halo_table, ends, summed, coupled, hidden, hidden_grad, coupled_grad, cotangent)
    mesh_totals = lax.psum(mesh_grads, ("band", "patch"))

    keep_grad, q0, q1, q2, q3, mesh_grad, grad_embed, grad_send, grad_recv, grad_out = call(
        encoder_back_kernel,
        [shape((chans, keep), BF16)] + [shape((chans, rim), BF16)] * 4 + [
            shape((nodes, dim), F32), shape((chans, dim), F32), shape((dim, dim), F32), shape((dim, dim), F32), shape((dim, dim), F32),
        ],
        scratch_shapes=[pltpu.VMEM((edges, dim), BF16), pltpu.VMEM((nodes, dim), BF16), pltpu.VMEM((nodes, dim), F32)],
    )(
        enc_src, enc_dst, halo_send, slope, keep_rows, rim_rows, gathered, mesh_feats, coupled_grad, lower_grad,
        *returned, w_embed, w_send, w_recv, w_out,
    )
    enc_totals = lax.psum((grad_embed, grad_send, grad_recv, grad_out), ("band", "patch"))
    back = trade(q0, q1, q2, q3)
    grid_grad = call(
        place_kernel,
        shape((chans, grid_rows), BF16),
        in_specs=[smem] + [vmem] * 8,
        scratch_shapes=[pltpu.VMEM((chans, grid_rows), BF16)],
    )(flags, send_rows, keep_grad, *back, q0, q1)
    return (grid_grad.T, mesh_grad, *enc_totals, *mesh_totals)


def solution(mesh):
    rows = P(("band", "patch"), None)
    in_specs = (rows,) * 3 + (P(),) * 9 + (rows,) * 3 + (P(("band", "patch"), None, None, None),) + (rows,) * 2
    out_specs = (rows,) * 2 + (P(),) * 9
    return jax.shard_map(body, mesh=mesh, in_specs=in_specs, out_specs=out_specs, check_vma=False)
```

```python
import functools

import jax
import jax.numpy as jnp
from jax import lax
from jax.experimental import pallas as pl
from jax.experimental.pallas import tpu as pltpu
from jax.sharding import Mesh
from jax.sharding import PartitionSpec as P

BF16 = jnp.bfloat16
F32 = jnp.float32
LANES = 128
EDGE_TILE = 512
ROW_TILE = 512
VMEM_LIMIT = 56 * 1024 * 1024
BAND = ("z", "core")
PATCH = ("y", "x")
CHIPS = ("z", "y", "x")


def mm(left, right):
    return lax.dot_general(left, right, (((1,), (0,)), ((), ())), preferred_element_type=F32)


def mm_left(left, right):
    return lax.dot_general(left, right, (((0,), (0,)), ((), ())), preferred_element_type=F32)


def mm_right(left, right):
    return lax.dot_general(left, right, (((1,), (1,)), ((), ())), preferred_element_type=F32)


def table_by_row(index, count):
    n = index.shape[1]
    rows = lax.broadcasted_iota(jnp.int32, (count, n), 0)
    return jnp.where(rows == index, 1.0, 0.0).astype(BF16)


def table_by_column(index, count):
    n = index.shape[1]
    parts = []
    for start in range(0, n, LANES):
        width = min(LANES, n - start)
        piece = jnp.broadcast_to(index[:, start : start + width], (LANES, width))
        column = jnp.transpose(piece)
        wide = jnp.concatenate([column] * (count // LANES), axis=1)
        columns = lax.broadcasted_iota(jnp.int32, (width, count), 1)
        parts.append(jnp.where(wide == columns, 1.0, 0.0).astype(BF16))
    return parts[0] if len(parts) == 1 else jnp.concatenate(parts, axis=0)


def silu_both(value):
    sigma = 0.5 * jnp.tanh(0.5 * value) + 0.5
    act = value * sigma
    return act, sigma + act * (1.0 - sigma)


def call(kernel, out_shape, **more):
    return pl.pallas_call(
        kernel,
        out_shape=out_shape,
        compiler_params=pltpu.CompilerParams(vmem_limit_bytes=VMEM_LIMIT),
        **more,
    )


def shape(dims, kind):
    return jax.ShapeDtypeStruct(tuple(dims), kind)


def pick_rim_kernel(order_ref, grid_ref, *out_refs):
    rim = out_refs[0].shape[1]
    keep = order_ref.shape[1] - 4 * rim
    table = table_by_row(order_ref[:, keep:], grid_ref.shape[1])
    picked = mm(grid_ref[...], table).astype(BF16)
    for k in range(4):
        out_refs[k][...] = picked[:, k * rim : (k + 1) * rim]


def keep_kernel(order_ref, grid_ref, mesh_ref, embed_ref, send_ref, recv_ref, rows_ref, sender_ref, node_ref):
    keep = rows_ref.shape[1]
    node_ref[...] = mm(mesh_ref[...], recv_ref[...]).astype(BF16)

    def step(i, carry):
        start = pl.multiple_of(i * ROW_TILE, ROW_TILE)
        table = table_by_row(order_ref[:, pl.ds(start, ROW_TILE)], grid_ref.shape[1])
        rows = mm(grid_ref[...], table).astype(BF16)
        rows_ref[:, pl.ds(start, ROW_TILE)] = rows
        embedded = silu_both(mm_left(rows, embed_ref[...]))[0].astype(BF16)
        sender_ref[pl.ds(start, ROW_TILE), :] = mm(embedded, send_ref[...]).astype(BF16)
        return carry

    lax.fori_loop(0, keep // ROW_TILE, step, 0)


def encode_kernel(
    flag_ref, src_ref, dst_ref, halo_ref, sender_ref, node_ref, mesh_ref, embed_ref, send_ref, out_w_ref,
    in0, in1, in2, in3, own0, own1,
    rim_ref, slope_ref, gathered_ref, latent_ref, h00, h01, h10, h11,
    table, total,
):
    step = pl.program_id(0)
    keep = sender_ref.shape[0]
    rim = in0.shape[1]
    rows = keep + 4 * rim
    nodes = node_ref.shape[0]

    @pl.when(step == 0)
    def _():
        table[0:keep, :] = sender_ref[...]
        table[rows : rows + nodes, :] = node_ref[...]
        rim_ref[:, 0:rim] = jnp.where(flag_ref[0] > 0, in0[...], own0[...])
        rim_ref[:, rim : 2 * rim] = jnp.where(flag_ref[1] > 0, in1[...], own1[...])
        rim_ref[:, 2 * rim : 3 * rim] = in2[...]
        rim_ref[:, 3 * rim : 4 * rim] = in3[...]
        embedded = silu_both(mm_left(rim_ref[...], embed_ref[...]))[0].astype(BF16)
        table[keep:rows, :] = mm(embedded, send_ref[...]).astype(BF16)
        total[...] = jnp.zeros_like(total)

    both = jnp.concatenate([table_by_column(src_ref[...], rows), table_by_column(dst_ref[...], nodes)], axis=1)
    act, slope = silu_both(mm(both, table[...]))
    slope_ref[...] = slope.astype(BF16)
    total[...] += mm(table_by_row(dst_ref[...], nodes), act.astype(BF16))

    @pl.when(step == pl.num_programs(0) - 1)
    def _():
        gathered = total[...].astype(BF16)
        gathered_ref[...] = gathered
        latent = (mesh_ref[...].astype(F32) + mm(gathered, out_w_ref[...])).astype(BF16)
        latent_ref[...] = latent
        lower = latent[:, latent.shape[1] // 2 :]
        for a, b, ref in ((0, 0, h00), (0, 1, h01), (1, 0, h10), (1, 1, h11)):
            pick = table_by_row(halo_ref[0, a, b : b + 1, :], nodes)
            ref[...] = mm_left(pick, lower).astype(BF16)


def mesh_kernel(
    src_ref, dst_ref, latent_ref, cot_ref, b0, b1, b2, b3, u_src_ref, u_dst_ref, u_out_ref, v_in_ref, v_out_ref,
    g0, g1, g2, g3, coupled_grad_ref, lower_grad_ref, halo_table_ref, ends_ref, summed_ref, coupled_ref, hidden_ref, hidden_grad_ref,
    table, slope_s, total, ends,
):
    nodes = latent_ref.shape[0]
    half = latent_ref.shape[1] // 2
    width = b0.shape[0]
    rows = nodes + 4 * width
    upper = latent_ref[:, :half]
    lower = latent_ref[:, half:]
    halo_table_ref[0:nodes, :] = lower
    for k, ref in enumerate((b0, b1, b2, b3)):
        halo_table_ref[nodes + k * width : nodes + (k + 1) * width, :] = ref[...]
    table[0:rows, :] = mm(halo_table_ref[...], u_src_ref[...]).astype(BF16)
    table[rows : rows + nodes, :] = mm(lower, u_dst_ref[...]).astype(BF16)
    total[...] = jnp.zeros_like(total)
    ends[...] = jnp.zeros_like(ends)
    steps = src_ref.shape[1] // EDGE_TILE

    def forward(i, carry):
        start = pl.multiple_of(i * EDGE_TILE, EDGE_TILE)
        src = src_ref[:, pl.ds(start, EDGE_TILE)]
        dst = dst_ref[:, pl.ds(start, EDGE_TILE)]
        both = jnp.concatenate([table_by_column(src, rows), table_by_column(dst, nodes)], axis=1)
        act, slope = silu_both(mm(both, table[...]))
        slope_s[pl.ds(start, EDGE_TILE), :] = slope.astype(BF16)
        total[...] += mm(table_by_row(dst, nodes), act.astype(BF16))
        return carry

    lax.fori_loop(0, steps, forward, 0)
    summed = total[...].astype(BF16)
    summed_ref[...] = summed
    coupled = (upper.astype(F32) + mm(summed, u_out_ref[...])).astype(BF16)
    coupled_ref[...] = coupled
    act, slope = silu_both(mm(coupled, v_in_ref[...]))
    hidden_ref[...] = act.astype(BF16)
    upper_cot = cot_ref[:, :half]
    lower_cot = cot_ref[:, half:]
    hidden_grad = (mm_right(lower_cot, v_out_ref[...]) * slope).astype(BF16)
    hidden_grad_ref[...] = hidden_grad
    coupled_grad = (upper_cot.astype(F32) + mm_right(hidden_grad, v_in_ref[...])).astype(BF16)
    coupled_grad_ref[...] = coupled_grad
    summed_grad = mm_right(coupled_grad, u_out_ref[...]).astype(BF16)

    def backward(i, carry):
        start = pl.multiple_of(i * EDGE_TILE, EDGE_TILE)
        src = src_ref[:, pl.ds(start, EDGE_TILE)]
        dst = dst_ref[:, pl.ds(start, EDGE_TILE)]
        grad = mm(table_by_column(dst, nodes), summed_grad) * slope_s[pl.ds(start, EDGE_TILE), :].astype(F32)
        both = jnp.concatenate([table_by_row(src, rows), table_by_row(dst, nodes)], axis=0)
        ends[...] += mm(both, grad.astype(BF16))
        return carry

    lax.fori_loop(0, steps, backward, 0)
    ends_ref[...] = ends[...].astype(BF16)
    source_grad = ends_ref[0:rows, :]
    target_grad = ends_ref[rows : rows + nodes, :]
    table_grad = mm_right(source_grad, u_src_ref[...])
    lower_grad_ref[...] = lower_cot.astype(F32) + mm_right(target_grad, u_dst_ref[...]) + table_grad[0:nodes, :]
    for k, ref in enumerate((g0, g1, g2, g3)):
        ref[...] = table_grad[nodes + k * width : nodes + (k + 1) * width, :].astype(BF16)


def store_halves(core_ref, mine_ref, other_ref, start, value):
    half = mine_ref.shape[0]
    value = value.astype(BF16)
    done = 0
    while done < value.shape[0]:
        row = start + done
        count = min(value.shape[0] - done, half - row % half)
        piece = value[done : done + count, :]
        here = row % half

        @pl.when(core_ref[0] == row // half)
        def _(piece=piece, here=here, count=count):
            mine_ref[here : here + count, :] = piece

        @pl.when(core_ref[0] != row // half)
        def _(piece=piece, here=here, count=count):
            other_ref[here : here + count, :] = piece

        done += count


def side_by_side(value):
    rows = value.shape[0] // 2
    return jnp.concatenate([value[:rows, :], value[rows:, :]], axis=1)


def mesh_weight_kernel(
    core_ref, halo_table_ref, ends_ref, summed_ref, coupled_ref, hidden_ref, hidden_grad_ref, coupled_grad_ref, cot_ref,
    mine_ref, other_ref,
):
    rows = halo_table_ref.shape[0]
    nodes, half = coupled_ref.shape
    parts = (
        mm_left(halo_table_ref[...], ends_ref[0:rows, :]),
        mm_left(halo_table_ref[0:nodes, :], ends_ref[rows : rows + nodes, :]),
        side_by_side(mm_left(summed_ref[...], coupled_grad_ref[...])),
        mm_left(coupled_ref[...], hidden_grad_ref[...]),
        side_by_side(mm_left(hidden_ref[...], cot_ref[:, half:])),
    )
    start = 0
    for part in parts:
        store_halves(core_ref, mine_ref, other_ref, start, part)
        start += part.shape[0]


def encoder_back_kernel(
    core_ref, src_ref, dst_ref, halo_ref, slope_ref, keep_rows_ref, rim_rows_ref, gathered_ref, mesh_ref,
    coupled_grad_ref, lower_grad_ref, r0, r1, r2, r3, embed_ref, send_ref, recv_ref, out_w_ref,
    keep_grad_ref, g0, g1, g2, g3, mesh_grad_ref, mine_ref, other_ref,
    grad_embed_ref, grad_send_ref, edge_s, latent_s, nodes_s,
):
    nodes = mesh_ref.shape[0]
    keep = keep_rows_ref.shape[1]
    rim = g0.shape[1]
    lower_grad = lower_grad_ref[...]
    for a, b, ref in ((0, 0, r0), (0, 1, r1), (1, 0, r2), (1, 1, r3)):
        lower_grad += mm(table_by_row(halo_ref[0, a, b : b + 1, :], nodes), ref[...])
    half = lower_grad.shape[1]
    latent_s[:, :half] = coupled_grad_ref[...]
    latent_s[:, half:] = lower_grad.astype(BF16)
    latent_grad = latent_s[...]
    dim = latent_grad.shape[1]
    store_halves(core_ref, mine_ref, other_ref, 0, mm_left(gathered_ref[...], latent_grad))
    gathered_grad = mm_right(latent_grad, out_w_ref[...]).astype(BF16)
    nodes_s[...] = jnp.zeros_like(nodes_s)

    def edges(i, carry):
        start = pl.multiple_of(i * EDGE_TILE, EDGE_TILE)
        dst = dst_ref[:, pl.ds(start, EDGE_TILE)]
        grad = mm(table_by_column(dst, nodes), gathered_grad) * slope_ref[pl.ds(start, EDGE_TILE), :].astype(F32)
        grad = grad.astype(BF16)
        edge_s[pl.ds(start, EDGE_TILE), :] = grad
        nodes_s[...] += mm(table_by_row(dst, nodes), grad)
        return carry

    lax.fori_loop(0, src_ref.shape[1] // EDGE_TILE, edges, 0)
    node_grad = nodes_s[...].astype(BF16)
    store_halves(core_ref, mine_ref, other_ref, dim, mm_left(mesh_ref[...], node_grad))
    mesh_grad_ref[...] = latent_grad.astype(F32) + mm_right(node_grad, recv_ref[...])
    grad_embed_ref[...] = jnp.zeros_like(grad_embed_ref)
    grad_send_ref[...] = jnp.zeros_like(grad_send_ref)

    def back(rows, start, count):
        ids = lax.broadcasted_iota(jnp.int32, (count, src_ref.shape[1]), 0) + start
        table = jnp.where(ids == src_ref[...], 1.0, 0.0).astype(BF16)
        sender_grad = mm(table, edge_s[...]).astype(BF16)
        act, slope = silu_both(mm_left(rows, embed_ref[...]))
        grad_send_ref[...] += mm_left(act.astype(BF16), sender_grad)
        embedded_grad = mm_right(sender_grad, send_ref[...]).astype(BF16)
        embed_grad = (embedded_grad.astype(F32) * slope).astype(BF16)
        grad_embed_ref[0 : rows.shape[0], :] += mm(rows, embed_grad)
        return mm_right(embed_ref[...], embed_grad).astype(BF16)

    rim_grad = back(rim_rows_ref[...], keep, 4 * rim)
    for k, ref in enumerate((g0, g1, g2, g3)):
        ref[...] = rim_grad[:, k * rim : (k + 1) * rim]

    def kept(i, carry):
        start = pl.multiple_of(i * ROW_TILE, ROW_TILE)
        keep_grad_ref[:, pl.ds(start, ROW_TILE)] = back(keep_rows_ref[:, pl.ds(start, ROW_TILE)], start, ROW_TILE)
        return carry

    lax.fori_loop(0, keep // ROW_TILE, kept, 0)
    store_halves(core_ref, mine_ref, other_ref, 2 * dim, grad_send_ref[...])
    store_halves(core_ref, mine_ref, other_ref, 3 * dim, grad_embed_ref[...])


def place_kernel(flag_ref, order_ref, keep_ref, in0, in1, in2, in3, own0, own1, grid_grad_ref, all_s):
    keep = keep_ref.shape[1]
    rim = in0.shape[1]
    all_s[:, 0:keep] = keep_ref[...]
    all_s[:, keep : keep + rim] = jnp.where(flag_ref[0] > 0, in0[...], own0[...])
    all_s[:, keep + rim : keep + 2 * rim] = jnp.where(flag_ref[1] > 0, in1[...], own1[...])
    all_s[:, keep + 2 * rim : keep + 3 * rim] = in2[...]
    all_s[:, keep + 3 * rim : keep + 4 * rim] = in3[...]

    def place(i, carry):
        start = pl.multiple_of(i * ROW_TILE, ROW_TILE)
        ids = lax.broadcasted_iota(jnp.int32, (ROW_TILE, order_ref.shape[1]), 0) + start
        table = jnp.where(ids == order_ref[...], 1.0, 0.0).astype(BF16)
        grid_grad_ref[:, pl.ds(start, ROW_TILE)] = mm_right(all_s[...], table).astype(BF16)
        return carry

    lax.fori_loop(0, grid_grad_ref.shape[1] // ROW_TILE, place, 0)


def add_kernel(a_mine, a_in, b_mine, b_in, sum_ref):
    count = a_mine.shape[0]
    sum_ref[0:count, :] = (a_mine[...].astype(F32) + a_in[...].astype(F32)).astype(BF16)
    sum_ref[count:, :] = (b_mine[...].astype(F32) + b_in[...].astype(F32)).astype(BF16)


def total_kernel(parts_ref, out_ref):
    total = parts_ref[0].astype(F32)
    for k in range(1, parts_ref.shape[0]):
        total += parts_ref[k].astype(F32)
    total = total.astype(BF16)
    for k in range(parts_ref.shape[0]):
        out_ref[k] = total


def unpack_kernel(a_rows, core_ref, mine_ref, other_ref, embed_ref, send_ref, recv_ref, out_ref, u_src_ref, u_dst_ref, u_out_ref, v_in_ref, v_out_ref):
    first = core_ref[0] == 0

    def read(base, half, start, count):
        pieces = []
        while count > 0:
            here = start % half
            some = min(count, half - here)
            mine = mine_ref[base + here : base + here + some, :]
            other = other_ref[base + here : base + here + some, :]
            pieces.append(jnp.where(first == (start < half), mine, other))
            start += some
            count -= some
        value = pieces[0] if len(pieces) == 1 else jnp.concatenate(pieces, axis=0)
        return value.astype(F32)

    dim, half = v_out_ref.shape
    a_half = a_rows // 2
    b_half = mine_ref.shape[0] - a_half
    for start, ref in ((0, u_src_ref), (half, u_dst_ref), (3 * half, v_in_ref)):
        ref[...] = read(0, a_half, start, half)
    for start, ref in ((2 * half, u_out_ref), (4 * half, v_out_ref)):
        value = read(0, a_half, start, half)
        ref[0:half, :] = value[:, :half]
        ref[half:, :] = value[:, half:]
    for start, ref in ((0, out_ref), (dim, recv_ref), (2 * dim, send_ref)):
        ref[...] = read(a_half, b_half, start, dim)
    ref = embed_ref
    ref[...] = read(a_half, b_half, 3 * dim, half)[0 : ref.shape[0], :]


def trade(below, above, west, east):
    bands = lax.axis_size(BAND)
    patches = lax.axis_size(PATCH)
    up = [(i, i + 1) for i in range(bands - 1)]
    down = [(i + 1, i) for i in range(bands - 1)]
    right = [(i, (i + 1) % patches) for i in range(patches)]
    left = [((i + 1) % patches, i) for i in range(patches)]
    return (
        lax.ppermute(above, BAND, up),
        lax.ppermute(below, BAND, down),
        lax.ppermute(east, PATCH, right),
        lax.ppermute(west, PATCH, left),
    )


def swap_cores(value):
    return lax.ppermute(value, "core", [(0, 1), (1, 0)])


def body(
    grid_feats, mesh_feats, cotangent, w_embed, w_send, w_recv, w_out, u_src, u_dst, u_out, v_in, v_out,
    send_rows, enc_src, enc_dst, halo_send, mesh_src, mesh_dst,
):
    chans = grid_feats.shape[1]
    grid_rows = grid_feats.shape[0]
    nodes, dim = mesh_feats.shape
    half = dim // 2
    rim = grid_rows // 16
    keep = grid_rows - 4 * rim
    edges = enc_src.shape[1]
    width = halo_send.shape[3]
    table_rows = nodes + 4 * width
    band = lax.axis_index(BAND)
    flags = jnp.stack([band, lax.axis_size(BAND) - 1 - band]).astype(jnp.int32)
    core = lax.axis_index("core").astype(jnp.int32).reshape(1)
    smem = pl.BlockSpec(memory_space=pltpu.SMEM)
    vmem = pl.BlockSpec(memory_space=pltpu.VMEM)

    grid_cols = grid_feats.T
    own = call(pick_rim_kernel, [shape((chans, rim), BF16)] * 4)(send_rows, grid_cols)
    arrived = trade(*own)
    keep_rows, keep_sender, node_part = call(
        keep_kernel,
        [shape((chans, keep), BF16), shape((keep, dim), BF16), shape((nodes, dim), BF16)],
    )(send_rows, grid_cols, mesh_feats, w_embed, w_send, w_recv)

    def whole(array):
        dims = array.shape
        return pl.BlockSpec(dims, lambda i: (0,) * len(dims))

    tile = pl.BlockSpec((1, EDGE_TILE), lambda i: (0, i))
    outs = [
        shape((chans, 4 * rim), BF16), shape((edges, dim), BF16), shape((nodes, dim), BF16), shape((nodes, dim), BF16),
    ] + [shape((width, half), BF16)] * 4
    ins = (halo_send, keep_sender, node_part, mesh_feats, w_embed, w_send, w_out, *arrived, own[0], own[1])
    rim_rows, slope, gathered, latent, h00, h01, h10, h11 = call(
        encode_kernel,
        outs,
        grid=(edges // EDGE_TILE,),
        in_specs=[smem, tile, tile] + [whole(x) for x in ins],
        out_specs=[
            whole(outs[0]), pl.BlockSpec((EDGE_TILE, dim), lambda i: (i, 0)),
        ] + [whole(x) for x in outs[2:]],
        scratch_shapes=[pltpu.VMEM((grid_rows + nodes, dim), BF16), pltpu.VMEM((nodes, dim), F32)],
    )(flags, enc_src, enc_dst, *ins)

    halos = trade(h00, h01, h10, h11)
    outs = [shape((width, half), BF16)] * 4 + [
        shape((nodes, half), BF16), shape((nodes, half), F32), shape((table_rows, half), BF16),
        shape((table_rows + nodes, dim), BF16), shape((nodes, dim), BF16), shape((nodes, half), BF16),
        shape((nodes, dim), BF16), shape((nodes, dim), BF16),
    ]
    (g0, g1, g2, g3, coupled_grad, lower_grad, halo_table, ends, summed, coupled, hidden, hidden_grad) = call(
        mesh_kernel,
        outs,
        scratch_shapes=[
            pltpu.VMEM((table_rows + nodes, dim), BF16), pltpu.VMEM((mesh_src.shape[1], dim), BF16),
            pltpu.VMEM((nodes, dim), F32), pltpu.VMEM((table_rows + nodes, dim), F32),
        ],
    )(mesh_src, mesh_dst, latent, cotangent, *halos, u_src, u_dst, u_out, v_in, v_out)
    returned = trade(g0, g1, g2, g3)
    a_rows = 5 * half
    a_mine, a_other = call(
        mesh_weight_kernel, [shape((a_rows // 2, dim), BF16)] * 2, in_specs=[smem] + [vmem] * 8,
    )(core, halo_table, ends, summed, coupled, hidden, hidden_grad, coupled_grad, cotangent)
    a_in = swap_cores(a_other)

    b_rows = 3 * dim + half
    keep_grad, q0, q1, q2, q3, mesh_grad, b_mine, b_other = call(
        encoder_back_kernel,
        [shape((chans, keep), BF16)] + [shape((chans, rim), BF16)] * 4 + [shape((nodes, dim), F32)]
        + [shape((b_rows // 2, dim), BF16)] * 2,
        in_specs=[smem] + [vmem] * 18,
        scratch_shapes=[
            pltpu.VMEM((half, dim), F32), pltpu.VMEM((dim, dim), F32),
            pltpu.VMEM((edges, dim), BF16), pltpu.VMEM((nodes, dim), BF16), pltpu.VMEM((nodes, dim), F32),
        ],
    )(
        core, enc_src, enc_dst, halo_send, slope, keep_rows, rim_rows, gathered, mesh_feats, coupled_grad, lower_grad,
        *returned, w_embed, w_send, w_recv, w_out,
    )
    b_in = swap_cores(b_other)
    back = trade(q0, q1, q2, q3)
    grid_grad = call(
        place_kernel,
        shape((chans, grid_rows), BF16),
        in_specs=[smem] + [vmem] * 8,
        scratch_shapes=[pltpu.VMEM((chans, grid_rows), BF16)],
    )(flags, send_rows, keep_grad, *back, q0, q1)
    chips = lax.axis_size(CHIPS)
    packed = (a_rows + b_rows) // 2
    pair = call(add_kernel, shape((packed, dim), BF16))(a_mine, a_in, b_mine, b_in)
    parts = lax.all_to_all(pair.reshape(chips, packed // chips, dim), CHIPS, 0, 0)
    parts = call(total_kernel, shape(parts.shape, BF16))(parts)
    mine = lax.all_to_all(parts, CHIPS, 0, 0).reshape(packed, dim)
    other = swap_cores(mine)
    totals = call(
        functools.partial(unpack_kernel, a_rows),
        [shape((chans, dim), F32)] + [shape((dim, dim), F32)] * 3 + [shape((half, dim), F32)] * 2
        + [shape((dim, half), F32), shape((half, dim), F32), shape((dim, half), F32)],
        in_specs=[smem] + [vmem] * 2,
    )(core, mine, other)
    return (grid_grad.T, mesh_grad, *totals)


def solution(mesh):
    chips = Mesh(mesh.devices.reshape(mesh.shape["band"] // 2, 2, 4, mesh.shape["patch"] // 4), ("z", "core", "y", "x"))
    everywhere = BAND + PATCH
    rows = P(everywhere, None)
    in_specs = (rows,) * 3 + (P(),) * 9 + (rows,) * 3 + (P(everywhere, None, None, None),) + (rows,) * 2
    out_specs = (rows,) * 2 + (P(),) * 9
    return jax.shard_map(body, mesh=chips, in_specs=in_specs, out_specs=out_specs, check_vma=False)
```

```python
import functools

import jax
import jax.numpy as jnp
from jax import lax
from jax.experimental import pallas as pl
from jax.experimental.pallas import tpu as pltpu
from jax.sharding import Mesh
from jax.sharding import PartitionSpec as P

BF16 = jnp.bfloat16
F32 = jnp.float32
LANES = 128
EDGE_TILE = 1024
ROW_TILE = 512
VMEM_LIMIT = 56 * 1024 * 1024
BAND = ("z", "core")
PATCH = ("y", "x")
CHIPS = ("z", "y", "x")


def mm(left, right):
    return lax.dot_general(left, right, (((1,), (0,)), ((), ())), preferred_element_type=F32)


def mm_left(left, right):
    return lax.dot_general(left, right, (((0,), (0,)), ((), ())), preferred_element_type=F32)


def mm_right(left, right):
    return lax.dot_general(left, right, (((1,), (1,)), ((), ())), preferred_element_type=F32)


def table_by_row(index, count):
    n = index.shape[1]
    rows = lax.broadcasted_iota(jnp.int32, (count, n), 0)
    return jnp.where(rows == index, 1.0, 0.0).astype(BF16)


def table_by_column(index, count):
    n = index.shape[1]
    parts = []
    for start in range(0, n, LANES):
        width = min(LANES, n - start)
        piece = jnp.broadcast_to(index[:, start : start + width], (LANES, width))
        column = jnp.transpose(piece)
        wide = jnp.concatenate([column] * (count // LANES), axis=1)
        columns = lax.broadcasted_iota(jnp.int32, (width, count), 1)
        parts.append(jnp.where(wide == columns, 1.0, 0.0).astype(BF16))
    return parts[0] if len(parts) == 1 else jnp.concatenate(parts, axis=0)


def silu_both(value):
    sigma = 0.5 * jnp.tanh(0.5 * value) + 0.5
    act = value * sigma
    return act, sigma + act * (1.0 - sigma)


def call(kernel, out_shape, work, **more):
    return pl.pallas_call(
        kernel,
        out_shape=out_shape,
        cost_estimate=pl.CostEstimate(flops=int(work * 1e9), bytes_accessed=int(work * 1e6), transcendentals=0),
        compiler_params=pltpu.CompilerParams(vmem_limit_bytes=VMEM_LIMIT),
        **more,
    )


def shape(dims, kind):
    return jax.ShapeDtypeStruct(tuple(dims), kind)


def pick_rim_kernel(order_ref, grid_ref, *out_refs):
    rim = out_refs[0].shape[1]
    keep = order_ref.shape[1] - 4 * rim
    table = table_by_row(order_ref[:, keep:], grid_ref.shape[1])
    picked = mm(grid_ref[...], table).astype(BF16)
    for k in range(4):
        out_refs[k][...] = picked[:, k * rim : (k + 1) * rim]


def keep_kernel(order_ref, grid_ref, mesh_ref, embed_ref, send_ref, recv_ref, rows_ref, sender_ref, node_ref):
    keep = rows_ref.shape[1]
    node_ref[...] = mm(mesh_ref[...], recv_ref[...]).astype(BF16)

    def step(i, carry):
        start = pl.multiple_of(i * ROW_TILE, ROW_TILE)
        table = table_by_row(order_ref[:, pl.ds(start, ROW_TILE)], grid_ref.shape[1])
        rows = mm(grid_ref[...], table).astype(BF16)
        rows_ref[:, pl.ds(start, ROW_TILE)] = rows
        embedded = silu_both(mm_left(rows, embed_ref[...]))[0].astype(BF16)
        sender_ref[pl.ds(start, ROW_TILE), :] = mm(embedded, send_ref[...]).astype(BF16)
        return carry

    lax.fori_loop(0, keep // ROW_TILE, step, 0)


def encode_kernel(
    flag_ref, src_ref, dst_ref, halo_ref, sender_ref, node_ref, mesh_ref, embed_ref, send_ref, out_w_ref,
    in0, in1, in2, in3, own0, own1,
    rim_ref, slope_ref, gathered_ref, latent_ref, h00, h01, h10, h11,
    table, total,
):
    step = pl.program_id(0)
    keep = sender_ref.shape[0]
    rim = in0.shape[1]
    rows = keep + 4 * rim
    nodes = node_ref.shape[0]

    @pl.when(step == 0)
    def _():
        table[0:keep, :] = sender_ref[...]
        table[rows : rows + nodes, :] = node_ref[...]
        rim_ref[:, 0:rim] = jnp.where(flag_ref[0] > 0, in0[...], own0[...])
        rim_ref[:, rim : 2 * rim] = jnp.where(flag_ref[1] > 0, in1[...], own1[...])
        rim_ref[:, 2 * rim : 3 * rim] = in2[...]
        rim_ref[:, 3 * rim : 4 * rim] = in3[...]
        embedded = silu_both(mm_left(rim_ref[...], embed_ref[...]))[0].astype(BF16)
        table[keep:rows, :] = mm(embedded, send_ref[...]).astype(BF16)
        total[...] = jnp.zeros_like(total)

    both = jnp.concatenate([table_by_column(src_ref[...], rows), table_by_column(dst_ref[...], nodes)], axis=1)
    act, slope = silu_both(mm(both, table[...]))
    slope_ref[...] = slope.astype(BF16)
    total[...] += mm(table_by_row(dst_ref[...], nodes), act.astype(BF16))

    @pl.when(step == pl.num_programs(0) - 1)
    def _():
        gathered = total[...].astype(BF16)
        gathered_ref[...] = gathered
        latent = (mesh_ref[...].astype(F32) + mm(gathered, out_w_ref[...])).astype(BF16)
        latent_ref[...] = latent
        lower = latent[:, latent.shape[1] // 2 :]
        for a, b, ref in ((0, 0, h00), (0, 1, h01), (1, 0, h10), (1, 1, h11)):
            pick = table_by_row(halo_ref[0, a, b : b + 1, :], nodes)
            ref[...] = mm_left(pick, lower).astype(BF16)


def mesh_kernel(
    src_ref, dst_ref, latent_ref, cot_ref, b0, b1, b2, b3, u_src_ref, u_dst_ref, u_out_ref, v_in_ref, v_out_ref,
    g0, g1, g2, g3, coupled_grad_ref, lower_grad_ref, halo_table_ref, ends_ref, summed_ref, coupled_ref, hidden_ref, hidden_grad_ref,
    table, slope_s, total, ends,
):
    nodes = latent_ref.shape[0]
    half = latent_ref.shape[1] // 2
    width = b0.shape[0]
    rows = nodes + 4 * width
    upper = latent_ref[:, :half]
    lower = latent_ref[:, half:]
    halo_table_ref[0:nodes, :] = lower
    for k, ref in enumerate((b0, b1, b2, b3)):
        halo_table_ref[nodes + k * width : nodes + (k + 1) * width, :] = ref[...]
    table[0:rows, :] = mm(halo_table_ref[...], u_src_ref[...]).astype(BF16)
    table[rows : rows + nodes, :] = mm(lower, u_dst_ref[...]).astype(BF16)
    total[...] = jnp.zeros_like(total)
    ends[...] = jnp.zeros_like(ends)
    steps = src_ref.shape[1] // EDGE_TILE

    def forward(i, carry):
        start = pl.multiple_of(i * EDGE_TILE, EDGE_TILE)
        src = src_ref[:, pl.ds(start, EDGE_TILE)]
        dst = dst_ref[:, pl.ds(start, EDGE_TILE)]
        both = jnp.concatenate([table_by_column(src, rows), table_by_column(dst, nodes)], axis=1)
        act, slope = silu_both(mm(both, table[...]))
        slope_s[pl.ds(start, EDGE_TILE), :] = slope.astype(BF16)
        total[...] += mm(table_by_row(dst, nodes), act.astype(BF16))
        return carry

    lax.fori_loop(0, steps, forward, 0)
    summed = total[...].astype(BF16)
    summed_ref[...] = summed
    coupled = (upper.astype(F32) + mm(summed, u_out_ref[...])).astype(BF16)
    coupled_ref[...] = coupled
    act, slope = silu_both(mm(coupled, v_in_ref[...]))
    hidden_ref[...] = act.astype(BF16)
    upper_cot = cot_ref[:, :half]
    lower_cot = cot_ref[:, half:]
    hidden_grad = (mm_right(lower_cot, v_out_ref[...]) * slope).astype(BF16)
    hidden_grad_ref[...] = hidden_grad
    coupled_grad = (upper_cot.astype(F32) + mm_right(hidden_grad, v_in_ref[...])).astype(BF16)
    coupled_grad_ref[...] = coupled_grad
    summed_grad = mm_right(coupled_grad, u_out_ref[...]).astype(BF16)

    def backward(i, carry):
        start = pl.multiple_of(i * EDGE_TILE, EDGE_TILE)
        src = src_ref[:, pl.ds(start, EDGE_TILE)]
        dst = dst_ref[:, pl.ds(start, EDGE_TILE)]
        grad = mm(table_by_column(dst, nodes), summed_grad) * slope_s[pl.ds(start, EDGE_TILE), :].astype(F32)
        both = jnp.concatenate([table_by_row(src, rows), table_by_row(dst, nodes)], axis=0)
        ends[...] += mm(both, grad.astype(BF16))
        return carry

    lax.fori_loop(0, steps, backward, 0)
    ends_ref[...] = ends[...].astype(BF16)
    source_grad = ends_ref[0:rows, :]
    target_grad = ends_ref[rows : rows + nodes, :]
    table_grad = mm_right(source_grad, u_src_ref[...])
    lower_grad_ref[...] = lower_cot.astype(F32) + mm_right(target_grad, u_dst_ref[...]) + table_grad[0:nodes, :]
    for k, ref in enumerate((g0, g1, g2, g3)):
        ref[...] = table_grad[nodes + k * width : nodes + (k + 1) * width, :].astype(BF16)


def store_halves(core_ref, mine_ref, other_ref, start, value):
    half = mine_ref.shape[0]
    value = value.astype(BF16)
    done = 0
    while done < value.shape[0]:
        row = start + done
        count = min(value.shape[0] - done, half - row % half)
        piece = value[done : done + count, :]
        here = row % half

        @pl.when(core_ref[0] == row // half)
        def _(piece=piece, here=here, count=count):
            mine_ref[here : here + count, :] = piece

        @pl.when(core_ref[0] != row // half)
        def _(piece=piece, here=here, count=count):
            other_ref[here : here + count, :] = piece

        done += count


def side_by_side(value):
    rows = value.shape[0] // 2
    return jnp.concatenate([value[:rows, :], value[rows:, :]], axis=1)


def mesh_weight_kernel(
    core_ref, halo_table_ref, ends_ref, summed_ref, coupled_ref, hidden_ref, hidden_grad_ref, coupled_grad_ref, cot_ref,
    mine_ref, other_ref,
):
    rows = halo_table_ref.shape[0]
    nodes, half = coupled_ref.shape
    parts = (
        mm_left(halo_table_ref[...], ends_ref[0:rows, :]),
        mm_left(halo_table_ref[0:nodes, :], ends_ref[rows : rows + nodes, :]),
        side_by_side(mm_left(summed_ref[...], coupled_grad_ref[...])),
        mm_left(coupled_ref[...], hidden_grad_ref[...]),
        side_by_side(mm_left(hidden_ref[...], cot_ref[:, half:])),
    )
    start = 0
    for part in parts:
        store_halves(core_ref, mine_ref, other_ref, start, part)
        start += part.shape[0]


def encoder_back_kernel(
    core_ref, src_ref, dst_ref, halo_ref, slope_ref, keep_rows_ref, rim_rows_ref, gathered_ref, mesh_ref,
    coupled_grad_ref, lower_grad_ref, r0, r1, r2, r3, embed_ref, send_ref, recv_ref, out_w_ref,
    keep_grad_ref, g0, g1, g2, g3, mesh_grad_ref, mine_ref, other_ref,
    grad_embed_ref, grad_send_ref, edge_s, latent_s, nodes_s,
):
    nodes = mesh_ref.shape[0]
    keep = keep_rows_ref.shape[1]
    rim = g0.shape[1]
    lower_grad = lower_grad_ref[...]
    for a, b, ref in ((0, 0, r0), (0, 1, r1), (1, 0, r2), (1, 1, r3)):
        lower_grad += mm(table_by_row(halo_ref[0, a, b : b + 1, :], nodes), ref[...])
    half = lower_grad.shape[1]
    latent_s[:, :half] = coupled_grad_ref[...]
    latent_s[:, half:] = lower_grad.astype(BF16)
    latent_grad = latent_s[...]
    dim = latent_grad.shape[1]
    store_halves(core_ref, mine_ref, other_ref, 0, mm_left(gathered_ref[...], latent_grad))
    gathered_grad = mm_right(latent_grad, out_w_ref[...]).astype(BF16)
    nodes_s[...] = jnp.zeros_like(nodes_s)

    def edges(i, carry):
        start = pl.multiple_of(i * EDGE_TILE, EDGE_TILE)
        dst = dst_ref[:, pl.ds(start, EDGE_TILE)]
        grad = mm(table_by_column(dst, nodes), gathered_grad) * slope_ref[pl.ds(start, EDGE_TILE), :].astype(F32)
        grad = grad.astype(BF16)
        edge_s[pl.ds(start, EDGE_TILE), :] = grad
        nodes_s[...] += mm(table_by_row(dst, nodes), grad)
        return carry

    lax.fori_loop(0, src_ref.shape[1] // EDGE_TILE, edges, 0)
    node_grad = nodes_s[...].astype(BF16)
    store_halves(core_ref, mine_ref, other_ref, dim, mm_left(mesh_ref[...], node_grad))
    mesh_grad_ref[...] = latent_grad.astype(F32) + mm_right(node_grad, recv_ref[...])
    grad_embed_ref[...] = jnp.zeros_like(grad_embed_ref)
    grad_send_ref[...] = jnp.zeros_like(grad_send_ref)

    def back(rows, start, count):
        ids = lax.broadcasted_iota(jnp.int32, (count, src_ref.shape[1]), 0) + start
        table = jnp.where(ids == src_ref[...], 1.0, 0.0).astype(BF16)
        sender_grad = mm(table, edge_s[...]).astype(BF16)
        act, slope = silu_both(mm_left(rows, embed_ref[...]))
        grad_send_ref[...] += mm_left(act.astype(BF16), sender_grad)
        embedded_grad = mm_right(sender_grad, send_ref[...]).astype(BF16)
        embed_grad = (embedded_grad.astype(F32) * slope).astype(BF16)
        grad_embed_ref[0 : rows.shape[0], :] += mm(rows, embed_grad)
        return mm_right(embed_ref[...], embed_grad).astype(BF16)

    rim_grad = back(rim_rows_ref[...], keep, 4 * rim)
    for k, ref in enumerate((g0, g1, g2, g3)):
        ref[...] = rim_grad[:, k * rim : (k + 1) * rim]

    def kept(i, carry):
        start = pl.multiple_of(i * ROW_TILE, ROW_TILE)
        keep_grad_ref[:, pl.ds(start, ROW_TILE)] = back(keep_rows_ref[:, pl.ds(start, ROW_TILE)], start, ROW_TILE)
        return carry

    lax.fori_loop(0, keep // ROW_TILE, kept, 0)
    store_halves(core_ref, mine_ref, other_ref, 2 * dim, grad_send_ref[...])
    store_halves(core_ref, mine_ref, other_ref, 3 * dim, grad_embed_ref[...])


def place_kernel(flag_ref, order_ref, keep_ref, in0, in1, in2, in3, own0, own1, grid_grad_ref, all_s):
    keep = keep_ref.shape[1]
    rim = in0.shape[1]
    all_s[:, 0:keep] = keep_ref[...]
    all_s[:, keep : keep + rim] = jnp.where(flag_ref[0] > 0, in0[...], own0[...])
    all_s[:, keep + rim : keep + 2 * rim] = jnp.where(flag_ref[1] > 0, in1[...], own1[...])
    all_s[:, keep + 2 * rim : keep + 3 * rim] = in2[...]
    all_s[:, keep + 3 * rim : keep + 4 * rim] = in3[...]

    def place(i, carry):
        start = pl.multiple_of(i * ROW_TILE, ROW_TILE)
        ids = lax.broadcasted_iota(jnp.int32, (ROW_TILE, order_ref.shape[1]), 0) + start
        table = jnp.where(ids == order_ref[...], 1.0, 0.0).astype(BF16)
        grid_grad_ref[:, pl.ds(start, ROW_TILE)] = mm_right(all_s[...], table).astype(BF16)
        return carry

    lax.fori_loop(0, grid_grad_ref.shape[1] // ROW_TILE, place, 0)


def unpack_kernel(a_rows, core_ref, mine_ref, other_ref, embed_ref, send_ref, recv_ref, out_ref, u_src_ref, u_dst_ref, u_out_ref, v_in_ref, v_out_ref):
    first = core_ref[0] == 0

    def read(base, half, start, count):
        pieces = []
        while count > 0:
            here = start % half
            some = min(count, half - here)
            mine = mine_ref[base + here : base + here + some, :]
            other = other_ref[base + here : base + here + some, :]
            pieces.append(jnp.where(first == (start < half), mine, other))
            start += some
            count -= some
        value = pieces[0] if len(pieces) == 1 else jnp.concatenate(pieces, axis=0)
        return value.astype(F32)

    dim, half = v_out_ref.shape
    a_half = a_rows // 2
    b_half = mine_ref.shape[0] - a_half
    for start, ref in ((0, u_src_ref), (half, u_dst_ref), (3 * half, v_in_ref)):
        ref[...] = read(0, a_half, start, half)
    for start, ref in ((2 * half, u_out_ref), (4 * half, v_out_ref)):
        value = read(0, a_half, start, half)
        ref[0:half, :] = value[:, :half]
        ref[half:, :] = value[:, half:]
    for start, ref in ((0, out_ref), (dim, recv_ref), (2 * dim, send_ref)):
        ref[...] = read(a_half, b_half, start, dim)
    ref = embed_ref
    ref[...] = read(a_half, b_half, 3 * dim, half)[0 : ref.shape[0], :]


def trade(below, above, west, east):
    bands = lax.axis_size(BAND)
    patches = lax.axis_size(PATCH)
    up = [(i, i + 1) for i in range(bands - 1)]
    down = [(i + 1, i) for i in range(bands - 1)]
    right = [(i, (i + 1) % patches) for i in range(patches)]
    left = [((i + 1) % patches, i) for i in range(patches)]
    return (
        lax.ppermute(above, BAND, up),
        lax.ppermute(below, BAND, down),
        lax.ppermute(east, PATCH, right),
        lax.ppermute(west, PATCH, left),
    )


def swap_cores(value):
    return lax.ppermute(value, "core", [(0, 1), (1, 0)])


def body(
    grid_feats, mesh_feats, cotangent, w_embed, w_send, w_recv, w_out, u_src, u_dst, u_out, v_in, v_out,
    send_rows, enc_src, enc_dst, halo_send, mesh_src, mesh_dst,
):
    chans = grid_feats.shape[1]
    grid_rows = grid_feats.shape[0]
    nodes, dim = mesh_feats.shape
    half = dim // 2
    rim = grid_rows // 16
    keep = grid_rows - 4 * rim
    edges = enc_src.shape[1]
    width = halo_send.shape[3]
    table_rows = nodes + 4 * width
    band = lax.axis_index(BAND)
    flags = jnp.stack([band, lax.axis_size(BAND) - 1 - band]).astype(jnp.int32)
    core = lax.axis_index("core").astype(jnp.int32).reshape(1)
    smem = pl.BlockSpec(memory_space=pltpu.SMEM)
    vmem = pl.BlockSpec(memory_space=pltpu.VMEM)

    grid_cols = grid_feats.T
    own = call(pick_rim_kernel, [shape((chans, rim), BF16)] * 4, 3)(send_rows, grid_cols)
    arrived = trade(*own)
    keep_rows, keep_sender, node_part = call(
        keep_kernel,
        [shape((chans, keep), BF16), shape((keep, dim), BF16), shape((nodes, dim), BF16)],
        7,
    )(send_rows, grid_cols, mesh_feats, w_embed, w_send, w_recv)

    def whole(array):
        dims = array.shape
        return pl.BlockSpec(dims, lambda i: (0,) * len(dims))

    tile = pl.BlockSpec((1, EDGE_TILE), lambda i: (0, i))
    outs = [
        shape((chans, 4 * rim), BF16), shape((edges, dim), BF16), shape((nodes, dim), BF16), shape((nodes, dim), BF16),
    ] + [shape((width, half), BF16)] * 4
    ins = (halo_send, keep_sender, node_part, mesh_feats, w_embed, w_send, w_out, *arrived, own[0], own[1])
    rim_rows, slope, gathered, latent, h00, h01, h10, h11 = call(
        encode_kernel,
        outs,
        20,
        grid=(edges // EDGE_TILE,),
        in_specs=[smem, tile, tile] + [whole(x) for x in ins],
        out_specs=[
            whole(outs[0]), pl.BlockSpec((EDGE_TILE, dim), lambda i: (i, 0)),
        ] + [whole(x) for x in outs[2:]],
        scratch_shapes=[pltpu.VMEM((grid_rows + nodes, dim), BF16), pltpu.VMEM((nodes, dim), F32)],
    )(flags, enc_src, enc_dst, *ins)

    halos = trade(h00, h01, h10, h11)
    outs = [shape((width, half), BF16)] * 4 + [
        shape((nodes, half), BF16), shape((nodes, half), F32), shape((table_rows, half), BF16),
        shape((table_rows + nodes, dim), BF16), shape((nodes, dim), BF16), shape((nodes, half), BF16),
        shape((nodes, dim), BF16), shape((nodes, dim), BF16),
    ]
    (g0, g1, g2, g3, coupled_grad, lower_grad, halo_table, ends, summed, coupled, hidden, hidden_grad) = call(
        mesh_kernel,
        outs,
        12,
        scratch_shapes=[
            pltpu.VMEM((table_rows + nodes, dim), BF16), pltpu.VMEM((mesh_src.shape[1], dim), BF16),
            pltpu.VMEM((nodes, dim), F32), pltpu.VMEM((table_rows + nodes, dim), F32),
        ],
    )(mesh_src, mesh_dst, latent, cotangent, *halos, u_src, u_dst, u_out, v_in, v_out)
    returned = trade(g0, g1, g2, g3)
    a_rows = 5 * half
    a_mine, a_other = call(
        mesh_weight_kernel, [shape((a_rows // 2, dim), BF16)] * 2, 4, in_specs=[smem] + [vmem] * 8,
    )(core, halo_table, ends, summed, coupled, hidden, hidden_grad, coupled_grad, cotangent)
    a_in = swap_cores(a_other)
    lower_grad, a_mine = lax.optimization_barrier((lower_grad, a_mine))

    b_rows = 3 * dim + half
    keep_grad, q0, q1, q2, q3, mesh_grad, b_mine, b_other = call(
        encoder_back_kernel,
        [shape((chans, keep), BF16)] + [shape((chans, rim), BF16)] * 4 + [shape((nodes, dim), F32)]
        + [shape((b_rows // 2, dim), BF16)] * 2,
        25,
        in_specs=[smem] + [vmem] * 18,
        scratch_shapes=[
            pltpu.VMEM((half, dim), F32), pltpu.VMEM((dim, dim), F32),
            pltpu.VMEM((edges, dim), BF16), pltpu.VMEM((nodes, dim), BF16), pltpu.VMEM((nodes, dim), F32),
        ],
    )(
        core, enc_src, enc_dst, halo_send, slope, keep_rows, rim_rows, gathered, mesh_feats, coupled_grad, lower_grad,
        *returned, w_embed, w_send, w_recv, w_out,
    )
    b_in = swap_cores(b_other)
    back = trade(q0, q1, q2, q3)
    grid_grad = call(
        place_kernel,
        shape((chans, grid_rows), BF16),
        5,
        in_specs=[smem] + [vmem] * 8,
        scratch_shapes=[pltpu.VMEM((chans, grid_rows), BF16)],
    )(flags, send_rows, keep_grad, *back, q0, q1)
    chips = lax.axis_size(CHIPS)
    packed = (a_rows + b_rows) // 2
    pair = jnp.concatenate([a_mine.astype(F32) + a_in.astype(F32), b_mine.astype(F32) + b_in.astype(F32)], axis=0)
    pair = pair.astype(BF16).reshape(chips, packed // chips, dim)
    parts = lax.all_to_all(pair, CHIPS, 0, 0)
    total = jnp.sum(parts.astype(F32), axis=0).astype(BF16)
    parts = jnp.broadcast_to(total[None], parts.shape)
    mine = lax.all_to_all(parts, CHIPS, 0, 0).reshape(packed, dim)
    other = swap_cores(mine)
    totals = call(
        functools.partial(unpack_kernel, a_rows),
        [shape((chans, dim), F32)] + [shape((dim, dim), F32)] * 3 + [shape((half, dim), F32)] * 2
        + [shape((dim, half), F32), shape((half, dim), F32), shape((dim, half), F32)],
        5,
        in_specs=[smem] + [vmem] * 2,
    )(core, mine, other)
    return (grid_grad.T, mesh_grad, *totals)


def solution(mesh):
    chips = Mesh(mesh.devices.reshape(mesh.shape["band"] // 2, 2, 4, mesh.shape["patch"] // 4), ("z", "core", "y", "x"))
    everywhere = BAND + PATCH
    rows = P(everywhere, None)
    in_specs = (rows,) * 3 + (P(),) * 9 + (rows,) * 3 + (P(everywhere, None, None, None),) + (rows,) * 2
    out_specs = (rows,) * 2 + (P(),) * 9
    return jax.shard_map(body, mesh=chips, in_specs=in_specs, out_specs=out_specs, check_vma=False)
```

```python
import functools

import jax
import jax.numpy as jnp
from jax import lax
from jax.experimental import pallas as pl
from jax.experimental.pallas import tpu as pltpu
from jax.sharding import Mesh
from jax.sharding import PartitionSpec as P

BF16 = jnp.bfloat16
F32 = jnp.float32
LANES = 128
EDGE_TILE = 1024
ROW_TILE = 512
VMEM_LIMIT = 56 * 1024 * 1024
BAND = ("z", "core")
PATCH = ("y", "x")


def mm(left, right):
    return lax.dot_general(left, right, (((1,), (0,)), ((), ())), preferred_element_type=F32)


def mm_left(left, right):
    return lax.dot_general(left, right, (((0,), (0,)), ((), ())), preferred_element_type=F32)


def mm_right(left, right):
    return lax.dot_general(left, right, (((1,), (1,)), ((), ())), preferred_element_type=F32)


def table_by_row(index, count):
    n = index.shape[1]
    rows = lax.broadcasted_iota(jnp.int32, (count, n), 0)
    return jnp.where(rows == index, 1.0, 0.0).astype(BF16)


def table_by_column(index, count):
    n = index.shape[1]
    parts = []
    for start in range(0, n, LANES):
        width = min(LANES, n - start)
        piece = jnp.broadcast_to(index[:, start : start + width], (LANES, width))
        column = jnp.transpose(piece)
        wide = jnp.concatenate([column] * (count // LANES), axis=1)
        columns = lax.broadcasted_iota(jnp.int32, (width, count), 1)
        parts.append(jnp.where(wide == columns, 1.0, 0.0).astype(BF16))
    return parts[0] if len(parts) == 1 else jnp.concatenate(parts, axis=0)


def table_by_wide(column, count):
    wide = jnp.concatenate([column.astype(F32)] * (count // LANES), axis=1)
    columns = lax.broadcasted_iota(jnp.int32, wide.shape, 1).astype(F32)
    return jnp.where(wide == columns, 1.0, 0.0).astype(BF16)


def silu_both(value):
    sigma = 0.5 * jnp.tanh(0.5 * value) + 0.5
    act = value * sigma
    return act, sigma + act * (1.0 - sigma)


def call(kernel, out_shape, work, **more):
    return pl.pallas_call(
        kernel,
        out_shape=out_shape,
        cost_estimate=pl.CostEstimate(flops=int(work * 1e9), bytes_accessed=int(work * 1e6), transcendentals=0),
        compiler_params=pltpu.CompilerParams(vmem_limit_bytes=VMEM_LIMIT),
        **more,
    )


def shape(dims, kind):
    return jax.ShapeDtypeStruct(tuple(dims), kind)


def pick_rim_kernel(order_ref, grid_ref, *out_refs):
    rim = out_refs[0].shape[1]
    keep = order_ref.shape[1] - 4 * rim
    table = table_by_row(order_ref[:, keep:], grid_ref.shape[1])
    picked = mm(grid_ref[...], table).astype(BF16)
    for k in range(4):
        out_refs[k][...] = picked[:, k * rim : (k + 1) * rim]


def keep_kernel(
    order_ref, src_ref, dst_ref, grid_ref, mesh_ref, embed_ref, send_ref, recv_ref,
    rows_ref, sender_ref, node_ref, column_ref, row_ref, dst_s,
):
    keep = rows_ref.shape[1]
    rows = order_ref.shape[1]
    for start in range(0, rows, LANES):
        piece = jnp.broadcast_to(dst_ref[:, start : start + LANES], (LANES, LANES))
        dst_s[start : start + LANES, :] = jnp.transpose(piece).astype(F32).astype(BF16)
    first = src_ref[:, 0:rows]

    def sort(i, carry):
        start = pl.multiple_of(i * ROW_TILE, ROW_TILE)
        ids = lax.broadcasted_iota(jnp.int32, (ROW_TILE, rows), 0) + start
        table = jnp.where(ids == first, 1.0, 0.0).astype(BF16)
        column = mm(table, dst_s[...])
        column_ref[pl.ds(start, ROW_TILE), :] = column.astype(BF16)
        for k in range(0, ROW_TILE, LANES):
            turned = jnp.transpose(column[k : k + LANES, :])
            row_ref[:, pl.ds(pl.multiple_of(start + k, LANES), LANES)] = turned[0:1, :].astype(jnp.int32)
        return carry

    lax.fori_loop(0, rows // ROW_TILE, sort, 0)
    node_ref[...] = mm(mesh_ref[...], recv_ref[...]).astype(BF16)

    def step(i, carry):
        start = pl.multiple_of(i * ROW_TILE, ROW_TILE)
        table = table_by_row(order_ref[:, pl.ds(start, ROW_TILE)], grid_ref.shape[1])
        rows = mm(grid_ref[...], table).astype(BF16)
        rows_ref[:, pl.ds(start, ROW_TILE)] = rows
        embedded = silu_both(mm_left(rows, embed_ref[...]))[0].astype(BF16)
        sender_ref[pl.ds(start, ROW_TILE), :] = mm(embedded, send_ref[...]).astype(BF16)
        return carry

    lax.fori_loop(0, keep // ROW_TILE, step, 0)


def encode_kernel(
    flag_ref, src_ref, dst_ref, column_ref, row_ref, halo_ref, sender_ref, node_ref, mesh_ref, embed_ref, send_ref, out_w_ref,
    in0, in1, in2, in3, own0, own1,
    rim_ref, slope_ref, gathered_ref, latent_ref, h00, h01, h10, h11,
    table, total,
):
    step = pl.program_id(0)
    keep = sender_ref.shape[0]
    rim = in0.shape[1]
    rows = keep + 4 * rim
    nodes = node_ref.shape[0]

    @pl.when(step == 0)
    def _():
        table[0:keep, :] = sender_ref[...]
        table[rows : rows + nodes, :] = node_ref[...]
        rim_ref[:, 0:rim] = jnp.where(flag_ref[0] > 0, in0[...], own0[...])
        rim_ref[:, rim : 2 * rim] = jnp.where(flag_ref[1] > 0, in1[...], own1[...])
        rim_ref[:, 2 * rim : 3 * rim] = in2[...]
        rim_ref[:, 3 * rim : 4 * rim] = in3[...]
        embedded = silu_both(mm_left(rim_ref[...], embed_ref[...]))[0].astype(BF16)
        table[keep:rows, :] = mm(embedded, send_ref[...]).astype(BF16)
        total[...] = jnp.zeros_like(total)

    def finish(value, by_row):
        act, slope = silu_both(value)
        slope_ref[...] = slope.astype(BF16)
        total[...] += mm(by_row, act.astype(BF16))

    tile = slope_ref.shape[0]
    early = rows // tile

    @pl.when(step < early)
    def _():
        start = pl.multiple_of(step * tile, tile)
        node = mm(table_by_wide(column_ref[...], nodes), node_ref[...])
        finish(table[pl.ds(start, tile), :].astype(F32) + node, table_by_row(row_ref[...], nodes))

    @pl.when(step >= early)
    def _():
        both = jnp.concatenate([table_by_column(src_ref[...], rows), table_by_column(dst_ref[...], nodes)], axis=1)
        finish(mm(both, table[...]), table_by_row(dst_ref[...], nodes))

    @pl.when(step == pl.num_programs(0) - 1)
    def _():
        gathered = total[...].astype(BF16)
        gathered_ref[...] = gathered
        latent = (mesh_ref[...].astype(F32) + mm(gathered, out_w_ref[...])).astype(BF16)
        latent_ref[...] = latent
        lower = latent[:, latent.shape[1] // 2 :]
        for a, b, ref in ((0, 0, h00), (0, 1, h01), (1, 0, h10), (1, 1, h11)):
            pick = table_by_row(halo_ref[0, a, b : b + 1, :], nodes)
            ref[...] = mm_left(pick, lower).astype(BF16)


def mesh_kernel(
    src_ref, dst_ref, latent_ref, cot_ref, b0, b1, b2, b3, u_src_ref, u_dst_ref, u_out_ref, v_in_ref, v_out_ref,
    g0, g1, g2, g3, coupled_grad_ref, lower_grad_ref, halo_table_ref, ends_ref, summed_ref, coupled_ref, hidden_ref, hidden_grad_ref,
    table, slope_s, total, ends,
):
    nodes = latent_ref.shape[0]
    half = latent_ref.shape[1] // 2
    width = b0.shape[0]
    rows = nodes + 4 * width
    upper = latent_ref[:, :half]
    lower = latent_ref[:, half:]
    halo_table_ref[0:nodes, :] = lower
    for k, ref in enumerate((b0, b1, b2, b3)):
        halo_table_ref[nodes + k * width : nodes + (k + 1) * width, :] = ref[...]
    table[0:rows, :] = mm(halo_table_ref[...], u_src_ref[...]).astype(BF16)
    table[rows : rows + nodes, :] = mm(lower, u_dst_ref[...]).astype(BF16)
    total[...] = jnp.zeros_like(total)
    ends[...] = jnp.zeros_like(ends)
    steps = src_ref.shape[1] // EDGE_TILE

    def forward(i, carry):
        start = pl.multiple_of(i * EDGE_TILE, EDGE_TILE)
        src = src_ref[:, pl.ds(start, EDGE_TILE)]
        dst = dst_ref[:, pl.ds(start, EDGE_TILE)]
        both = jnp.concatenate([table_by_column(src, rows), table_by_column(dst, nodes)], axis=1)
        act, slope = silu_both(mm(both, table[...]))
        slope_s[pl.ds(start, EDGE_TILE), :] = slope.astype(BF16)
        total[...] += mm(table_by_row(dst, nodes), act.astype(BF16))
        return carry

    lax.fori_loop(0, steps, forward, 0)
    summed = total[...].astype(BF16)
    summed_ref[...] = summed
    coupled = (upper.astype(F32) + mm(summed, u_out_ref[...])).astype(BF16)
    coupled_ref[...] = coupled
    act, slope = silu_both(mm(coupled, v_in_ref[...]))
    hidden_ref[...] = act.astype(BF16)
    upper_cot = cot_ref[:, :half]
    lower_cot = cot_ref[:, half:]
    hidden_grad = (mm_right(lower_cot, v_out_ref[...]) * slope).astype(BF16)
    hidden_grad_ref[...] = hidden_grad
    coupled_grad = (upper_cot.astype(F32) + mm_right(hidden_grad, v_in_ref[...])).astype(BF16)
    coupled_grad_ref[...] = coupled_grad
    summed_grad = mm_right(coupled_grad, u_out_ref[...]).astype(BF16)

    def backward(i, carry):
        start = pl.multiple_of(i * EDGE_TILE, EDGE_TILE)
        src = src_ref[:, pl.ds(start, EDGE_TILE)]
        dst = dst_ref[:, pl.ds(start, EDGE_TILE)]
        grad = mm(table_by_column(dst, nodes), summed_grad) * slope_s[pl.ds(start, EDGE_TILE), :].astype(F32)
        both = jnp.concatenate([table_by_row(src, rows), table_by_row(dst, nodes)], axis=0)
        ends[...] += mm(both, grad.astype(BF16))
        return carry

    lax.fori_loop(0, steps, backward, 0)
    ends_ref[...] = ends[...].astype(BF16)
    source_grad = ends_ref[0:rows, :]
    target_grad = ends_ref[rows : rows + nodes, :]
    table_grad = mm_right(source_grad, u_src_ref[...])
    lower_grad_ref[...] = lower_cot.astype(F32) + mm_right(target_grad, u_dst_ref[...]) + table_grad[0:nodes, :]
    for k, ref in enumerate((g0, g1, g2, g3)):
        ref[...] = table_grad[nodes + k * width : nodes + (k + 1) * width, :].astype(BF16)


def store_halves(core_ref, mine_ref, other_ref, start, value):
    half = mine_ref.shape[0]
    value = value.astype(BF16)
    done = 0
    while done < value.shape[0]:
        row = start + done
        count = min(value.shape[0] - done, half - row % half)
        piece = value[done : done + count, :]
        here = row % half

        @pl.when(core_ref[0] == row // half)
        def _(piece=piece, here=here, count=count):
            mine_ref[here : here + count, :] = piece

        @pl.when(core_ref[0] != row // half)
        def _(piece=piece, here=here, count=count):
            other_ref[here : here + count, :] = piece

        done += count


def side_by_side(value):
    rows = value.shape[0] // 2
    return jnp.concatenate([value[:rows, :], value[rows:, :]], axis=1)


def mesh_weight_kernel(
    core_ref, halo_table_ref, ends_ref, summed_ref, coupled_ref, hidden_ref, hidden_grad_ref, coupled_grad_ref, cot_ref,
    mine_ref, other_ref,
):
    rows = halo_table_ref.shape[0]
    nodes, half = coupled_ref.shape
    parts = (
        mm_left(halo_table_ref[...], ends_ref[0:rows, :]),
        mm_left(halo_table_ref[0:nodes, :], ends_ref[rows : rows + nodes, :]),
        side_by_side(mm_left(summed_ref[...], coupled_grad_ref[...])),
        mm_left(coupled_ref[...], hidden_grad_ref[...]),
        side_by_side(mm_left(hidden_ref[...], cot_ref[:, half:])),
    )
    start = 0
    for part in parts:
        store_halves(core_ref, mine_ref, other_ref, start, part)
        start += part.shape[0]


def encoder_back_kernel(
    core_ref, src_ref, dst_ref, column_ref, row_ref, halo_ref, slope_ref, keep_rows_ref, rim_rows_ref, gathered_ref, mesh_ref,
    coupled_grad_ref, lower_grad_ref, r0, r1, r2, r3, embed_ref, send_ref, recv_ref, out_w_ref,
    keep_grad_ref, g0, g1, g2, g3, mesh_grad_ref, mine_ref, other_ref,
    grad_embed_ref, grad_send_ref, edge_s, latent_s, nodes_s,
):
    nodes = mesh_ref.shape[0]
    keep = keep_rows_ref.shape[1]
    rim = g0.shape[1]
    lower_grad = lower_grad_ref[...]
    for a, b, ref in ((0, 0, r0), (0, 1, r1), (1, 0, r2), (1, 1, r3)):
        lower_grad += mm(table_by_row(halo_ref[0, a, b : b + 1, :], nodes), ref[...])
    half = lower_grad.shape[1]
    latent_s[:, :half] = coupled_grad_ref[...]
    latent_s[:, half:] = lower_grad.astype(BF16)
    latent_grad = latent_s[...]
    dim = latent_grad.shape[1]
    store_halves(core_ref, mine_ref, other_ref, 0, mm_left(gathered_ref[...], latent_grad))
    gathered_grad = mm_right(latent_grad, out_w_ref[...]).astype(BF16)
    nodes_s[...] = jnp.zeros_like(nodes_s)

    rows = column_ref.shape[0]

    def edge(start, by_column, by_row):
        grad = mm(by_column, gathered_grad) * slope_ref[pl.ds(start, EDGE_TILE), :].astype(F32)
        grad = grad.astype(BF16)
        edge_s[pl.ds(start, EDGE_TILE), :] = grad
        nodes_s[...] += mm(by_row, grad)

    def first(i, carry):
        start = pl.multiple_of(i * EDGE_TILE, EDGE_TILE)
        column = column_ref[pl.ds(start, EDGE_TILE), :]
        edge(start, table_by_wide(column, nodes), table_by_row(row_ref[:, pl.ds(start, EDGE_TILE)], nodes))
        return carry

    def later(i, carry):
        start = pl.multiple_of(i * EDGE_TILE, EDGE_TILE)
        dst = dst_ref[:, pl.ds(start, EDGE_TILE)]
        edge(start, table_by_column(dst, nodes), table_by_row(dst, nodes))
        return carry

    lax.fori_loop(0, rows // EDGE_TILE, first, 0)
    lax.fori_loop(rows // EDGE_TILE, src_ref.shape[1] // EDGE_TILE, later, 0)
    node_grad = nodes_s[...].astype(BF16)
    store_halves(core_ref, mine_ref, other_ref, dim, mm_left(mesh_ref[...], node_grad))
    mesh_grad_ref[...] = latent_grad.astype(F32) + mm_right(node_grad, recv_ref[...])
    grad_embed_ref[...] = jnp.zeros_like(grad_embed_ref)
    grad_send_ref[...] = jnp.zeros_like(grad_send_ref)

    extra = src_ref[:, rows:]

    def back(cols, start, count):
        ids = lax.broadcasted_iota(jnp.int32, (count, extra.shape[1]), 0) + start
        table = jnp.where(ids == extra, 1.0, 0.0).astype(BF16)
        own = edge_s[pl.ds(start, count), :].astype(F32)
        sender_grad = (own + mm(table, edge_s[rows:, :])).astype(BF16)
        act, slope = silu_both(mm_left(cols, embed_ref[...]))
        grad_send_ref[...] += mm_left(act.astype(BF16), sender_grad)
        embedded_grad = mm_right(sender_grad, send_ref[...]).astype(BF16)
        embed_grad = (embedded_grad.astype(F32) * slope).astype(BF16)
        grad_embed_ref[0 : cols.shape[0], :] += mm(cols, embed_grad)
        return mm_right(embed_ref[...], embed_grad).astype(BF16)

    rim_grad = back(rim_rows_ref[...], keep, 4 * rim)
    for k, ref in enumerate((g0, g1, g2, g3)):
        ref[...] = rim_grad[:, k * rim : (k + 1) * rim]

    def kept(i, carry):
        start = pl.multiple_of(i * ROW_TILE, ROW_TILE)
        keep_grad_ref[:, pl.ds(start, ROW_TILE)] = back(keep_rows_ref[:, pl.ds(start, ROW_TILE)], start, ROW_TILE)
        return carry

    lax.fori_loop(0, keep // ROW_TILE, kept, 0)
    store_halves(core_ref, mine_ref, other_ref, 2 * dim, grad_send_ref[...])
    store_halves(core_ref, mine_ref, other_ref, 3 * dim, grad_embed_ref[...])


def place_kernel(flag_ref, order_ref, keep_ref, in0, in1, in2, in3, own0, own1, grid_grad_ref, all_s):
    keep = keep_ref.shape[1]
    rim = in0.shape[1]
    all_s[:, 0:keep] = keep_ref[...]
    all_s[:, keep : keep + rim] = jnp.where(flag_ref[0] > 0, in0[...], own0[...])
    all_s[:, keep + rim : keep + 2 * rim] = jnp.where(flag_ref[1] > 0, in1[...], own1[...])
    all_s[:, keep + 2 * rim : keep + 3 * rim] = in2[...]
    all_s[:, keep + 3 * rim : keep + 4 * rim] = in3[...]

    def place(i, carry):
        start = pl.multiple_of(i * ROW_TILE, ROW_TILE)
        ids = lax.broadcasted_iota(jnp.int32, (ROW_TILE, order_ref.shape[1]), 0) + start
        table = jnp.where(ids == order_ref[...], 1.0, 0.0).astype(BF16)
        grid_grad_ref[:, pl.ds(start, ROW_TILE)] = mm_right(all_s[...], table).astype(BF16)
        return carry

    lax.fori_loop(0, grid_grad_ref.shape[1] // ROW_TILE, place, 0)


def unpack_kernel(a_rows, core_ref, mine_ref, other_ref, embed_ref, send_ref, recv_ref, out_ref, u_src_ref, u_dst_ref, u_out_ref, v_in_ref, v_out_ref):
    first = core_ref[0] == 0

    def read(base, half, start, count):
        pieces = []
        while count > 0:
            here = start % half
            some = min(count, half - here)
            mine = mine_ref[base + here : base + here + some, :]
            other = other_ref[base + here : base + here + some, :]
            pieces.append(jnp.where(first == (start < half), mine, other))
            start += some
            count -= some
        value = pieces[0] if len(pieces) == 1 else jnp.concatenate(pieces, axis=0)
        return value.astype(F32)

    dim, half = v_out_ref.shape
    a_half = a_rows // 2
    b_half = mine_ref.shape[0] - a_half
    for start, ref in ((0, u_src_ref), (half, u_dst_ref), (3 * half, v_in_ref)):
        ref[...] = read(0, a_half, start, half)
    for start, ref in ((2 * half, u_out_ref), (4 * half, v_out_ref)):
        value = read(0, a_half, start, half)
        ref[0:half, :] = value[:, :half]
        ref[half:, :] = value[:, half:]
    for start, ref in ((0, out_ref), (dim, recv_ref), (2 * dim, send_ref)):
        ref[...] = read(a_half, b_half, start, dim)
    ref = embed_ref
    ref[...] = read(a_half, b_half, 3 * dim, half)[0 : ref.shape[0], :]


def trade(below, above, west, east):
    bands = lax.axis_size(BAND)
    patches = lax.axis_size(PATCH)
    up = [(i, i + 1) for i in range(bands - 1)]
    down = [(i + 1, i) for i in range(bands - 1)]
    right = [(i, (i + 1) % patches) for i in range(patches)]
    left = [((i + 1) % patches, i) for i in range(patches)]
    return (
        lax.ppermute(above, BAND, up),
        lax.ppermute(below, BAND, down),
        lax.ppermute(east, PATCH, right),
        lax.ppermute(west, PATCH, left),
    )


def swap_cores(value):
    return lax.ppermute(value, "core", [(0, 1), (1, 0)])


def body(
    grid_feats, mesh_feats, cotangent, w_embed, w_send, w_recv, w_out, u_src, u_dst, u_out, v_in, v_out,
    send_rows, enc_src, enc_dst, halo_send, mesh_src, mesh_dst,
):
    chans = grid_feats.shape[1]
    grid_rows = grid_feats.shape[0]
    nodes, dim = mesh_feats.shape
    half = dim // 2
    rim = grid_rows // 16
    keep = grid_rows - 4 * rim
    edges = enc_src.shape[1]
    width = halo_send.shape[3]
    table_rows = nodes + 4 * width
    band = lax.axis_index(BAND)
    flags = jnp.stack([band, lax.axis_size(BAND) - 1 - band]).astype(jnp.int32)
    core = lax.axis_index("core").astype(jnp.int32).reshape(1)
    smem = pl.BlockSpec(memory_space=pltpu.SMEM)
    vmem = pl.BlockSpec(memory_space=pltpu.VMEM)

    grid_cols = grid_feats.T
    own = call(pick_rim_kernel, [shape((chans, rim), BF16)] * 4, 3)(send_rows, grid_cols)
    arrived = trade(*own)
    keep_rows, keep_sender, node_part, column, row = call(
        keep_kernel,
        [
            shape((chans, keep), BF16), shape((keep, dim), BF16), shape((nodes, dim), BF16),
            shape((grid_rows, LANES), BF16), shape((1, grid_rows), jnp.int32),
        ],
        9,
        scratch_shapes=[pltpu.VMEM((grid_rows, LANES), BF16)],
    )(send_rows, enc_src, enc_dst, grid_cols, mesh_feats, w_embed, w_send, w_recv)

    def whole(array):
        dims = array.shape
        return pl.BlockSpec(dims, lambda i: (0,) * len(dims))

    early = grid_rows // EDGE_TILE
    tile = pl.BlockSpec((1, EDGE_TILE), lambda i: (0, jnp.maximum(i, early)))
    column_tile = pl.BlockSpec((EDGE_TILE, LANES), lambda i: (jnp.minimum(i, early - 1), 0))
    row_tile = pl.BlockSpec((1, EDGE_TILE), lambda i: (0, jnp.minimum(i, early - 1)))
    outs = [
        shape((chans, 4 * rim), BF16), shape((edges, dim), BF16), shape((nodes, dim), BF16), shape((nodes, dim), BF16),
    ] + [shape((width, half), BF16)] * 4
    ins = (halo_send, keep_sender, node_part, mesh_feats, w_embed, w_send, w_out, *arrived, own[0], own[1])
    rim_rows, slope, gathered, latent, h00, h01, h10, h11 = call(
        encode_kernel,
        outs,
        20,
        grid=(edges // EDGE_TILE,),
        in_specs=[smem, tile, tile, column_tile, row_tile] + [whole(x) for x in ins],
        out_specs=[
            whole(outs[0]), pl.BlockSpec((EDGE_TILE, dim), lambda i: (i, 0)),
        ] + [whole(x) for x in outs[2:]],
        scratch_shapes=[pltpu.VMEM((grid_rows + nodes, dim), BF16), pltpu.VMEM((nodes, dim), F32)],
    )(flags, enc_src, enc_dst, column, row, *ins)

    halos = trade(h00, h01, h10, h11)
    outs = [shape((width, half), BF16)] * 4 + [
        shape((nodes, half), BF16), shape((nodes, half), F32), shape((table_rows, half), BF16),
        shape((table_rows + nodes, dim), BF16), shape((nodes, dim), BF16), shape((nodes, half), BF16),
        shape((nodes, dim), BF16), shape((nodes, dim), BF16),
    ]
    (g0, g1, g2, g3, coupled_grad, lower_grad, halo_table, ends, summed, coupled, hidden, hidden_grad) = call(
        mesh_kernel,
        outs,
        12,
        scratch_shapes=[
            pltpu.VMEM((table_rows + nodes, dim), BF16), pltpu.VMEM((mesh_src.shape[1], dim), BF16),
            pltpu.VMEM((nodes, dim), F32), pltpu.VMEM((table_rows + nodes, dim), F32),
        ],
    )(mesh_src, mesh_dst, latent, cotangent, *halos, u_src, u_dst, u_out, v_in, v_out)
    returned = trade(g0, g1, g2, g3)
    a_rows = 5 * half
    a_mine, a_other = call(
        mesh_weight_kernel, [shape((a_rows // 2, dim), BF16)] * 2, 4, in_specs=[smem] + [vmem] * 8,
    )(core, halo_table, ends, summed, coupled, hidden, hidden_grad, coupled_grad, cotangent)
    a_in = swap_cores(a_other)
    lower_grad, a_mine = lax.optimization_barrier((lower_grad, a_mine))

    b_rows = 3 * dim + half
    keep_grad, q0, q1, q2, q3, mesh_grad, b_mine, b_other = call(
        encoder_back_kernel,
        [shape((chans, keep), BF16)] + [shape((chans, rim), BF16)] * 4 + [shape((nodes, dim), F32)]
        + [shape((b_rows // 2, dim), BF16)] * 2,
        25,
        in_specs=[smem] + [vmem] * 20,
        scratch_shapes=[
            pltpu.VMEM((half, dim), F32), pltpu.VMEM((dim, dim), F32),
            pltpu.VMEM((edges, dim), BF16), pltpu.VMEM((nodes, dim), BF16), pltpu.VMEM((nodes, dim), F32),
        ],
    )(
        core, enc_src, enc_dst, column, row, halo_send, slope, keep_rows, rim_rows, gathered, mesh_feats, coupled_grad, lower_grad,
        *returned, w_embed, w_send, w_recv, w_out,
    )
    b_in = swap_cores(b_other)
    back = trade(q0, q1, q2, q3)
    grid_grad = call(
        place_kernel,
        shape((chans, grid_rows), BF16),
        5,
        in_specs=[smem] + [vmem] * 8,
        scratch_shapes=[pltpu.VMEM((chans, grid_rows), BF16)],
    )(flags, send_rows, keep_grad, *back, q0, q1)
    patches = lax.axis_size(PATCH)
    packed = (a_rows + b_rows) // 2
    pair = jnp.concatenate([a_mine.astype(F32) + a_in.astype(F32), b_mine.astype(F32) + b_in.astype(F32)], axis=0)
    pair = pair.astype(BF16).reshape(patches, packed // patches, dim)
    parts = lax.all_to_all(pair, PATCH, 0, 0)
    part = jnp.sum(parts.astype(F32), axis=0).astype(BF16)
    away = [part] + [lax.ppermute(part, "z", [(i, (i + k) % 4) for i in range(4)]) for k in (1, 2, 3)]
    away = [piece.astype(F32) for piece in away]
    total = ((away[0] + away[2]) + (away[1] + away[3])).astype(BF16)
    mine = lax.all_to_all(jnp.broadcast_to(total[None], parts.shape), PATCH, 0, 0).reshape(packed, dim)
    other = swap_cores(mine)
    totals = call(
        functools.partial(unpack_kernel, a_rows),
        [shape((chans, dim), F32)] + [shape((dim, dim), F32)] * 3 + [shape((half, dim), F32)] * 2
        + [shape((dim, half), F32), shape((half, dim), F32), shape((dim, half), F32)],
        5,
        in_specs=[smem] + [vmem] * 2,
    )(core, mine, other)
    return (grid_grad.T, mesh_grad, *totals)


def solution(mesh):
    chips = Mesh(mesh.devices.reshape(mesh.shape["band"] // 2, 2, 4, mesh.shape["patch"] // 4), ("z", "core", "y", "x"))
    everywhere = BAND + PATCH
    rows = P(everywhere, None)
    in_specs = (rows,) * 3 + (P(),) * 9 + (rows,) * 3 + (P(everywhere, None, None, None),) + (rows,) * 2
    out_specs = (rows,) * 2 + (P(),) * 9
    return jax.shard_map(body, mesh=chips, in_specs=in_specs, out_specs=out_specs, check_vma=False)
```

```python
import functools

import jax
import jax.numpy as jnp
from jax import lax
from jax.experimental import pallas as pl
from jax.experimental.pallas import tpu as pltpu
from jax.sharding import Mesh
from jax.sharding import PartitionSpec as P

BF16 = jnp.bfloat16
F32 = jnp.float32
LANES = 128
EDGE_TILE = 1024
ROW_TILE = 512
VMEM_LIMIT = 32 * 1024 * 1024
PIECES = 4
BAND = ("z", "core")
PATCH = ("y", "x")


def mm(left, right):
    return lax.dot_general(left, right, (((1,), (0,)), ((), ())), preferred_element_type=F32)


def mm_left(left, right):
    return lax.dot_general(left, right, (((0,), (0,)), ((), ())), preferred_element_type=F32)


def mm_right(left, right):
    return lax.dot_general(left, right, (((1,), (1,)), ((), ())), preferred_element_type=F32)


def table_by_row(index, count):
    n = index.shape[1]
    rows = lax.broadcasted_iota(jnp.int32, (count, n), 0)
    return jnp.where(rows == index, 1.0, 0.0).astype(BF16)


def table_by_column(index, count):
    n = index.shape[1]
    parts = []
    for start in range(0, n, LANES):
        width = min(LANES, n - start)
        piece = jnp.broadcast_to(index[:, start : start + width], (LANES, width))
        column = jnp.transpose(piece)
        wide = jnp.concatenate([column] * (count // LANES), axis=1)
        columns = lax.broadcasted_iota(jnp.int32, (width, count), 1)
        parts.append(jnp.where(wide == columns, 1.0, 0.0).astype(BF16))
    return parts[0] if len(parts) == 1 else jnp.concatenate(parts, axis=0)


def table_by_wide(column, count):
    wide = jnp.concatenate([column.astype(F32)] * (count // LANES), axis=1)
    columns = lax.broadcasted_iota(jnp.int32, wide.shape, 1).astype(F32)
    return jnp.where(wide == columns, 1.0, 0.0).astype(BF16)


def silu_both(value):
    sigma = 0.5 * jnp.tanh(0.5 * value) + 0.5
    act = value * sigma
    return act, sigma + act * (1.0 - sigma)


class Sent:
    def __init__(self, target, buffer, semaphores):
        self.target, self.buffer, self.semaphores = target, buffer, semaphores
        self.shape = buffer.shape
        self.copies = []

    def __setitem__(self, index, value):
        self.buffer[index] = value

    def __getitem__(self, index):
        return self.buffer[index]

    def send(self, start=0, count=None):
        rows = pl.ds(start, self.shape[0] if count is None else count)
        copy = pltpu.make_async_copy(self.buffer.at[rows], self.target.at[rows], self.semaphores.at[len(self.copies)])
        copy.start()
        self.copies.append(copy)


def call(kernel, out_shape, work, args, scalars=0, sent=(), scratch=()):
    outs = list(out_shape)
    buffers = [pltpu.VMEM(outs[k].shape, outs[k].dtype) for k in sent]
    buffers += [pltpu.SemaphoreType.DMA((PIECES,)) for _ in sent]

    def run(*refs):
        ins, results, rest = refs[: len(args)], list(refs[len(args) : len(args) + len(outs)]), refs[len(args) + len(outs) :]
        for k, place in enumerate(sent):
            results[place] = Sent(results[place], rest[k], rest[len(sent) + k])
        kernel(*ins, *results, *rest[len(buffers) :])
        for place in sent:
            for copy in results[place].copies:
                copy.wait()

    spaces = [pltpu.SMEM] * scalars + [pltpu.VMEM] * (len(args) - scalars)
    return pl.pallas_call(
        run,
        out_shape=outs,
        in_specs=[pl.BlockSpec(memory_space=space) for space in spaces],
        out_specs=[pl.BlockSpec(memory_space=pl.ANY if k in sent else pltpu.VMEM) for k in range(len(outs))],
        scratch_shapes=buffers + list(scratch),
        cost_estimate=pl.CostEstimate(flops=int(work * 1e9), bytes_accessed=int(work * 1e6), transcendentals=0),
        compiler_params=pltpu.CompilerParams(vmem_limit_bytes=VMEM_LIMIT),
    )(*args)


def shape(dims, kind):
    return jax.ShapeDtypeStruct(tuple(dims), kind)


def pick_rim_kernel(order_ref, grid_ref, *out_refs):
    rim = out_refs[0].shape[1]
    keep = order_ref.shape[1] - 4 * rim
    table = table_by_row(order_ref[:, keep:], grid_ref.shape[1])
    picked = mm(grid_ref[...], table).astype(BF16)
    for k in range(4):
        out_refs[k][...] = picked[:, k * rim : (k + 1) * rim]


def keep_kernel(
    order_ref, src_ref, dst_ref, grid_ref, mesh_ref, embed_ref, send_ref, recv_ref,
    rows_ref, sender_ref, node_ref, column_ref, row_ref, dst_s,
):
    keep = rows_ref.shape[1]
    rows = order_ref.shape[1]
    for start in range(0, rows, LANES):
        piece = jnp.broadcast_to(dst_ref[:, start : start + LANES], (LANES, LANES))
        dst_s[start : start + LANES, :] = jnp.transpose(piece).astype(F32).astype(BF16)
    first = src_ref[:, 0:rows]

    for start in range(0, rows, ROW_TILE):
        ids = lax.broadcasted_iota(jnp.int32, (ROW_TILE, rows), 0) + start
        table = jnp.where(ids == first, 1.0, 0.0).astype(BF16)
        column = mm(table, dst_s[...])
        column_ref[start : start + ROW_TILE, :] = column.astype(BF16)
        for k in range(0, ROW_TILE, LANES):
            turned = jnp.transpose(column[k : k + LANES, :])
            row_ref[:, start + k : start + k + LANES] = turned[0:1, :].astype(jnp.int32)
    for start in range(0, keep, ROW_TILE):
        stop = start + ROW_TILE
        table = table_by_row(order_ref[:, start:stop], grid_ref.shape[1])
        cols = mm(grid_ref[...], table).astype(BF16)
        rows_ref[:, start:stop] = cols
        embedded = silu_both(mm_left(cols, embed_ref[...]))[0].astype(BF16)
        sender_ref[start:stop, :] = mm(embedded, send_ref[...]).astype(BF16)
    node_ref[...] = mm(mesh_ref[...], recv_ref[...]).astype(BF16)


def encode_kernel(
    flag_ref, src_ref, dst_ref, row_ref, halo_ref, in0, in1, in2, in3, own0, own1, embed_ref, send_ref,
    sender_ref, node_ref, column_ref, out_w_ref, mesh_ref,
    rim_ref, slope0, slope1, gathered_ref, latent_ref, h00, h01, h10, h11,
    table, total,
):
    keep = sender_ref.shape[0]
    rim = in0.shape[1]
    rows = keep + 4 * rim
    nodes = node_ref.shape[0]
    rim_ref[:, 0:rim] = jnp.where(flag_ref[0] > 0, in0[...], own0[...])
    rim_ref[:, rim : 2 * rim] = jnp.where(flag_ref[1] > 0, in1[...], own1[...])
    rim_ref[:, 2 * rim : 3 * rim] = in2[...]
    rim_ref[:, 3 * rim : 4 * rim] = in3[...]
    embedded = silu_both(mm_left(rim_ref[...], embed_ref[...]))[0].astype(BF16)
    table[keep:rows, :] = mm(embedded, send_ref[...]).astype(BF16)
    table[0:keep, :] = sender_ref[...]
    table[rows : rows + nodes, :] = node_ref[...]
    for start in range(0, src_ref.shape[1], EDGE_TILE):
        stop = start + EDGE_TILE
        if start < rows:
            node = mm(table_by_wide(column_ref[start:stop, :], nodes), node_ref[...])
            value = table[start:stop, :].astype(F32) + node
            by_row = table_by_row(row_ref[:, start:stop], nodes)
        else:
            src = src_ref[:, start:stop]
            dst = dst_ref[:, start:stop]
            both = jnp.concatenate([table_by_column(src, rows), table_by_column(dst, nodes)], axis=1)
            value = mm(both, table[...])
            by_row = table_by_row(dst, nodes)
        act, slope = silu_both(value)
        ref, base = (slope0, 0) if start < rows else (slope1, rows)
        ref[start - base : stop - base, :] = slope.astype(BF16)
        part = mm(by_row, act.astype(BF16))
        total[...] = part if start == 0 else total[...] + part
    gathered = total[...].astype(BF16)
    gathered_ref[...] = gathered
    latent = (mesh_ref[...].astype(F32) + mm(gathered, out_w_ref[...])).astype(BF16)
    latent_ref[...] = latent
    lower = latent[:, latent.shape[1] // 2 :]
    for a, b, ref in ((0, 0, h00), (0, 1, h01), (1, 0, h10), (1, 1, h11)):
        pick = table_by_row(halo_ref[0, a, b : b + 1, :], nodes)
        ref[...] = mm_left(pick, lower).astype(BF16)


def mesh_kernel(
    src_ref, dst_ref, latent_ref, cot_ref, b0, b1, b2, b3, u_src_ref, u_dst_ref, u_out_ref, v_in_ref, v_out_ref,
    g0, g1, g2, g3, coupled_grad_ref, lower_grad_ref, halo_table_ref, ends_ref, summed_ref, coupled_ref, hidden_ref, hidden_grad_ref,
    table, slope_s, total, ends,
):
    nodes = latent_ref.shape[0]
    half = latent_ref.shape[1] // 2
    width = b0.shape[0]
    rows = nodes + 4 * width
    upper = latent_ref[:, :half]
    lower = latent_ref[:, half:]
    halo_table_ref[0:nodes, :] = lower
    for k, ref in enumerate((b0, b1, b2, b3)):
        halo_table_ref[nodes + k * width : nodes + (k + 1) * width, :] = ref[...]
    table[0:rows, :] = mm(halo_table_ref[...], u_src_ref[...]).astype(BF16)
    table[rows : rows + nodes, :] = mm(lower, u_dst_ref[...]).astype(BF16)
    for start in range(0, src_ref.shape[1], EDGE_TILE):
        stop = start + EDGE_TILE
        src = src_ref[:, start:stop]
        dst = dst_ref[:, start:stop]
        both = jnp.concatenate([table_by_column(src, rows), table_by_column(dst, nodes)], axis=1)
        act, slope = silu_both(mm(both, table[...]))
        slope_s[start:stop, :] = slope.astype(BF16)
        part = mm(table_by_row(dst, nodes), act.astype(BF16))
        total[...] = part if start == 0 else total[...] + part
    summed = total[...].astype(BF16)
    summed_ref[...] = summed
    coupled = (upper.astype(F32) + mm(summed, u_out_ref[...])).astype(BF16)
    coupled_ref[...] = coupled
    act, slope = silu_both(mm(coupled, v_in_ref[...]))
    hidden_ref[...] = act.astype(BF16)
    upper_cot = cot_ref[:, :half]
    lower_cot = cot_ref[:, half:]
    hidden_grad = (mm_right(lower_cot, v_out_ref[...]) * slope).astype(BF16)
    hidden_grad_ref[...] = hidden_grad
    coupled_grad = (upper_cot.astype(F32) + mm_right(hidden_grad, v_in_ref[...])).astype(BF16)
    coupled_grad_ref[...] = coupled_grad
    summed_grad = mm_right(coupled_grad, u_out_ref[...]).astype(BF16)

    for start in range(0, src_ref.shape[1], EDGE_TILE):
        stop = start + EDGE_TILE
        src = src_ref[:, start:stop]
        dst = dst_ref[:, start:stop]
        grad = mm(table_by_column(dst, nodes), summed_grad) * slope_s[start:stop, :].astype(F32)
        both = jnp.concatenate([table_by_row(src, rows), table_by_row(dst, nodes)], axis=0)
        part = mm(both, grad.astype(BF16))
        ends[...] = part if start == 0 else ends[...] + part
    ends_ref[...] = ends[...].astype(BF16)
    source_grad = ends_ref[0:rows, :]
    target_grad = ends_ref[rows : rows + nodes, :]
    table_grad = mm_right(source_grad, u_src_ref[...])
    lower_grad_ref[...] = lower_cot.astype(F32) + mm_right(target_grad, u_dst_ref[...]) + table_grad[0:nodes, :]
    for k, ref in enumerate((g0, g1, g2, g3)):
        ref[...] = table_grad[nodes + k * width : nodes + (k + 1) * width, :].astype(BF16)


def store_halves(core_ref, mine_ref, other_ref, start, value):
    half = mine_ref.shape[0]
    value = value.astype(BF16)
    done = 0
    while done < value.shape[0]:
        row = start + done
        count = min(value.shape[0] - done, half - row % half)
        piece = value[done : done + count, :]
        here = row % half

        @pl.when(core_ref[0] == row // half)
        def _(piece=piece, here=here, count=count):
            mine_ref[here : here + count, :] = piece

        @pl.when(core_ref[0] != row // half)
        def _(piece=piece, here=here, count=count):
            other_ref[here : here + count, :] = piece

        done += count


def side_by_side(value):
    rows = value.shape[0] // 2
    return jnp.concatenate([value[:rows, :], value[rows:, :]], axis=1)


def mesh_weight_kernel(
    core_ref, halo_table_ref, ends_ref, summed_ref, coupled_ref, hidden_ref, hidden_grad_ref, coupled_grad_ref, cot_ref,
    mine_ref, other_ref,
):
    rows = halo_table_ref.shape[0]
    nodes, half = coupled_ref.shape
    parts = (
        mm_left(halo_table_ref[...], ends_ref[0:rows, :]),
        mm_left(halo_table_ref[0:nodes, :], ends_ref[rows : rows + nodes, :]),
        side_by_side(mm_left(summed_ref[...], coupled_grad_ref[...])),
        mm_left(coupled_ref[...], hidden_grad_ref[...]),
        side_by_side(mm_left(hidden_ref[...], cot_ref[:, half:])),
    )
    start = 0
    for part in parts:
        store_halves(core_ref, mine_ref, other_ref, start, part)
        start += part.shape[0]


def encoder_back_kernel(
    core_ref, src_ref, dst_ref, row_ref, halo_ref, r0, r1, r2, r3, lower_grad_ref, coupled_grad_ref, out_w_ref,
    column_ref, slope0, slope1, gathered_ref, recv_ref, mesh_ref, rim_rows_ref, embed_ref, send_ref, keep_rows_ref,
    keep_grad_ref, g0, g1, g2, g3, mesh_grad_ref, mine_ref, other_ref,
    edge_s, latent_s, nodes_s,
):
    nodes, dim = mesh_ref.shape
    keep = keep_rows_ref.shape[1]
    rim = g0.shape[1]
    lower_grad = lower_grad_ref[...]
    for a, b, ref in ((0, 0, r0), (0, 1, r1), (1, 0, r2), (1, 1, r3)):
        lower_grad += mm(table_by_row(halo_ref[0, a, b : b + 1, :], nodes), ref[...])
    half = lower_grad.shape[1]
    latent_s[:, :half] = coupled_grad_ref[...]
    latent_s[:, half:] = lower_grad.astype(BF16)
    latent_grad = latent_s[...]
    gathered_grad = mm_right(latent_grad, out_w_ref[...]).astype(BF16)
    rows = column_ref.shape[0]
    for start in range(0, src_ref.shape[1], EDGE_TILE):
        stop = start + EDGE_TILE
        if start < rows:
            by_column = table_by_wide(column_ref[start:stop, :], nodes)
            by_row = table_by_row(row_ref[:, start:stop], nodes)
            slope = slope0[start:stop, :]
        else:
            dst = dst_ref[:, start:stop]
            by_column = table_by_column(dst, nodes)
            by_row = table_by_row(dst, nodes)
            slope = slope1[start - rows : stop - rows, :]
        grad = (mm(by_column, gathered_grad) * slope.astype(F32)).astype(BF16)
        edge_s[start:stop, :] = grad
        part = mm(by_row, grad)
        nodes_s[...] = part if start == 0 else nodes_s[...] + part
    store_halves(core_ref, mine_ref, other_ref, 0, mm_left(gathered_ref[...], latent_grad))
    node_grad = nodes_s[...].astype(BF16)
    store_halves(core_ref, mine_ref, other_ref, dim, mm_left(mesh_ref[...], node_grad))
    mesh_grad_ref[...] = latent_grad.astype(F32) + mm_right(node_grad, recv_ref[...])
    mesh_grad_ref.send()
    extra = src_ref[:, rows:]

    def back(cols, start, count):
        ids = lax.broadcasted_iota(jnp.int32, (count, extra.shape[1]), 0) + start
        table = jnp.where(ids == extra, 1.0, 0.0).astype(BF16)
        own = edge_s[start : start + count, :].astype(F32)
        sender_grad = (own + mm(table, edge_s[rows:, :])).astype(BF16)
        act, slope = silu_both(mm_left(cols, embed_ref[...]))
        embedded_grad = mm_right(sender_grad, send_ref[...]).astype(BF16)
        embed_grad = (embedded_grad.astype(F32) * slope).astype(BF16)
        cols_grad = mm_right(embed_ref[...], embed_grad).astype(BF16)
        return cols_grad, mm_left(act.astype(BF16), sender_grad), mm(cols, embed_grad)

    rim_grad, grad_send, grad_embed = back(rim_rows_ref[...], keep, 4 * rim)
    for k, ref in enumerate((g0, g1, g2, g3)):
        ref[...] = rim_grad[:, k * rim : (k + 1) * rim]
    for start in range(0, keep, ROW_TILE):
        stop = start + ROW_TILE
        cols_grad, send_part, embed_part = back(keep_rows_ref[:, start:stop], start, ROW_TILE)
        keep_grad_ref[:, start:stop] = cols_grad
        grad_send += send_part
        grad_embed += embed_part
    store_halves(core_ref, mine_ref, other_ref, 2 * dim, grad_send)
    pad = jnp.zeros((half - grad_embed.shape[0], dim), F32)
    store_halves(core_ref, mine_ref, other_ref, 3 * dim, jnp.concatenate([grad_embed, pad], axis=0))


def place_kernel(flag_ref, order_ref, keep_ref, in0, in1, in2, in3, own0, own1, grid_grad_ref, all_s):
    keep = keep_ref.shape[1]
    rim = in0.shape[1]
    all_s[:, 0:keep] = keep_ref[...]
    all_s[:, keep : keep + rim] = jnp.where(flag_ref[0] > 0, in0[...], own0[...])
    all_s[:, keep + rim : keep + 2 * rim] = jnp.where(flag_ref[1] > 0, in1[...], own1[...])
    all_s[:, keep + 2 * rim : keep + 3 * rim] = in2[...]
    all_s[:, keep + 3 * rim : keep + 4 * rim] = in3[...]

    for start in range(0, grid_grad_ref.shape[1], ROW_TILE):
        ids = lax.broadcasted_iota(jnp.int32, (ROW_TILE, order_ref.shape[1]), 0) + start
        table = jnp.where(ids == order_ref[...], 1.0, 0.0).astype(BF16)
        grid_grad_ref[:, start : start + ROW_TILE] = mm_right(all_s[...], table).astype(BF16)


def unpack_kernel(a_rows, core_ref, mine_ref, other_ref, embed_ref, send_ref, recv_ref, out_ref, u_src_ref, u_dst_ref, u_out_ref, v_in_ref, v_out_ref):
    first = core_ref[0] == 0

    def read(base, half, start, count):
        pieces = []
        while count > 0:
            here = start % half
            some = min(count, half - here)
            mine = mine_ref[base + here : base + here + some, :]
            other = other_ref[base + here : base + here + some, :]
            pieces.append(jnp.where(first == (start < half), mine, other))
            start += some
            count -= some
        value = pieces[0] if len(pieces) == 1 else jnp.concatenate(pieces, axis=0)
        return value.astype(F32)

    dim, half = v_out_ref.shape
    a_half = a_rows // 2
    b_half = mine_ref.shape[0] - a_half
    for start, ref in ((0, u_src_ref), (half, u_dst_ref), (3 * half, v_in_ref)):
        ref[...] = read(0, a_half, start, half)
        ref.send()
    for start, ref in ((2 * half, u_out_ref), (4 * half, v_out_ref)):
        value = read(0, a_half, start, half)
        ref[0:half, :] = value[:, :half]
        ref[half:, :] = value[:, half:]
        ref.send()
    for start, ref in ((0, out_ref), (dim, recv_ref), (2 * dim, send_ref)):
        ref[...] = read(a_half, b_half, start, dim)
        ref.send()
    ref = embed_ref
    ref[...] = read(a_half, b_half, 3 * dim, half)[0 : ref.shape[0], :]
    ref.send()


def trade(below, above, west, east):
    bands = lax.axis_size(BAND)
    patches = lax.axis_size(PATCH)
    up = [(i, i + 1) for i in range(bands - 1)]
    down = [(i + 1, i) for i in range(bands - 1)]
    right = [(i, (i + 1) % patches) for i in range(patches)]
    left = [((i + 1) % patches, i) for i in range(patches)]
    return (
        lax.ppermute(above, BAND, up),
        lax.ppermute(below, BAND, down),
        lax.ppermute(east, PATCH, right),
        lax.ppermute(west, PATCH, left),
    )


def swap_cores(value):
    return lax.ppermute(value, "core", [(0, 1), (1, 0)])


def body(
    grid_feats, mesh_feats, cotangent, w_embed, w_send, w_recv, w_out, u_src, u_dst, u_out, v_in, v_out,
    send_rows, enc_src, enc_dst, halo_send, mesh_src, mesh_dst,
):
    chans = grid_feats.shape[1]
    grid_rows = grid_feats.shape[0]
    nodes, dim = mesh_feats.shape
    half = dim // 2
    rim = grid_rows // 16
    keep = grid_rows - 4 * rim
    edges = enc_src.shape[1]
    width = halo_send.shape[3]
    table_rows = nodes + 4 * width
    band = lax.axis_index(BAND)
    flags = jnp.stack([band, lax.axis_size(BAND) - 1 - band]).astype(jnp.int32)
    core = lax.axis_index("core").astype(jnp.int32).reshape(1)

    grid_cols = grid_feats.T
    own = call(pick_rim_kernel, [shape((chans, rim), BF16)] * 4, 1, (send_rows, grid_cols))
    arrived = trade(*own)
    outs = [
        shape((chans, keep), BF16), shape((keep, dim), BF16), shape((nodes, dim), BF16),
        shape((grid_rows, LANES), BF16), shape((1, grid_rows), jnp.int32),
    ]
    ins = (send_rows, enc_src, enc_dst, grid_cols, mesh_feats, w_embed, w_send, w_recv)
    keep_rows, keep_sender, node_part, column, row = call(
        keep_kernel, outs, 6, ins, scratch=[pltpu.VMEM((grid_rows, LANES), BF16)]
    )

    outs = [
        shape((chans, 4 * rim), BF16), shape((grid_rows, dim), BF16), shape((edges - grid_rows, dim), BF16),
        shape((nodes, dim), BF16), shape((nodes, dim), BF16),
    ] + [shape((width, half), BF16)] * 4
    ins = (
        flags, enc_src, enc_dst, row, halo_send, *arrived, own[0], own[1], w_embed, w_send,
        keep_sender, node_part, column, w_out, mesh_feats,
    )
    rim_rows, slope0, slope1, gathered, latent, h00, h01, h10, h11 = call(
        encode_kernel, outs, 12, ins, scalars=1,
        scratch=[pltpu.VMEM((grid_rows + nodes, dim), BF16), pltpu.VMEM((nodes, dim), F32)],
    )

    halos = trade(h00, h01, h10, h11)
    outs = [shape((width, half), BF16)] * 4 + [
        shape((nodes, half), BF16), shape((nodes, half), F32), shape((table_rows, half), BF16),
        shape((table_rows + nodes, dim), BF16), shape((nodes, dim), BF16), shape((nodes, half), BF16),
        shape((nodes, dim), BF16), shape((nodes, dim), BF16),
    ]
    ins = (mesh_src, mesh_dst, latent, cotangent, *halos, u_src, u_dst, u_out, v_in, v_out)
    (g0, g1, g2, g3, coupled_grad, lower_grad, halo_table, ends, summed, coupled, hidden, hidden_grad) = call(
        mesh_kernel, outs, 6, ins,
        scratch=[
            pltpu.VMEM((table_rows + nodes, dim), BF16), pltpu.VMEM((mesh_src.shape[1], dim), BF16),
            pltpu.VMEM((nodes, dim), F32), pltpu.VMEM((table_rows + nodes, dim), F32),
        ],
    )
    returned = trade(g0, g1, g2, g3)
    a_rows = 5 * half
    ins = (core, halo_table, ends, summed, coupled, hidden, hidden_grad, coupled_grad, cotangent)
    a_mine, a_other = call(mesh_weight_kernel, [shape((a_rows // 2, dim), BF16)] * 2, 1, ins, scalars=1)
    a_in = swap_cores(a_other)
    lower_grad, a_mine = lax.optimization_barrier((lower_grad, a_mine))

    b_rows = 3 * dim + half
    outs = [shape((chans, keep), BF16)] + [shape((chans, rim), BF16)] * 4 + [shape((nodes, dim), F32)]
    outs += [shape((b_rows // 2, dim), BF16)] * 2
    ins = (
        core, enc_src, enc_dst, row, halo_send, *returned, lower_grad, coupled_grad, w_out,
        column, slope0, slope1, gathered, w_recv, mesh_feats, rim_rows, w_embed, w_send, keep_rows,
    )
    keep_grad, q0, q1, q2, q3, mesh_grad, b_mine, b_other = call(
        encoder_back_kernel, outs, 14, ins, scalars=1, sent=(5,),
        scratch=[pltpu.VMEM((edges, dim), BF16), pltpu.VMEM((nodes, dim), BF16), pltpu.VMEM((nodes, dim), F32)],
    )
    b_in = swap_cores(b_other)
    back = trade(q0, q1, q2, q3)
    ins = (flags, send_rows, keep_grad, *back, q0, q1)
    (grid_grad,) = call(
        place_kernel, [shape((chans, grid_rows), BF16)], 5, ins, scalars=1, scratch=[pltpu.VMEM((chans, grid_rows), BF16)]
    )
    patches = lax.axis_size(PATCH)
    packed = (a_rows + b_rows) // 2
    pair = jnp.concatenate([a_mine.astype(F32) + a_in.astype(F32), b_mine.astype(F32) + b_in.astype(F32)], axis=0)
    pair = pair.astype(BF16).reshape(patches, packed // patches, dim)
    parts = lax.all_to_all(pair, PATCH, 0, 0)
    part = jnp.sum(parts.astype(F32), axis=0).astype(BF16)
    away = [part] + [lax.ppermute(part, "z", [(i, (i + k) % 4) for i in range(4)]) for k in (1, 2, 3)]
    away = [piece.astype(F32) for piece in away]
    total = ((away[0] + away[2]) + (away[1] + away[3])).astype(BF16)
    mine = lax.all_to_all(jnp.broadcast_to(total[None], parts.shape), PATCH, 0, 0).reshape(packed, dim)
    other = swap_cores(mine)
    outs = [shape((chans, dim), F32)] + [shape((dim, dim), F32)] * 3 + [shape((half, dim), F32)] * 2
    outs += [shape((dim, half), F32), shape((half, dim), F32), shape((dim, half), F32)]
    totals = call(functools.partial(unpack_kernel, a_rows), outs, 4, (core, mine, other), scalars=1, sent=tuple(range(9)))
    return (grid_grad.T, mesh_grad, *totals)


def solution(mesh):
    chips = Mesh(mesh.devices.reshape(mesh.shape["band"] // 2, 2, 4, mesh.shape["patch"] // 4), ("z", "core", "y", "x"))
    everywhere = BAND + PATCH
    rows = P(everywhere, None)
    in_specs = (rows,) * 3 + (P(),) * 9 + (rows,) * 3 + (P(everywhere, None, None, None),) + (rows,) * 2
    out_specs = (rows,) * 2 + (P(),) * 9
    return jax.shard_map(body, mesh=chips, in_specs=in_specs, out_specs=out_specs, check_vma=False)
```

```python
import functools

import jax
import jax.numpy as jnp
from jax import lax
from jax.experimental import pallas as pl
from jax.experimental.pallas import tpu as pltpu
from jax.sharding import Mesh
from jax.sharding import PartitionSpec as P

BF16 = jnp.bfloat16
F32 = jnp.float32
LANES = 128
EDGE_TILE = 1024
ROW_TILE = 512
VMEM_LIMIT = 32 * 1024 * 1024
PIECES = 4
BAND = ("z", "core")
PATCH = ("y", "x")


def mm(left, right):
    return lax.dot_general(left, right, (((1,), (0,)), ((), ())), preferred_element_type=F32)


def mm_left(left, right):
    return lax.dot_general(left, right, (((0,), (0,)), ((), ())), preferred_element_type=F32)


def mm_right(left, right):
    return lax.dot_general(left, right, (((1,), (1,)), ((), ())), preferred_element_type=F32)


def table_by_row(index, count):
    n = index.shape[1]
    rows = lax.broadcasted_iota(jnp.int32, (count, n), 0)
    return jnp.where(rows == index, 1.0, 0.0).astype(BF16)


def table_by_column(index, count):
    n = index.shape[1]
    parts = []
    for start in range(0, n, LANES):
        width = min(LANES, n - start)
        piece = jnp.broadcast_to(index[:, start : start + width], (LANES, width))
        column = jnp.transpose(piece)
        wide = jnp.concatenate([column] * (count // LANES), axis=1)
        columns = lax.broadcasted_iota(jnp.int32, (width, count), 1)
        parts.append(jnp.where(wide == columns, 1.0, 0.0).astype(BF16))
    return parts[0] if len(parts) == 1 else jnp.concatenate(parts, axis=0)


def table_by_wide(column, count):
    wide = jnp.concatenate([column.astype(F32)] * (count // LANES), axis=1)
    columns = lax.broadcasted_iota(jnp.int32, wide.shape, 1).astype(F32)
    return jnp.where(wide == columns, 1.0, 0.0).astype(BF16)


def silu_both(value):
    sigma = 0.5 * jnp.tanh(0.5 * value) + 0.5
    act = value * sigma
    return act, sigma + act * (1.0 - sigma)


class Sent:
    def __init__(self, target, buffer, semaphores):
        self.target, self.buffer, self.semaphores = target, buffer, semaphores
        self.shape = buffer.shape
        self.copies = []

    def __setitem__(self, index, value):
        self.buffer[index] = value

    def __getitem__(self, index):
        return self.buffer[index]

    def send(self, start=0, count=None):
        rows = pl.ds(start, self.shape[0] if count is None else count)
        copy = pltpu.make_async_copy(self.buffer.at[rows], self.target.at[rows], self.semaphores.at[len(self.copies)])
        copy.start()
        self.copies.append(copy)


def call(kernel, out_shape, work, args, scalars=0, sent=(), scratch=()):
    outs = list(out_shape)
    buffers = [pltpu.VMEM(outs[k].shape, outs[k].dtype) for k in sent]
    buffers += [pltpu.SemaphoreType.DMA((PIECES,)) for _ in sent]

    def run(*refs):
        ins, results, rest = refs[: len(args)], list(refs[len(args) : len(args) + len(outs)]), refs[len(args) + len(outs) :]
        for k, place in enumerate(sent):
            results[place] = Sent(results[place], rest[k], rest[len(sent) + k])
        kernel(*ins, *results, *rest[len(buffers) :])
        for place in sent:
            for copy in results[place].copies:
                copy.wait()

    spaces = [pltpu.SMEM] * scalars + [pltpu.VMEM] * (len(args) - scalars)
    return pl.pallas_call(
        run,
        out_shape=outs,
        in_specs=[pl.BlockSpec(memory_space=space) for space in spaces],
        out_specs=[pl.BlockSpec(memory_space=pl.ANY if k in sent else pltpu.VMEM) for k in range(len(outs))],
        scratch_shapes=buffers + list(scratch),
        cost_estimate=pl.CostEstimate(flops=int(work * 1e9), bytes_accessed=int(work * 1e6), transcendentals=0),
        compiler_params=pltpu.CompilerParams(vmem_limit_bytes=VMEM_LIMIT),
    )(*args)


def shape(dims, kind):
    return jax.ShapeDtypeStruct(tuple(dims), kind)


def pick_rim_kernel(order_ref, grid_ref, *out_refs):
    rim = out_refs[0].shape[1]
    keep = order_ref.shape[1] - 4 * rim
    table = table_by_row(order_ref[:, keep:], grid_ref.shape[1])
    picked = mm(grid_ref[...], table).astype(BF16)
    for k in range(4):
        out_refs[k][...] = picked[:, k * rim : (k + 1) * rim]


def keep_kernel(
    order_ref, src_ref, dst_ref, grid_ref, mesh_ref, embed_ref, send_ref, recv_ref,
    rows_ref, sender_ref, node_ref, column_ref, row_ref, dst_s,
):
    keep = rows_ref.shape[1]
    rows = order_ref.shape[1]
    for start in range(0, rows, LANES):
        piece = jnp.broadcast_to(dst_ref[:, start : start + LANES], (LANES, LANES))
        dst_s[start : start + LANES, :] = jnp.transpose(piece).astype(F32).astype(BF16)
    first = src_ref[:, 0:rows]

    for start in range(0, rows, ROW_TILE):
        ids = lax.broadcasted_iota(jnp.int32, (ROW_TILE, rows), 0) + start
        table = jnp.where(ids == first, 1.0, 0.0).astype(BF16)
        column = mm(table, dst_s[...])
        column_ref[start : start + ROW_TILE, :] = column.astype(BF16)
        for k in range(0, ROW_TILE, LANES):
            turned = jnp.transpose(column[k : k + LANES, :])
            row_ref[:, start + k : start + k + LANES] = turned[0:1, :].astype(jnp.int32)
    for start in range(0, keep, ROW_TILE):
        stop = start + ROW_TILE
        table = table_by_row(order_ref[:, start:stop], grid_ref.shape[1])
        cols = mm(grid_ref[...], table).astype(BF16)
        rows_ref[:, start:stop] = cols
        embedded = silu_both(mm_left(cols, embed_ref[...]))[0].astype(BF16)
        sender_ref[start:stop, :] = mm(embedded, send_ref[...]).astype(BF16)
    node_ref[...] = mm(mesh_ref[...], recv_ref[...]).astype(BF16)


def encode_kernel(
    flag_ref, src_ref, dst_ref, row_ref, halo_ref, in0, in1, in2, in3, own0, own1, embed_ref, send_ref,
    sender_ref, node_ref, column_ref, out_w_ref, mesh_ref,
    rim_ref, slope0, slope1, gathered_ref, latent_ref, h00, h01, h10, h11,
    table, total,
):
    keep = sender_ref.shape[0]
    rim = in0.shape[1]
    rows = keep + 4 * rim
    nodes = node_ref.shape[0]
    rim_ref[:, 0:rim] = jnp.where(flag_ref[0] > 0, in0[...], own0[...])
    rim_ref[:, rim : 2 * rim] = jnp.where(flag_ref[1] > 0, in1[...], own1[...])
    rim_ref[:, 2 * rim : 3 * rim] = in2[...]
    rim_ref[:, 3 * rim : 4 * rim] = in3[...]
    embedded = silu_both(mm_left(rim_ref[...], embed_ref[...]))[0].astype(BF16)
    table[keep:rows, :] = mm(embedded, send_ref[...]).astype(BF16)
    table[0:keep, :] = sender_ref[...]
    table[rows : rows + nodes, :] = node_ref[...]
    for start in range(0, src_ref.shape[1], EDGE_TILE):
        stop = start + EDGE_TILE
        if start < rows:
            node = mm(table_by_wide(column_ref[start:stop, :], nodes), node_ref[...])
            value = table[start:stop, :].astype(F32) + node
            by_row = table_by_row(row_ref[:, start:stop], nodes)
        else:
            src = src_ref[:, start:stop]
            dst = dst_ref[:, start:stop]
            both = jnp.concatenate([table_by_column(src, rows), table_by_column(dst, nodes)], axis=1)
            value = mm(both, table[...])
            by_row = table_by_row(dst, nodes)
        act, slope = silu_both(value)
        ref, base = (slope0, 0) if start < rows else (slope1, rows)
        ref[start - base : stop - base, :] = slope.astype(BF16)
        part = mm(by_row, act.astype(BF16))
        total[...] = part if start == 0 else total[...] + part
    gathered = total[...].astype(BF16)
    gathered_ref[...] = gathered
    latent = (mesh_ref[...].astype(F32) + mm(gathered, out_w_ref[...])).astype(BF16)
    latent_ref[...] = latent
    lower = latent[:, latent.shape[1] // 2 :]
    for a, b, ref in ((0, 0, h00), (0, 1, h01), (1, 0, h10), (1, 1, h11)):
        pick = table_by_row(halo_ref[0, a, b : b + 1, :], nodes)
        ref[...] = mm_left(pick, lower).astype(BF16)


def mesh_kernel(
    flag_ref, src_ref, dst_ref, latent_ref, cot_ref, b0, b1, b2, b3, u_src_ref, u_dst_ref, u_out_ref, v_in_ref, v_out_ref,
    g0, g1, g2, g3, coupled_grad_ref, lower_grad_ref, halo_table_ref, ends_ref, summed_ref, coupled_ref, hidden_ref, hidden_grad_ref,
    table, slope_s, total, ends,
):
    nodes = latent_ref.shape[0]
    half = latent_ref.shape[1] // 2
    width = b0.shape[0]
    rows = nodes + 4 * width
    upper = latent_ref[:, :half]
    lower = latent_ref[:, half:]
    halo_table_ref[0:nodes, :] = lower
    for k, ref in enumerate((b0, b1, b2, b3)):
        value = ref[...] if k > 1 else jnp.where(flag_ref[k] > 0, ref[...], jnp.zeros_like(ref[...]))
        halo_table_ref[nodes + k * width : nodes + (k + 1) * width, :] = value
    table[0:rows, :] = mm(halo_table_ref[...], u_src_ref[...]).astype(BF16)
    table[rows : rows + nodes, :] = mm(lower, u_dst_ref[...]).astype(BF16)
    for start in range(0, src_ref.shape[1], EDGE_TILE):
        stop = start + EDGE_TILE
        src = src_ref[:, start:stop]
        dst = dst_ref[:, start:stop]
        both = jnp.concatenate([table_by_column(src, rows), table_by_column(dst, nodes)], axis=1)
        act, slope = silu_both(mm(both, table[...]))
        slope_s[start:stop, :] = slope.astype(BF16)
        part = mm(table_by_row(dst, nodes), act.astype(BF16))
        total[...] = part if start == 0 else total[...] + part
    summed = total[...].astype(BF16)
    summed_ref[...] = summed
    coupled = (upper.astype(F32) + mm(summed, u_out_ref[...])).astype(BF16)
    coupled_ref[...] = coupled
    act, slope = silu_both(mm(coupled, v_in_ref[...]))
    hidden_ref[...] = act.astype(BF16)
    upper_cot = cot_ref[:, :half]
    lower_cot = cot_ref[:, half:]
    hidden_grad = (mm_right(lower_cot, v_out_ref[...]) * slope).astype(BF16)
    hidden_grad_ref[...] = hidden_grad
    coupled_grad = (upper_cot.astype(F32) + mm_right(hidden_grad, v_in_ref[...])).astype(BF16)
    coupled_grad_ref[...] = coupled_grad
    summed_grad = mm_right(coupled_grad, u_out_ref[...]).astype(BF16)

    for start in range(0, src_ref.shape[1], EDGE_TILE):
        stop = start + EDGE_TILE
        src = src_ref[:, start:stop]
        dst = dst_ref[:, start:stop]
        grad = mm(table_by_column(dst, nodes), summed_grad) * slope_s[start:stop, :].astype(F32)
        both = jnp.concatenate([table_by_row(src, rows), table_by_row(dst, nodes)], axis=0)
        part = mm(both, grad.astype(BF16))
        ends[...] = part if start == 0 else ends[...] + part
    ends_ref[...] = ends[...].astype(BF16)
    source_grad = ends_ref[0:rows, :]
    target_grad = ends_ref[rows : rows + nodes, :]
    table_grad = mm_right(source_grad, u_src_ref[...])
    lower_grad_ref[...] = lower_cot.astype(F32) + mm_right(target_grad, u_dst_ref[...]) + table_grad[0:nodes, :]
    for k, ref in enumerate((g0, g1, g2, g3)):
        ref[...] = table_grad[nodes + k * width : nodes + (k + 1) * width, :].astype(BF16)


def store_halves(core_ref, mine_ref, other_ref, start, value):
    half = mine_ref.shape[0]
    value = value.astype(BF16)
    done = 0
    while done < value.shape[0]:
        row = start + done
        count = min(value.shape[0] - done, half - row % half)
        piece = value[done : done + count, :]
        here = row % half

        @pl.when(core_ref[0] == row // half)
        def _(piece=piece, here=here, count=count):
            mine_ref[here : here + count, :] = piece

        @pl.when(core_ref[0] != row // half)
        def _(piece=piece, here=here, count=count):
            other_ref[here : here + count, :] = piece

        done += count


def side_by_side(value):
    rows = value.shape[0] // 2
    return jnp.concatenate([value[:rows, :], value[rows:, :]], axis=1)


def mesh_weight_kernel(
    core_ref, halo_table_ref, ends_ref, summed_ref, coupled_ref, hidden_ref, hidden_grad_ref, coupled_grad_ref, cot_ref,
    mine_ref, other_ref,
):
    rows = halo_table_ref.shape[0]
    nodes, half = coupled_ref.shape
    parts = (
        mm_left(halo_table_ref[...], ends_ref[0:rows, :]),
        mm_left(halo_table_ref[0:nodes, :], ends_ref[rows : rows + nodes, :]),
        side_by_side(mm_left(summed_ref[...], coupled_grad_ref[...])),
        mm_left(coupled_ref[...], hidden_grad_ref[...]),
        side_by_side(mm_left(hidden_ref[...], cot_ref[:, half:])),
    )
    start = 0
    for part in parts:
        store_halves(core_ref, mine_ref, other_ref, start, part)
        start += part.shape[0]


def encoder_back_kernel(
    core_ref, flag_ref, src_ref, dst_ref, row_ref, halo_ref, r0, r1, r2, r3, lower_grad_ref, coupled_grad_ref, out_w_ref,
    column_ref, slope0, slope1, gathered_ref, recv_ref, mesh_ref, rim_rows_ref, embed_ref, send_ref, keep_rows_ref,
    keep_grad_ref, g0, g1, g2, g3, mesh_grad_ref, mine_ref, other_ref,
    edge_s, latent_s, nodes_s,
):
    nodes, dim = mesh_ref.shape
    keep = keep_rows_ref.shape[1]
    rim = g0.shape[1]
    lower_grad = lower_grad_ref[...]
    for a, b, ref in ((0, 0, r0), (0, 1, r1), (1, 0, r2), (1, 1, r3)):
        value = ref[...] if a else jnp.where(flag_ref[b] > 0, ref[...], jnp.zeros_like(ref[...]))
        lower_grad += mm(table_by_row(halo_ref[0, a, b : b + 1, :], nodes), value)
    half = lower_grad.shape[1]
    latent_s[:, :half] = coupled_grad_ref[...]
    latent_s[:, half:] = lower_grad.astype(BF16)
    latent_grad = latent_s[...]
    gathered_grad = mm_right(latent_grad, out_w_ref[...]).astype(BF16)
    rows = column_ref.shape[0]
    for start in range(0, src_ref.shape[1], EDGE_TILE):
        stop = start + EDGE_TILE
        if start < rows:
            by_column = table_by_wide(column_ref[start:stop, :], nodes)
            by_row = table_by_row(row_ref[:, start:stop], nodes)
            slope = slope0[start:stop, :]
        else:
            dst = dst_ref[:, start:stop]
            by_column = table_by_column(dst, nodes)
            by_row = table_by_row(dst, nodes)
            slope = slope1[start - rows : stop - rows, :]
        grad = (mm(by_column, gathered_grad) * slope.astype(F32)).astype(BF16)
        edge_s[start:stop, :] = grad
        part = mm(by_row, grad)
        nodes_s[...] = part if start == 0 else nodes_s[...] + part
    store_halves(core_ref, mine_ref, other_ref, 0, mm_left(gathered_ref[...], latent_grad))
    node_grad = nodes_s[...].astype(BF16)
    store_halves(core_ref, mine_ref, other_ref, dim, mm_left(mesh_ref[...], node_grad))
    mesh_grad_ref[...] = latent_grad.astype(F32) + mm_right(node_grad, recv_ref[...])
    mesh_grad_ref.send()
    extra = src_ref[:, rows:]

    def back(cols, start, count):
        ids = lax.broadcasted_iota(jnp.int32, (count, extra.shape[1]), 0) + start
        table = jnp.where(ids == extra, 1.0, 0.0).astype(BF16)
        own = edge_s[start : start + count, :].astype(F32)
        sender_grad = (own + mm(table, edge_s[rows:, :])).astype(BF16)
        act, slope = silu_both(mm_left(cols, embed_ref[...]))
        embedded_grad = mm_right(sender_grad, send_ref[...]).astype(BF16)
        embed_grad = (embedded_grad.astype(F32) * slope).astype(BF16)
        cols_grad = mm_right(embed_ref[...], embed_grad).astype(BF16)
        return cols_grad, mm_left(act.astype(BF16), sender_grad), mm(cols, embed_grad)

    rim_grad, grad_send, grad_embed = back(rim_rows_ref[...], keep, 4 * rim)
    for k, ref in enumerate((g0, g1, g2, g3)):
        ref[...] = rim_grad[:, k * rim : (k + 1) * rim]
    for start in range(0, keep, ROW_TILE):
        stop = start + ROW_TILE
        cols_grad, send_part, embed_part = back(keep_rows_ref[:, start:stop], start, ROW_TILE)
        keep_grad_ref[:, start:stop] = cols_grad
        grad_send += send_part
        grad_embed += embed_part
    store_halves(core_ref, mine_ref, other_ref, 2 * dim, grad_send)
    pad = jnp.zeros((half - grad_embed.shape[0], dim), F32)
    store_halves(core_ref, mine_ref, other_ref, 3 * dim, jnp.concatenate([grad_embed, pad], axis=0))


def place_kernel(flag_ref, order_ref, keep_ref, in0, in1, in2, in3, own0, own1, grid_grad_ref, all_s):
    keep = keep_ref.shape[1]
    rim = in0.shape[1]
    all_s[:, 0:keep] = keep_ref[...]
    all_s[:, keep : keep + rim] = jnp.where(flag_ref[0] > 0, in0[...], own0[...])
    all_s[:, keep + rim : keep + 2 * rim] = jnp.where(flag_ref[1] > 0, in1[...], own1[...])
    all_s[:, keep + 2 * rim : keep + 3 * rim] = in2[...]
    all_s[:, keep + 3 * rim : keep + 4 * rim] = in3[...]

    for start in range(0, grid_grad_ref.shape[1], ROW_TILE):
        ids = lax.broadcasted_iota(jnp.int32, (ROW_TILE, order_ref.shape[1]), 0) + start
        table = jnp.where(ids == order_ref[...], 1.0, 0.0).astype(BF16)
        grid_grad_ref[:, start : start + ROW_TILE] = mm_right(all_s[...], table).astype(BF16)


def unpack_kernel(a_rows, core_ref, mine_ref, other_ref, embed_ref, send_ref, recv_ref, out_ref, u_src_ref, u_dst_ref, u_out_ref, v_in_ref, v_out_ref):
    first = core_ref[0] == 0

    def read(base, half, start, count):
        pieces = []
        while count > 0:
            here = start % half
            some = min(count, half - here)
            mine = mine_ref[base + here : base + here + some, :]
            other = other_ref[base + here : base + here + some, :]
            pieces.append(jnp.where(first == (start < half), mine, other))
            start += some
            count -= some
        value = pieces[0] if len(pieces) == 1 else jnp.concatenate(pieces, axis=0)
        return value.astype(F32)

    dim, half = v_out_ref.shape
    a_half = a_rows // 2
    b_half = mine_ref.shape[0] - a_half
    for start, ref in ((0, u_src_ref), (half, u_dst_ref), (3 * half, v_in_ref)):
        ref[...] = read(0, a_half, start, half)
        ref.send()
    for start, ref in ((2 * half, u_out_ref), (4 * half, v_out_ref)):
        value = read(0, a_half, start, half)
        ref[0:half, :] = value[:, :half]
        ref[half:, :] = value[:, half:]
        ref.send()
    for start, ref in ((0, out_ref), (dim, recv_ref), (2 * dim, send_ref)):
        ref[...] = read(a_half, b_half, start, dim)
        ref.send()
    ref = embed_ref
    ref[...] = read(a_half, b_half, 3 * dim, half)[0 : ref.shape[0], :]
    ref.send()


def trade(below, above, west, east):
    bands = lax.axis_size(BAND)
    patches = lax.axis_size(PATCH)
    up = [(i, (i + 1) % bands) for i in range(bands)]
    down = [((i + 1) % bands, i) for i in range(bands)]
    right = [(i, (i + 1) % patches) for i in range(patches)]
    left = [((i + 1) % patches, i) for i in range(patches)]
    return (
        lax.ppermute(above, BAND, up),
        lax.ppermute(below, BAND, down),
        lax.ppermute(east, PATCH, right),
        lax.ppermute(west, PATCH, left),
    )


def swap_cores(value):
    return lax.ppermute(value, "core", [(0, 1), (1, 0)])


def body(
    grid_feats, mesh_feats, cotangent, w_embed, w_send, w_recv, w_out, u_src, u_dst, u_out, v_in, v_out,
    send_rows, enc_src, enc_dst, halo_send, mesh_src, mesh_dst,
):
    chans = grid_feats.shape[1]
    grid_rows = grid_feats.shape[0]
    nodes, dim = mesh_feats.shape
    half = dim // 2
    rim = grid_rows // 16
    keep = grid_rows - 4 * rim
    edges = enc_src.shape[1]
    width = halo_send.shape[3]
    table_rows = nodes + 4 * width
    band = lax.axis_index(BAND)
    flags = jnp.stack([band, lax.axis_size(BAND) - 1 - band]).astype(jnp.int32)
    core = lax.axis_index("core").astype(jnp.int32).reshape(1)

    grid_cols = grid_feats.T
    own = call(pick_rim_kernel, [shape((chans, rim), BF16)] * 4, 1, (send_rows, grid_cols))
    arrived = trade(*own)
    outs = [
        shape((chans, keep), BF16), shape((keep, dim), BF16), shape((nodes, dim), BF16),
        shape((grid_rows, LANES), BF16), shape((1, grid_rows), jnp.int32),
    ]
    ins = (send_rows, enc_src, enc_dst, grid_cols, mesh_feats, w_embed, w_send, w_recv)
    keep_rows, keep_sender, node_part, column, row = call(
        keep_kernel, outs, 6, ins, scratch=[pltpu.VMEM((grid_rows, LANES), BF16)]
    )

    outs = [
        shape((chans, 4 * rim), BF16), shape((grid_rows, dim), BF16), shape((edges - grid_rows, dim), BF16),
        shape((nodes, dim), BF16), shape((nodes, dim), BF16),
    ] + [shape((width, half), BF16)] * 4
    ins = (
        flags, enc_src, enc_dst, row, halo_send, *arrived, own[0], own[1], w_embed, w_send,
        keep_sender, node_part, column, w_out, mesh_feats,
    )
    rim_rows, slope0, slope1, gathered, latent, h00, h01, h10, h11 = call(
        encode_kernel, outs, 12, ins, scalars=1,
        scratch=[pltpu.VMEM((grid_rows + nodes, dim), BF16), pltpu.VMEM((nodes, dim), F32)],
    )

    halos = trade(h00, h01, h10, h11)
    outs = [shape((width, half), BF16)] * 4 + [
        shape((nodes, half), BF16), shape((nodes, half), F32), shape((table_rows, half), BF16),
        shape((table_rows + nodes, dim), BF16), shape((nodes, dim), BF16), shape((nodes, half), BF16),
        shape((nodes, dim), BF16), shape((nodes, dim), BF16),
    ]
    ins = (flags, mesh_src, mesh_dst, latent, cotangent, *halos, u_src, u_dst, u_out, v_in, v_out)
    (g0, g1, g2, g3, coupled_grad, lower_grad, halo_table, ends, summed, coupled, hidden, hidden_grad) = call(
        mesh_kernel, outs, 6, ins, scalars=1,
        scratch=[
            pltpu.VMEM((table_rows + nodes, dim), BF16), pltpu.VMEM((mesh_src.shape[1], dim), BF16),
            pltpu.VMEM((nodes, dim), F32), pltpu.VMEM((table_rows + nodes, dim), F32),
        ],
    )
    returned = trade(g0, g1, g2, g3)
    a_rows = 5 * half
    ins = (core, halo_table, ends, summed, coupled, hidden, hidden_grad, coupled_grad, cotangent)
    a_mine, a_other = call(mesh_weight_kernel, [shape((a_rows // 2, dim), BF16)] * 2, 1, ins, scalars=1)
    a_in = swap_cores(a_other)
    lower_grad, a_mine = lax.optimization_barrier((lower_grad, a_mine))

    b_rows = 3 * dim + half
    outs = [shape((chans, keep), BF16)] + [shape((chans, rim), BF16)] * 4 + [shape((nodes, dim), F32)]
    outs += [shape((b_rows // 2, dim), BF16)] * 2
    ins = (
        core, flags, enc_src, enc_dst, row, halo_send, *returned, lower_grad, coupled_grad, w_out,
        column, slope0, slope1, gathered, w_recv, mesh_feats, rim_rows, w_embed, w_send, keep_rows,
    )
    keep_grad, q0, q1, q2, q3, mesh_grad, b_mine, b_other = call(
        encoder_back_kernel, outs, 14, ins, scalars=2, sent=(5,),
        scratch=[pltpu.VMEM((edges, dim), BF16), pltpu.VMEM((nodes, dim), BF16), pltpu.VMEM((nodes, dim), F32)],
    )
    b_in = swap_cores(b_other)
    back = trade(q0, q1, q2, q3)
    patches = lax.axis_size(PATCH)
    packed = (a_rows + b_rows) // 2
    pair = jnp.concatenate([a_mine.astype(F32) + a_in.astype(F32), b_mine.astype(F32) + b_in.astype(F32)], axis=0)
    pair = pair.astype(BF16).reshape(patches, packed // patches, dim)
    pair, *back = lax.optimization_barrier((pair, *back))
    parts = lax.all_to_all(pair, PATCH, 0, 0)
    part = jnp.sum(parts.astype(F32), axis=0).astype(BF16)
    away = [part] + [lax.ppermute(part, "z", [(i, (i + k) % 4) for i in range(4)]) for k in (1, 2, 3)]
    away = [piece.astype(F32) for piece in away]
    total = ((away[0] + away[2]) + (away[1] + away[3])).astype(BF16)
    mine = lax.all_to_all(jnp.broadcast_to(total[None], parts.shape), PATCH, 0, 0).reshape(packed, dim)
    other = swap_cores(mine)
    ins = (flags, send_rows, keep_grad, *back, q0, q1)
    (grid_grad,) = call(
        place_kernel, [shape((chans, grid_rows), BF16)], 5, ins, scalars=1, scratch=[pltpu.VMEM((chans, grid_rows), BF16)]
    )
    outs = [shape((chans, dim), F32)] + [shape((dim, dim), F32)] * 3 + [shape((half, dim), F32)] * 2
    outs += [shape((dim, half), F32), shape((half, dim), F32), shape((dim, half), F32)]
    totals = call(functools.partial(unpack_kernel, a_rows), outs, 4, (core, mine, other), scalars=1, sent=tuple(range(9)))
    return (grid_grad.T, mesh_grad, *totals)


def solution(mesh):
    chips = Mesh(mesh.devices.reshape(mesh.shape["band"] // 2, 2, 4, mesh.shape["patch"] // 4), ("z", "core", "y", "x"))
    everywhere = BAND + PATCH
    rows = P(everywhere, None)
    in_specs = (rows,) * 3 + (P(),) * 9 + (rows,) * 3 + (P(everywhere, None, None, None),) + (rows,) * 2
    out_specs = (rows,) * 2 + (P(),) * 9
    return jax.shard_map(body, mesh=chips, in_specs=in_specs, out_specs=out_specs, check_vma=False)
```

```python
import functools

import jax
import jax.numpy as jnp
from jax import lax
from jax.experimental import pallas as pl
from jax.experimental.pallas import tpu as pltpu
from jax.sharding import Mesh
from jax.sharding import PartitionSpec as P

BF16 = jnp.bfloat16
F32 = jnp.float32
LANES = 128
EDGE_TILE = 1024
ROW_TILE = 512
VMEM_LIMIT = 32 * 1024 * 1024
PIECES = 4
BAND = ("z", "core")
PATCH = ("y", "x")


def mm(left, right):
    return lax.dot_general(left, right, (((1,), (0,)), ((), ())), preferred_element_type=F32)


def mm_left(left, right):
    return lax.dot_general(left, right, (((0,), (0,)), ((), ())), preferred_element_type=F32)


def mm_right(left, right):
    return lax.dot_general(left, right, (((1,), (1,)), ((), ())), preferred_element_type=F32)


def table_by_row(index, count):
    n = index.shape[1]
    rows = lax.broadcasted_iota(jnp.int32, (count, n), 0)
    return jnp.where(rows == index, 1.0, 0.0).astype(BF16)


def table_by_column(index, count):
    n = index.shape[1]
    parts = []
    for start in range(0, n, LANES):
        width = min(LANES, n - start)
        piece = jnp.broadcast_to(index[:, start : start + width], (LANES, width))
        column = jnp.transpose(piece)
        wide = jnp.concatenate([column] * (count // LANES), axis=1)
        columns = lax.broadcasted_iota(jnp.int32, (width, count), 1)
        parts.append(jnp.where(wide == columns, 1.0, 0.0).astype(BF16))
    return parts[0] if len(parts) == 1 else jnp.concatenate(parts, axis=0)


def table_by_wide(column, count):
    wide = jnp.concatenate([column.astype(F32)] * (count // LANES), axis=1)
    columns = lax.broadcasted_iota(jnp.int32, wide.shape, 1).astype(F32)
    return jnp.where(wide == columns, 1.0, 0.0).astype(BF16)


def tiles(stop, size, body):
    def step(i, carry):
        body(pl.multiple_of(i * size, size))
        return carry

    lax.fori_loop(0, stop // size, step, 0)


def silu_both(value):
    sigma = 0.5 * jnp.tanh(0.5 * value) + 0.5
    act = value * sigma
    return act, sigma + act * (1.0 - sigma)


class Sent:
    def __init__(self, target, buffer, semaphores):
        self.target, self.buffer, self.semaphores = target, buffer, semaphores
        self.shape = buffer.shape
        self.copies = []

    def __setitem__(self, index, value):
        self.buffer[index] = value

    def __getitem__(self, index):
        return self.buffer[index]

    def send(self, start=0, count=None):
        rows = pl.ds(start, self.shape[0] if count is None else count)
        copy = pltpu.make_async_copy(self.buffer.at[rows], self.target.at[rows], self.semaphores.at[len(self.copies)])
        copy.start()
        self.copies.append(copy)


def call(kernel, out_shape, work, args, scalars=0, sent=(), scratch=()):
    outs = list(out_shape)
    buffers = [pltpu.VMEM(outs[k].shape, outs[k].dtype) for k in sent]
    buffers += [pltpu.SemaphoreType.DMA((PIECES,)) for _ in sent]

    def run(*refs):
        ins, results, rest = refs[: len(args)], list(refs[len(args) : len(args) + len(outs)]), refs[len(args) + len(outs) :]
        for k, place in enumerate(sent):
            results[place] = Sent(results[place], rest[k], rest[len(sent) + k])
        kernel(*ins, *results, *rest[len(buffers) :])
        for place in sent:
            for copy in results[place].copies:
                copy.wait()

    spaces = [pltpu.SMEM] * scalars + [pltpu.VMEM] * (len(args) - scalars)
    return pl.pallas_call(
        run,
        out_shape=outs,
        in_specs=[pl.BlockSpec(memory_space=space) for space in spaces],
        out_specs=[pl.BlockSpec(memory_space=pl.ANY if k in sent else pltpu.VMEM) for k in range(len(outs))],
        scratch_shapes=buffers + list(scratch),
        cost_estimate=pl.CostEstimate(flops=int(work * 1e9), bytes_accessed=int(work * 1e6), transcendentals=0),
        compiler_params=pltpu.CompilerParams(vmem_limit_bytes=VMEM_LIMIT),
    )(*args)


def shape(dims, kind):
    return jax.ShapeDtypeStruct(tuple(dims), kind)


def pick_rim_kernel(order_ref, grid_ref, *out_refs):
    rim = out_refs[0].shape[1]
    keep = order_ref.shape[1] - 4 * rim
    table = table_by_row(order_ref[:, keep:], grid_ref.shape[1])
    picked = mm(grid_ref[...], table).astype(BF16)
    for k in range(4):
        out_refs[k][...] = picked[:, k * rim : (k + 1) * rim]


def keep_kernel(
    order_ref, src_ref, dst_ref, grid_ref, mesh_ref, embed_ref, send_ref, recv_ref,
    rows_ref, sender_ref, node_ref, column_ref, row_ref, dst_s,
):
    keep = rows_ref.shape[1]
    rows = order_ref.shape[1]
    for start in range(0, rows, LANES):
        piece = jnp.broadcast_to(dst_ref[:, start : start + LANES], (LANES, LANES))
        dst_s[start : start + LANES, :] = jnp.transpose(piece).astype(F32).astype(BF16)
    first = src_ref[:, 0:rows]


    def sort(start):
        ids = lax.broadcasted_iota(jnp.int32, (ROW_TILE, rows), 0) + start
        table = jnp.where(ids == first, 1.0, 0.0).astype(BF16)
        column = mm(table, dst_s[...])
        column_ref[pl.ds(start, ROW_TILE), :] = column.astype(BF16)
        for k in range(0, ROW_TILE, LANES):
            turned = jnp.transpose(column[k : k + LANES, :])
            row_ref[:, pl.ds(pl.multiple_of(start + k, LANES), LANES)] = turned[0:1, :].astype(jnp.int32)

    tiles(rows, ROW_TILE, sort)
    for start in range(0, keep, ROW_TILE):
        stop = start + ROW_TILE
        table = table_by_row(order_ref[:, start:stop], grid_ref.shape[1])
        cols = mm(grid_ref[...], table).astype(BF16)
        rows_ref[:, start:stop] = cols
        embedded = silu_both(mm_left(cols, embed_ref[...]))[0].astype(BF16)
        sender_ref[start:stop, :] = mm(embedded, send_ref[...]).astype(BF16)
    node_ref[...] = mm(mesh_ref[...], recv_ref[...]).astype(BF16)


def encode_kernel(
    flag_ref, src_ref, dst_ref, row_ref, halo_ref, in0, in1, in2, in3, own0, own1, embed_ref, send_ref,
    sender_ref, node_ref, column_ref, out_w_ref, mesh_ref,
    rim_ref, slope0, slope1, gathered_ref, latent_ref, h00, h01, h10, h11,
    table, total,
):
    keep = sender_ref.shape[0]
    rim = in0.shape[1]
    rows = keep + 4 * rim
    nodes = node_ref.shape[0]
    rim_ref[:, 0:rim] = jnp.where(flag_ref[0] > 0, in0[...], own0[...])
    rim_ref[:, rim : 2 * rim] = jnp.where(flag_ref[1] > 0, in1[...], own1[...])
    rim_ref[:, 2 * rim : 3 * rim] = in2[...]
    rim_ref[:, 3 * rim : 4 * rim] = in3[...]
    embedded = silu_both(mm_left(rim_ref[...], embed_ref[...]))[0].astype(BF16)
    table[keep:rows, :] = mm(embedded, send_ref[...]).astype(BF16)
    table[0:keep, :] = sender_ref[...]
    table[rows : rows + nodes, :] = node_ref[...]
    for start in range(0, src_ref.shape[1], EDGE_TILE):
        stop = start + EDGE_TILE
        if start < rows:
            node = mm(table_by_wide(column_ref[start:stop, :], nodes), node_ref[...])
            value = table[start:stop, :].astype(F32) + node
            by_row = table_by_row(row_ref[:, start:stop], nodes)
        else:
            src = src_ref[:, start:stop]
            dst = dst_ref[:, start:stop]
            both = jnp.concatenate([table_by_column(src, rows), table_by_column(dst, nodes)], axis=1)
            value = mm(both, table[...])
            by_row = table_by_row(dst, nodes)
        act, slope = silu_both(value)
        ref, base = (slope0, 0) if start < rows else (slope1, rows)
        ref[start - base : stop - base, :] = slope.astype(BF16)
        part = mm(by_row, act.astype(BF16))
        total[...] = part if start == 0 else total[...] + part
    gathered = total[...].astype(BF16)
    gathered_ref[...] = gathered
    latent = (mesh_ref[...].astype(F32) + mm(gathered, out_w_ref[...])).astype(BF16)
    latent_ref[...] = latent
    lower = latent[:, latent.shape[1] // 2 :]
    for a, b, ref in ((0, 0, h00), (0, 1, h01), (1, 0, h10), (1, 1, h11)):
        pick = table_by_row(halo_ref[0, a, b : b + 1, :], nodes)
        ref[...] = mm_left(pick, lower).astype(BF16)


def mesh_kernel(
    flag_ref, src_ref, dst_ref, latent_ref, cot_ref, b0, b1, b2, b3, u_src_ref, u_dst_ref, u_out_ref, v_in_ref, v_out_ref,
    g0, g1, g2, g3, coupled_grad_ref, lower_grad_ref, halo_table_ref, ends_ref, summed_ref, coupled_ref, hidden_ref, hidden_grad_ref,
    table, slope_s, total, ends,
):
    nodes = latent_ref.shape[0]
    half = latent_ref.shape[1] // 2
    width = b0.shape[0]
    rows = nodes + 4 * width
    upper = latent_ref[:, :half]
    lower = latent_ref[:, half:]
    halo_table_ref[0:nodes, :] = lower
    for k, ref in enumerate((b0, b1, b2, b3)):
        value = ref[...] if k > 1 else jnp.where(flag_ref[k] > 0, ref[...], jnp.zeros_like(ref[...]))
        halo_table_ref[nodes + k * width : nodes + (k + 1) * width, :] = value
    table[0:rows, :] = mm(halo_table_ref[...], u_src_ref[...]).astype(BF16)
    table[rows : rows + nodes, :] = mm(lower, u_dst_ref[...]).astype(BF16)
    for start in range(0, src_ref.shape[1], EDGE_TILE):
        stop = start + EDGE_TILE
        src = src_ref[:, start:stop]
        dst = dst_ref[:, start:stop]
        both = jnp.concatenate([table_by_column(src, rows), table_by_column(dst, nodes)], axis=1)
        act, slope = silu_both(mm(both, table[...]))
        slope_s[start:stop, :] = slope.astype(BF16)
        part = mm(table_by_row(dst, nodes), act.astype(BF16))
        total[...] = part if start == 0 else total[...] + part
    summed = total[...].astype(BF16)
    summed_ref[...] = summed
    coupled = (upper.astype(F32) + mm(summed, u_out_ref[...])).astype(BF16)
    coupled_ref[...] = coupled
    act, slope = silu_both(mm(coupled, v_in_ref[...]))
    hidden_ref[...] = act.astype(BF16)
    upper_cot = cot_ref[:, :half]
    lower_cot = cot_ref[:, half:]
    hidden_grad = (mm_right(lower_cot, v_out_ref[...]) * slope).astype(BF16)
    hidden_grad_ref[...] = hidden_grad
    coupled_grad = (upper_cot.astype(F32) + mm_right(hidden_grad, v_in_ref[...])).astype(BF16)
    coupled_grad_ref[...] = coupled_grad
    summed_grad = mm_right(coupled_grad, u_out_ref[...]).astype(BF16)

    for start in range(0, src_ref.shape[1], EDGE_TILE):
        stop = start + EDGE_TILE
        src = src_ref[:, start:stop]
        dst = dst_ref[:, start:stop]
        grad = mm(table_by_column(dst, nodes), summed_grad) * slope_s[start:stop, :].astype(F32)
        both = jnp.concatenate([table_by_row(src, rows), table_by_row(dst, nodes)], axis=0)
        part = mm(both, grad.astype(BF16))
        ends[...] = part if start == 0 else ends[...] + part
    ends_ref[...] = ends[...].astype(BF16)
    source_grad = ends_ref[0:rows, :]
    target_grad = ends_ref[rows : rows + nodes, :]
    table_grad = mm_right(source_grad, u_src_ref[...])
    lower_grad_ref[...] = lower_cot.astype(F32) + mm_right(target_grad, u_dst_ref[...]) + table_grad[0:nodes, :]
    for k, ref in enumerate((g0, g1, g2, g3)):
        ref[...] = table_grad[nodes + k * width : nodes + (k + 1) * width, :].astype(BF16)


def store_halves(core_ref, mine_ref, other_ref, start, value):
    half = mine_ref.shape[0]
    value = value.astype(BF16)
    done = 0
    while done < value.shape[0]:
        row = start + done
        count = min(value.shape[0] - done, half - row % half)
        piece = value[done : done + count, :]
        here = row % half

        @pl.when(core_ref[0] == row // half)
        def _(piece=piece, here=here, count=count):
            mine_ref[here : here + count, :] = piece

        @pl.when(core_ref[0] != row // half)
        def _(piece=piece, here=here, count=count):
            other_ref[here : here + count, :] = piece

        done += count


def side_by_side(value):
    rows = value.shape[0] // 2
    return jnp.concatenate([value[:rows, :], value[rows:, :]], axis=1)


def mesh_weight_kernel(
    core_ref, halo_table_ref, ends_ref, summed_ref, coupled_ref, hidden_ref, hidden_grad_ref, coupled_grad_ref, cot_ref,
    mine_ref, other_ref,
):
    rows = halo_table_ref.shape[0]
    nodes, half = coupled_ref.shape
    parts = (
        mm_left(halo_table_ref[...], ends_ref[0:rows, :]),
        mm_left(halo_table_ref[0:nodes, :], ends_ref[rows : rows + nodes, :]),
        side_by_side(mm_left(summed_ref[...], coupled_grad_ref[...])),
        mm_left(coupled_ref[...], hidden_grad_ref[...]),
        side_by_side(mm_left(hidden_ref[...], cot_ref[:, half:])),
    )
    start = 0
    for part in parts:
        store_halves(core_ref, mine_ref, other_ref, start, part)
        start += part.shape[0]


def encoder_back_kernel(
    core_ref, flag_ref, src_ref, dst_ref, row_ref, halo_ref, r0, r1, r2, r3, lower_grad_ref, coupled_grad_ref, out_w_ref,
    column_ref, slope0, slope1, gathered_ref, recv_ref, mesh_ref, rim_rows_ref, embed_ref, send_ref, keep_rows_ref,
    keep_grad_ref, g0, g1, g2, g3, mesh_grad_ref, mine_ref, other_ref,
    edge_s, latent_s, nodes_s, sum_send, sum_embed,
):
    nodes, dim = mesh_ref.shape
    keep = keep_rows_ref.shape[1]
    rim = g0.shape[1]
    lower_grad = lower_grad_ref[...]
    for a, b, ref in ((0, 0, r0), (0, 1, r1), (1, 0, r2), (1, 1, r3)):
        value = ref[...] if a else jnp.where(flag_ref[b] > 0, ref[...], jnp.zeros_like(ref[...]))
        lower_grad += mm(table_by_row(halo_ref[0, a, b : b + 1, :], nodes), value)
    half = lower_grad.shape[1]
    latent_s[:, :half] = coupled_grad_ref[...]
    latent_s[:, half:] = lower_grad.astype(BF16)
    latent_grad = latent_s[...]
    gathered_grad = mm_right(latent_grad, out_w_ref[...]).astype(BF16)
    rows = column_ref.shape[0]
    for start in range(0, src_ref.shape[1], EDGE_TILE):
        stop = start + EDGE_TILE
        if start < rows:
            by_column = table_by_wide(column_ref[start:stop, :], nodes)
            by_row = table_by_row(row_ref[:, start:stop], nodes)
            slope = slope0[start:stop, :]
        else:
            dst = dst_ref[:, start:stop]
            by_column = table_by_column(dst, nodes)
            by_row = table_by_row(dst, nodes)
            slope = slope1[start - rows : stop - rows, :]
        grad = (mm(by_column, gathered_grad) * slope.astype(F32)).astype(BF16)
        edge_s[start:stop, :] = grad
        part = mm(by_row, grad)
        nodes_s[...] = part if start == 0 else nodes_s[...] + part
    store_halves(core_ref, mine_ref, other_ref, 0, mm_left(gathered_ref[...], latent_grad))
    node_grad = nodes_s[...].astype(BF16)
    store_halves(core_ref, mine_ref, other_ref, dim, mm_left(mesh_ref[...], node_grad))
    mesh_grad_ref[...] = latent_grad.astype(F32) + mm_right(node_grad, recv_ref[...])
    mesh_grad_ref.send()
    extra = src_ref[:, rows:]

    def back(cols, start, count):
        ids = lax.broadcasted_iota(jnp.int32, (count, extra.shape[1]), 0) + start
        table = jnp.where(ids == extra, 1.0, 0.0).astype(BF16)
        own = edge_s[pl.ds(start, count), :].astype(F32)
        sender_grad = (own + mm(table, edge_s[rows:, :])).astype(BF16)
        act, slope = silu_both(mm_left(cols, embed_ref[...]))
        embedded_grad = mm_right(sender_grad, send_ref[...]).astype(BF16)
        embed_grad = (embedded_grad.astype(F32) * slope).astype(BF16)
        cols_grad = mm_right(embed_ref[...], embed_grad).astype(BF16)
        return cols_grad, mm_left(act.astype(BF16), sender_grad), mm(cols, embed_grad)

    rim_grad, send_part, embed_part = back(rim_rows_ref[...], keep, 4 * rim)
    sum_send[...] = send_part
    sum_embed[...] = embed_part
    for k, ref in enumerate((g0, g1, g2, g3)):
        ref[...] = rim_grad[:, k * rim : (k + 1) * rim]

    def kept(start):
        here = pl.ds(start, ROW_TILE)
        cols_grad, send_part, embed_part = back(keep_rows_ref[:, here], start, ROW_TILE)
        keep_grad_ref[:, here] = cols_grad
        sum_send[...] += send_part
        sum_embed[...] += embed_part

    tiles(keep, ROW_TILE, kept)
    store_halves(core_ref, mine_ref, other_ref, 2 * dim, sum_send[...])
    grad_embed = sum_embed[...]
    pad = jnp.zeros((half - grad_embed.shape[0], dim), F32)
    store_halves(core_ref, mine_ref, other_ref, 3 * dim, jnp.concatenate([grad_embed, pad], axis=0))


def place_kernel(flag_ref, order_ref, keep_ref, in0, in1, in2, in3, own0, own1, grid_grad_ref, all_s):
    keep = keep_ref.shape[1]
    rim = in0.shape[1]
    all_s[:, 0:keep] = keep_ref[...]
    all_s[:, keep : keep + rim] = jnp.where(flag_ref[0] > 0, in0[...], own0[...])
    all_s[:, keep + rim : keep + 2 * rim] = jnp.where(flag_ref[1] > 0, in1[...], own1[...])
    all_s[:, keep + 2 * rim : keep + 3 * rim] = in2[...]
    all_s[:, keep + 3 * rim : keep + 4 * rim] = in3[...]


    def place(start):
        ids = lax.broadcasted_iota(jnp.int32, (ROW_TILE, order_ref.shape[1]), 0) + start
        table = jnp.where(ids == order_ref[...], 1.0, 0.0).astype(BF16)
        grid_grad_ref[:, pl.ds(start, ROW_TILE)] = mm_right(all_s[...], table).astype(BF16)

    tiles(grid_grad_ref.shape[1], ROW_TILE, place)


def unpack_kernel(a_rows, core_ref, mine_ref, other_ref, embed_ref, send_ref, recv_ref, out_ref, u_src_ref, u_dst_ref, u_out_ref, v_in_ref, v_out_ref):
    first = core_ref[0] == 0

    def read(base, half, start, count):
        pieces = []
        while count > 0:
            here = start % half
            some = min(count, half - here)
            mine = mine_ref[base + here : base + here + some, :]
            other = other_ref[base + here : base + here + some, :]
            pieces.append(jnp.where(first == (start < half), mine, other))
            start += some
            count -= some
        value = pieces[0] if len(pieces) == 1 else jnp.concatenate(pieces, axis=0)
        return value.astype(F32)

    dim, half = v_out_ref.shape
    a_half = a_rows // 2
    b_half = mine_ref.shape[0] - a_half
    for start, ref in ((0, u_src_ref), (half, u_dst_ref), (3 * half, v_in_ref)):
        ref[...] = read(0, a_half, start, half)
        ref.send()
    for start, ref in ((2 * half, u_out_ref), (4 * half, v_out_ref)):
        value = read(0, a_half, start, half)
        ref[0:half, :] = value[:, :half]
        ref[half:, :] = value[:, half:]
        ref.send()
    for start, ref in ((0, out_ref), (dim, recv_ref), (2 * dim, send_ref)):
        ref[...] = read(a_half, b_half, start, dim)
        ref.send()
    ref = embed_ref
    ref[...] = read(a_half, b_half, 3 * dim, half)[0 : ref.shape[0], :]
    ref.send()


def trade(below, above, west, east):
    bands = lax.axis_size(BAND)
    patches = lax.axis_size(PATCH)
    up = [(i, (i + 1) % bands) for i in range(bands)]
    down = [((i + 1) % bands, i) for i in range(bands)]
    right = [(i, (i + 1) % patches) for i in range(patches)]
    left = [((i + 1) % patches, i) for i in range(patches)]
    return (
        lax.ppermute(above, BAND, up),
        lax.ppermute(below, BAND, down),
        lax.ppermute(east, PATCH, right),
        lax.ppermute(west, PATCH, left),
    )


def swap_cores(value):
    return lax.ppermute(value, "core", [(0, 1), (1, 0)])


def body(
    grid_feats, mesh_feats, cotangent, w_embed, w_send, w_recv, w_out, u_src, u_dst, u_out, v_in, v_out,
    send_rows, enc_src, enc_dst, halo_send, mesh_src, mesh_dst,
):
    chans = grid_feats.shape[1]
    grid_rows = grid_feats.shape[0]
    nodes, dim = mesh_feats.shape
    half = dim // 2
    rim = grid_rows // 16
    keep = grid_rows - 4 * rim
    edges = enc_src.shape[1]
    width = halo_send.shape[3]
    table_rows = nodes + 4 * width
    band = lax.axis_index(BAND)
    flags = jnp.stack([band, lax.axis_size(BAND) - 1 - band]).astype(jnp.int32)
    core = lax.axis_index("core").astype(jnp.int32).reshape(1)

    grid_cols = grid_feats.T
    own = call(pick_rim_kernel, [shape((chans, rim), BF16)] * 4, 1, (send_rows, grid_cols))
    arrived = trade(*own)
    outs = [
        shape((chans, keep), BF16), shape((keep, dim), BF16), shape((nodes, dim), BF16),
        shape((grid_rows, LANES), BF16), shape((1, grid_rows), jnp.int32),
    ]
    ins = (send_rows, enc_src, enc_dst, grid_cols, mesh_feats, w_embed, w_send, w_recv)
    keep_rows, keep_sender, node_part, column, row = call(
        keep_kernel, outs, 6, ins, scratch=[pltpu.VMEM((grid_rows, LANES), BF16)]
    )

    outs = [
        shape((chans, 4 * rim), BF16), shape((grid_rows, dim), BF16), shape((edges - grid_rows, dim), BF16),
        shape((nodes, dim), BF16), shape((nodes, dim), BF16),
    ] + [shape((width, half), BF16)] * 4
    ins = (
        flags, enc_src, enc_dst, row, halo_send, *arrived, own[0], own[1], w_embed, w_send,
        keep_sender, node_part, column, w_out, mesh_feats,
    )
    rim_rows, slope0, slope1, gathered, latent, h00, h01, h10, h11 = call(
        encode_kernel, outs, 12, ins, scalars=1,
        scratch=[pltpu.VMEM((grid_rows + nodes, dim), BF16), pltpu.VMEM((nodes, dim), F32)],
    )

    halos = trade(h00, h01, h10, h11)
    outs = [shape((width, half), BF16)] * 4 + [
        shape((nodes, half), BF16), shape((nodes, half), F32), shape((table_rows, half), BF16),
        shape((table_rows + nodes, dim), BF16), shape((nodes, dim), BF16), shape((nodes, half), BF16),
        shape((nodes, dim), BF16), shape((nodes, dim), BF16),
    ]
    ins = (flags, mesh_src, mesh_dst, latent, cotangent, *halos, u_src, u_dst, u_out, v_in, v_out)
    (g0, g1, g2, g3, coupled_grad, lower_grad, halo_table, ends, summed, coupled, hidden, hidden_grad) = call(
        mesh_kernel, outs, 6, ins, scalars=1,
        scratch=[
            pltpu.VMEM((table_rows + nodes, dim), BF16), pltpu.VMEM((mesh_src.shape[1], dim), BF16),
            pltpu.VMEM((nodes, dim), F32), pltpu.VMEM((table_rows + nodes, dim), F32),
        ],
    )
    returned = trade(g0, g1, g2, g3)
    a_rows = 5 * half
    ins = (core, halo_table, ends, summed, coupled, hidden, hidden_grad, coupled_grad, cotangent)
    a_mine, a_other = call(mesh_weight_kernel, [shape((a_rows // 2, dim), BF16)] * 2, 1, ins, scalars=1)
    a_in = swap_cores(a_other)
    lower_grad, a_mine = lax.optimization_barrier((lower_grad, a_mine))

    b_rows = 3 * dim + half
    outs = [shape((chans, keep), BF16)] + [shape((chans, rim), BF16)] * 4 + [shape((nodes, dim), F32)]
    outs += [shape((b_rows // 2, dim), BF16)] * 2
    ins = (
        core, flags, enc_src, enc_dst, row, halo_send, *returned, lower_grad, coupled_grad, w_out,
        column, slope0, slope1, gathered, w_recv, mesh_feats, rim_rows, w_embed, w_send, keep_rows,
    )
    keep_grad, q0, q1, q2, q3, mesh_grad, b_mine, b_other = call(
        encoder_back_kernel, outs, 14, ins, scalars=2, sent=(5,),
        scratch=[
            pltpu.VMEM((edges, dim), BF16), pltpu.VMEM((nodes, dim), BF16), pltpu.VMEM((nodes, dim), F32),
            pltpu.VMEM((dim, dim), F32), pltpu.VMEM((chans, dim), F32),
        ],
    )
    b_in = swap_cores(b_other)
    back = trade(q0, q1, q2, q3)
    patches = lax.axis_size(PATCH)
    packed = (a_rows + b_rows) // 2
    pair = jnp.concatenate([a_mine.astype(F32) + a_in.astype(F32), b_mine.astype(F32) + b_in.astype(F32)], axis=0)
    pair = pair.astype(BF16).reshape(patches, packed // patches, dim)
    pair, *back = lax.optimization_barrier((pair, *back))
    parts = lax.all_to_all(pair, PATCH, 0, 0)
    part = jnp.sum(parts.astype(F32), axis=0).astype(BF16)
    away = [part] + [lax.ppermute(part, "z", [(i, (i + k) % 4) for i in range(4)]) for k in (1, 2, 3)]
    away = [piece.astype(F32) for piece in away]
    total = ((away[0] + away[2]) + (away[1] + away[3])).astype(BF16)
    mine = lax.all_to_all(jnp.broadcast_to(total[None], parts.shape), PATCH, 0, 0).reshape(packed, dim)
    other = swap_cores(mine)
    ins = (flags, send_rows, keep_grad, *back, q0, q1)
    (grid_grad,) = call(
        place_kernel, [shape((chans, grid_rows), BF16)], 5, ins, scalars=1, scratch=[pltpu.VMEM((chans, grid_rows), BF16)]
    )
    outs = [shape((chans, dim), F32)] + [shape((dim, dim), F32)] * 3 + [shape((half, dim), F32)] * 2
    outs += [shape((dim, half), F32), shape((half, dim), F32), shape((dim, half), F32)]
    totals = call(functools.partial(unpack_kernel, a_rows), outs, 4, (core, mine, other), scalars=1, sent=tuple(range(9)))
    return (grid_grad.T, mesh_grad, *totals)


def solution(mesh):
    chips = Mesh(mesh.devices.reshape(mesh.shape["band"] // 2, 2, 4, mesh.shape["patch"] // 4), ("z", "core", "y", "x"))
    everywhere = BAND + PATCH
    rows = P(everywhere, None)
    in_specs = (rows,) * 3 + (P(),) * 9 + (rows,) * 3 + (P(everywhere, None, None, None),) + (rows,) * 2
    out_specs = (rows,) * 2 + (P(),) * 9
    return jax.shard_map(body, mesh=chips, in_specs=in_specs, out_specs=out_specs, check_vma=False)
```

```python
import functools

import jax
import jax.numpy as jnp
from jax import lax
from jax.experimental import pallas as pl
from jax.experimental.pallas import tpu as pltpu
from jax.sharding import Mesh
from jax.sharding import PartitionSpec as P

BF16 = jnp.bfloat16
F32 = jnp.float32
LANES = 128
EDGE_TILE = 1024
ROW_TILE = 512
BACK_TILE = 1024
VMEM_LIMIT = 32 * 1024 * 1024
PIECES = 4
BAND = ("z", "core")
PATCH = ("y", "x")


def mm(left, right):
    return lax.dot_general(left, right, (((1,), (0,)), ((), ())), preferred_element_type=F32)


def mm_left(left, right):
    return lax.dot_general(left, right, (((0,), (0,)), ((), ())), preferred_element_type=F32)


def mm_right(left, right):
    return lax.dot_general(left, right, (((1,), (1,)), ((), ())), preferred_element_type=F32)


def table_by_row(index, count):
    n = index.shape[1]
    rows = lax.broadcasted_iota(jnp.int32, (count, n), 0)
    return jnp.where(rows == index, 1.0, 0.0).astype(BF16)


def table_by_column(index, count):
    n = index.shape[1]
    parts = []
    for start in range(0, n, LANES):
        width = min(LANES, n - start)
        piece = jnp.broadcast_to(index[:, start : start + width], (LANES, width))
        column = jnp.transpose(piece)
        wide = jnp.concatenate([column] * (count // LANES), axis=1)
        columns = lax.broadcasted_iota(jnp.int32, (width, count), 1)
        parts.append(jnp.where(wide == columns, 1.0, 0.0).astype(BF16))
    return parts[0] if len(parts) == 1 else jnp.concatenate(parts, axis=0)


def table_by_wide(column, count):
    wide = jnp.concatenate([column.astype(F32)] * (count // LANES), axis=1)
    columns = lax.broadcasted_iota(jnp.int32, wide.shape, 1).astype(F32)
    return jnp.where(wide == columns, 1.0, 0.0).astype(BF16)


def tiles(stop, size, body):
    def step(i, carry):
        body(pl.multiple_of(i * size, size))
        return carry

    lax.fori_loop(0, stop // size, step, 0)


def silu_both(value):
    sigma = 0.5 * jnp.tanh(0.5 * value) + 0.5
    act = value * sigma
    return act, sigma + act * (1.0 - sigma)


class Sent:
    def __init__(self, target, buffer, semaphores):
        self.target, self.buffer, self.semaphores = target, buffer, semaphores
        self.shape = buffer.shape
        self.copies = []

    def __setitem__(self, index, value):
        self.buffer[index] = value

    def __getitem__(self, index):
        return self.buffer[index]

    def send(self, start=0, count=None):
        rows = pl.ds(start, self.shape[0] if count is None else count)
        copy = pltpu.make_async_copy(self.buffer.at[rows], self.target.at[rows], self.semaphores.at[len(self.copies)])
        copy.start()
        self.copies.append(copy)


def call(kernel, out_shape, work, args, scalars=0, sent=(), scratch=()):
    outs = list(out_shape)
    buffers = [pltpu.VMEM(outs[k].shape, outs[k].dtype) for k in sent]
    buffers += [pltpu.SemaphoreType.DMA((PIECES,)) for _ in sent]

    def run(*refs):
        ins, results, rest = refs[: len(args)], list(refs[len(args) : len(args) + len(outs)]), refs[len(args) + len(outs) :]
        for k, place in enumerate(sent):
            results[place] = Sent(results[place], rest[k], rest[len(sent) + k])
        kernel(*ins, *results, *rest[len(buffers) :])
        for place in sent:
            for copy in results[place].copies:
                copy.wait()

    spaces = [pltpu.SMEM] * scalars + [pltpu.VMEM] * (len(args) - scalars)
    return pl.pallas_call(
        run,
        out_shape=outs,
        in_specs=[pl.BlockSpec(memory_space=space) for space in spaces],
        out_specs=[pl.BlockSpec(memory_space=pl.ANY if k in sent else pltpu.VMEM) for k in range(len(outs))],
        scratch_shapes=buffers + list(scratch),
        cost_estimate=pl.CostEstimate(flops=int(work * 1e9), bytes_accessed=int(work * 1e6), transcendentals=0),
        compiler_params=pltpu.CompilerParams(vmem_limit_bytes=VMEM_LIMIT),
    )(*args)


def shape(dims, kind):
    return jax.ShapeDtypeStruct(tuple(dims), kind)


def pick_rim_kernel(order_ref, grid_ref, *out_refs):
    rim = out_refs[0].shape[1]
    keep = order_ref.shape[1] - 4 * rim
    table = table_by_row(order_ref[:, keep:], grid_ref.shape[1])
    picked = mm(grid_ref[...], table).astype(BF16)
    for k in range(4):
        out_refs[k][...] = picked[:, k * rim : (k + 1) * rim]


def keep_kernel(
    order_ref, src_ref, dst_ref, grid_ref, mesh_ref, embed_ref, send_ref, recv_ref,
    rows_ref, sender_ref, node_ref, column_ref, row_ref, dst_s,
):
    keep = rows_ref.shape[1]
    rows = order_ref.shape[1]
    for start in range(0, rows, LANES):
        piece = jnp.broadcast_to(dst_ref[:, start : start + LANES], (LANES, LANES))
        dst_s[start : start + LANES, :] = jnp.transpose(piece).astype(F32).astype(BF16)
    first = src_ref[:, 0:rows]


    def sort(start):
        ids = lax.broadcasted_iota(jnp.int32, (ROW_TILE, rows), 0) + start
        table = jnp.where(ids == first, 1.0, 0.0).astype(BF16)
        column = mm(table, dst_s[...])
        column_ref[pl.ds(start, ROW_TILE), :] = column.astype(BF16)
        for k in range(0, ROW_TILE, LANES):
            turned = jnp.transpose(column[k : k + LANES, :])
            row_ref[:, pl.ds(pl.multiple_of(start + k, LANES), LANES)] = turned[0:1, :].astype(jnp.int32)

    tiles(rows, ROW_TILE, sort)
    for start in range(0, keep, ROW_TILE):
        stop = start + ROW_TILE
        table = table_by_row(order_ref[:, start:stop], grid_ref.shape[1])
        cols = mm(grid_ref[...], table).astype(BF16)
        rows_ref[:, start:stop] = cols
        embedded = silu_both(mm_left(cols, embed_ref[...]))[0].astype(BF16)
        sender_ref[start:stop, :] = mm(embedded, send_ref[...]).astype(BF16)
    node_ref[...] = mm(mesh_ref[...], recv_ref[...]).astype(BF16)


def encode_kernel(
    flag_ref, src_ref, dst_ref, row_ref, halo_ref, in0, in1, in2, in3, own0, own1, embed_ref, send_ref,
    keep_rows_ref, sender_ref, node_ref, column_ref, out_w_ref, mesh_ref,
    rows_ref, slope0, slope1, gathered_ref, latent_ref, h00, h01, h10, h11,
    table, total,
):
    keep = sender_ref.shape[0]
    rim = in0.shape[1]
    rows = keep + 4 * rim
    nodes = node_ref.shape[0]
    rows_ref[:, 0:keep] = keep_rows_ref[...]
    rows_ref[:, keep : keep + rim] = jnp.where(flag_ref[0] > 0, in0[...], own0[...])
    rows_ref[:, keep + rim : keep + 2 * rim] = jnp.where(flag_ref[1] > 0, in1[...], own1[...])
    rows_ref[:, keep + 2 * rim : keep + 3 * rim] = in2[...]
    rows_ref[:, keep + 3 * rim : rows] = in3[...]
    embedded = silu_both(mm_left(rows_ref[:, keep:], embed_ref[...]))[0].astype(BF16)
    table[keep:rows, :] = mm(embedded, send_ref[...]).astype(BF16)
    table[0:keep, :] = sender_ref[...]
    table[rows : rows + nodes, :] = node_ref[...]
    for start in range(0, src_ref.shape[1], EDGE_TILE):
        stop = start + EDGE_TILE
        if start < rows:
            node = mm(table_by_wide(column_ref[start:stop, :], nodes), node_ref[...])
            value = table[start:stop, :].astype(F32) + node
            by_row = table_by_row(row_ref[:, start:stop], nodes)
        else:
            src = src_ref[:, start:stop]
            dst = dst_ref[:, start:stop]
            both = jnp.concatenate([table_by_column(src, rows), table_by_column(dst, nodes)], axis=1)
            value = mm(both, table[...])
            by_row = table_by_row(dst, nodes)
        act, slope = silu_both(value)
        ref, base = (slope0, 0) if start < rows else (slope1, rows)
        ref[start - base : stop - base, :] = slope.astype(BF16)
        part = mm(by_row, act.astype(BF16))
        total[...] = part if start == 0 else total[...] + part
    gathered = total[...].astype(BF16)
    gathered_ref[...] = gathered
    latent = (mesh_ref[...].astype(F32) + mm(gathered, out_w_ref[...])).astype(BF16)
    latent_ref[...] = latent
    lower = latent[:, latent.shape[1] // 2 :]
    for a, b, ref in ((0, 0, h00), (0, 1, h01), (1, 0, h10), (1, 1, h11)):
        pick = table_by_row(halo_ref[0, a, b : b + 1, :], nodes)
        ref[...] = mm_left(pick, lower).astype(BF16)


def mesh_kernel(
    flag_ref, src_ref, dst_ref, latent_ref, cot_ref, b0, b1, b2, b3, u_src_ref, u_dst_ref, u_out_ref, v_in_ref, v_out_ref,
    g0, g1, g2, g3, coupled_grad_ref, lower_grad_ref, halo_table_ref, ends_ref, summed_ref, coupled_ref, hidden_ref, hidden_grad_ref,
    table, slope_s, total, ends,
):
    nodes = latent_ref.shape[0]
    half = latent_ref.shape[1] // 2
    width = b0.shape[0]
    rows = nodes + 4 * width
    upper = latent_ref[:, :half]
    lower = latent_ref[:, half:]
    halo_table_ref[0:nodes, :] = lower
    for k, ref in enumerate((b0, b1, b2, b3)):
        value = ref[...] if k > 1 else jnp.where(flag_ref[k] > 0, ref[...], jnp.zeros_like(ref[...]))
        halo_table_ref[nodes + k * width : nodes + (k + 1) * width, :] = value
    table[0:rows, :] = mm(halo_table_ref[...], u_src_ref[...]).astype(BF16)
    table[rows : rows + nodes, :] = mm(lower, u_dst_ref[...]).astype(BF16)
    for start in range(0, src_ref.shape[1], EDGE_TILE):
        stop = start + EDGE_TILE
        src = src_ref[:, start:stop]
        dst = dst_ref[:, start:stop]
        both = jnp.concatenate([table_by_column(src, rows), table_by_column(dst, nodes)], axis=1)
        act, slope = silu_both(mm(both, table[...]))
        slope_s[start:stop, :] = slope.astype(BF16)
        part = mm(table_by_row(dst, nodes), act.astype(BF16))
        total[...] = part if start == 0 else total[...] + part
    summed = total[...].astype(BF16)
    summed_ref[...] = summed
    coupled = (upper.astype(F32) + mm(summed, u_out_ref[...])).astype(BF16)
    coupled_ref[...] = coupled
    act, slope = silu_both(mm(coupled, v_in_ref[...]))
    hidden_ref[...] = act.astype(BF16)
    upper_cot = cot_ref[:, :half]
    lower_cot = cot_ref[:, half:]
    hidden_grad = (mm_right(lower_cot, v_out_ref[...]) * slope).astype(BF16)
    hidden_grad_ref[...] = hidden_grad
    coupled_grad = (upper_cot.astype(F32) + mm_right(hidden_grad, v_in_ref[...])).astype(BF16)
    coupled_grad_ref[...] = coupled_grad
    summed_grad = mm_right(coupled_grad, u_out_ref[...]).astype(BF16)

    for start in range(0, src_ref.shape[1], EDGE_TILE):
        stop = start + EDGE_TILE
        src = src_ref[:, start:stop]
        dst = dst_ref[:, start:stop]
        grad = mm(table_by_column(dst, nodes), summed_grad) * slope_s[start:stop, :].astype(F32)
        both = jnp.concatenate([table_by_row(src, rows), table_by_row(dst, nodes)], axis=0)
        part = mm(both, grad.astype(BF16))
        ends[...] = part if start == 0 else ends[...] + part
    ends_ref[...] = ends[...].astype(BF16)
    source_grad = ends_ref[0:rows, :]
    target_grad = ends_ref[rows : rows + nodes, :]
    table_grad = mm_right(source_grad, u_src_ref[...])
    lower_grad_ref[...] = lower_cot.astype(F32) + mm_right(target_grad, u_dst_ref[...]) + table_grad[0:nodes, :]
    for k, ref in enumerate((g0, g1, g2, g3)):
        ref[...] = table_grad[nodes + k * width : nodes + (k + 1) * width, :].astype(BF16)


def store_halves(core_ref, mine_ref, other_ref, start, value):
    half = mine_ref.shape[0]
    value = value.astype(BF16)
    done = 0
    while done < value.shape[0]:
        row = start + done
        count = min(value.shape[0] - done, half - row % half)
        piece = value[done : done + count, :]
        here = row % half

        @pl.when(core_ref[0] == row // half)
        def _(piece=piece, here=here, count=count):
            mine_ref[here : here + count, :] = piece

        @pl.when(core_ref[0] != row // half)
        def _(piece=piece, here=here, count=count):
            other_ref[here : here + count, :] = piece

        done += count


def side_by_side(value):
    rows = value.shape[0] // 2
    return jnp.concatenate([value[:rows, :], value[rows:, :]], axis=1)


def mesh_weight_kernel(
    core_ref, halo_table_ref, ends_ref, summed_ref, coupled_ref, hidden_ref, hidden_grad_ref, coupled_grad_ref, cot_ref,
    mine_ref, other_ref,
):
    rows = halo_table_ref.shape[0]
    nodes, half = coupled_ref.shape
    parts = (
        mm_left(halo_table_ref[...], ends_ref[0:rows, :]),
        mm_left(halo_table_ref[0:nodes, :], ends_ref[rows : rows + nodes, :]),
        side_by_side(mm_left(summed_ref[...], coupled_grad_ref[...])),
        mm_left(coupled_ref[...], hidden_grad_ref[...]),
        side_by_side(mm_left(hidden_ref[...], cot_ref[:, half:])),
    )
    start = 0
    for part in parts:
        store_halves(core_ref, mine_ref, other_ref, start, part)
        start += part.shape[0]


def encoder_back_kernel(
    core_ref, flag_ref, src_ref, dst_ref, row_ref, halo_ref, r0, r1, r2, r3, lower_grad_ref, coupled_grad_ref, out_w_ref,
    column_ref, slope0, slope1, gathered_ref, recv_ref, mesh_ref, embed_ref, send_ref, rows_ref,
    rows_grad_ref, g0, g1, g2, g3, mesh_grad_ref, mine_ref, other_ref,
    edge_s, latent_s, nodes_s, sum_send, sum_embed,
):
    nodes, dim = mesh_ref.shape
    rim = g0.shape[1]
    lower_grad = lower_grad_ref[...]
    for a, b, ref in ((0, 0, r0), (0, 1, r1), (1, 0, r2), (1, 1, r3)):
        value = ref[...] if a else jnp.where(flag_ref[b] > 0, ref[...], jnp.zeros_like(ref[...]))
        lower_grad += mm(table_by_row(halo_ref[0, a, b : b + 1, :], nodes), value)
    half = lower_grad.shape[1]
    latent_s[:, :half] = coupled_grad_ref[...]
    latent_s[:, half:] = lower_grad.astype(BF16)
    latent_grad = latent_s[...]
    gathered_grad = mm_right(latent_grad, out_w_ref[...]).astype(BF16)
    rows = column_ref.shape[0]
    for start in range(0, src_ref.shape[1], EDGE_TILE):
        stop = start + EDGE_TILE
        if start < rows:
            by_column = table_by_wide(column_ref[start:stop, :], nodes)
            by_row = table_by_row(row_ref[:, start:stop], nodes)
            slope = slope0[start:stop, :]
        else:
            dst = dst_ref[:, start:stop]
            by_column = table_by_column(dst, nodes)
            by_row = table_by_row(dst, nodes)
            slope = slope1[start - rows : stop - rows, :]
        grad = (mm(by_column, gathered_grad) * slope.astype(F32)).astype(BF16)
        edge_s[start:stop, :] = grad
        part = mm(by_row, grad)
        nodes_s[...] = part if start == 0 else nodes_s[...] + part
    store_halves(core_ref, mine_ref, other_ref, 0, mm_left(gathered_ref[...], latent_grad))
    node_grad = nodes_s[...].astype(BF16)
    store_halves(core_ref, mine_ref, other_ref, dim, mm_left(mesh_ref[...], node_grad))
    mesh_grad_ref[...] = latent_grad.astype(F32) + mm_right(node_grad, recv_ref[...])
    mesh_grad_ref.send()
    extra = src_ref[:, rows:]

    sum_send[...] = jnp.zeros_like(sum_send)
    sum_embed[...] = jnp.zeros_like(sum_embed)

    def back(start):
        here = pl.ds(start, BACK_TILE)
        cols = rows_ref[:, here]
        ids = lax.broadcasted_iota(jnp.int32, (BACK_TILE, extra.shape[1]), 0) + start
        table = jnp.where(ids == extra, 1.0, 0.0).astype(BF16)
        own = edge_s[here, :].astype(F32)
        sender_grad = (own + mm(table, edge_s[rows:, :])).astype(BF16)
        act, slope = silu_both(mm_left(cols, embed_ref[...]))
        embedded_grad = mm_right(sender_grad, send_ref[...]).astype(BF16)
        embed_grad = (embedded_grad.astype(F32) * slope).astype(BF16)
        rows_grad_ref[:, here] = mm_right(embed_ref[...], embed_grad).astype(BF16)
        sum_send[...] += mm_left(act.astype(BF16), sender_grad)
        sum_embed[...] += mm(cols, embed_grad)

    tiles(rows, BACK_TILE, back)
    for k, ref in enumerate((g0, g1, g2, g3)):
        start = rows - (4 - k) * rim
        ref[...] = rows_grad_ref[:, start : start + rim]
    store_halves(core_ref, mine_ref, other_ref, 2 * dim, sum_send[...])
    grad_embed = sum_embed[...]
    pad = jnp.zeros((half - grad_embed.shape[0], dim), F32)
    store_halves(core_ref, mine_ref, other_ref, 3 * dim, jnp.concatenate([grad_embed, pad], axis=0))


def place_kernel(flag_ref, order_ref, rows_ref, in0, in1, in2, in3, own0, own1, grid_grad_ref, all_s):
    rim = in0.shape[1]
    keep = rows_ref.shape[1] - 4 * rim
    all_s[:, 0:keep] = rows_ref[:, 0:keep]
    all_s[:, keep : keep + rim] = jnp.where(flag_ref[0] > 0, in0[...], own0[...])
    all_s[:, keep + rim : keep + 2 * rim] = jnp.where(flag_ref[1] > 0, in1[...], own1[...])
    all_s[:, keep + 2 * rim : keep + 3 * rim] = in2[...]
    all_s[:, keep + 3 * rim : keep + 4 * rim] = in3[...]


    def place(start):
        ids = lax.broadcasted_iota(jnp.int32, (ROW_TILE, order_ref.shape[1]), 0) + start
        table = jnp.where(ids == order_ref[...], 1.0, 0.0).astype(BF16)
        grid_grad_ref[:, pl.ds(start, ROW_TILE)] = mm_right(all_s[...], table).astype(BF16)

    tiles(grid_grad_ref.shape[1], ROW_TILE, place)


def unpack_kernel(a_rows, core_ref, mine_ref, other_ref, embed_ref, send_ref, recv_ref, out_ref, u_src_ref, u_dst_ref, u_out_ref, v_in_ref, v_out_ref):
    first = core_ref[0] == 0

    def read(base, half, start, count):
        pieces = []
        while count > 0:
            here = start % half
            some = min(count, half - here)
            mine = mine_ref[base + here : base + here + some, :]
            other = other_ref[base + here : base + here + some, :]
            pieces.append(jnp.where(first == (start < half), mine, other))
            start += some
            count -= some
        value = pieces[0] if len(pieces) == 1 else jnp.concatenate(pieces, axis=0)
        return value.astype(F32)

    dim, half = v_out_ref.shape
    a_half = a_rows // 2
    b_half = mine_ref.shape[0] - a_half
    for start, ref in ((0, u_src_ref), (half, u_dst_ref), (3 * half, v_in_ref)):
        ref[...] = read(0, a_half, start, half)
        ref.send()
    for start, ref in ((2 * half, u_out_ref), (4 * half, v_out_ref)):
        value = read(0, a_half, start, half)
        ref[0:half, :] = value[:, :half]
        ref[half:, :] = value[:, half:]
        ref.send()
    for start, ref in ((0, out_ref), (dim, recv_ref), (2 * dim, send_ref)):
        ref[...] = read(a_half, b_half, start, dim)
        ref.send()
    ref = embed_ref
    ref[...] = read(a_half, b_half, 3 * dim, half)[0 : ref.shape[0], :]
    ref.send()


def trade(below, above, west, east):
    bands = lax.axis_size(BAND)
    patches = lax.axis_size(PATCH)
    up = [(i, (i + 1) % bands) for i in range(bands)]
    down = [((i + 1) % bands, i) for i in range(bands)]
    right = [(i, (i + 1) % patches) for i in range(patches)]
    left = [((i + 1) % patches, i) for i in range(patches)]
    return (
        lax.ppermute(above, BAND, up),
        lax.ppermute(below, BAND, down),
        lax.ppermute(east, PATCH, right),
        lax.ppermute(west, PATCH, left),
    )


def swap_cores(value):
    return lax.ppermute(value, "core", [(0, 1), (1, 0)])


def body(
    grid_feats, mesh_feats, cotangent, w_embed, w_send, w_recv, w_out, u_src, u_dst, u_out, v_in, v_out,
    send_rows, enc_src, enc_dst, halo_send, mesh_src, mesh_dst,
):
    chans = grid_feats.shape[1]
    grid_rows = grid_feats.shape[0]
    nodes, dim = mesh_feats.shape
    half = dim // 2
    rim = grid_rows // 16
    keep = grid_rows - 4 * rim
    edges = enc_src.shape[1]
    width = halo_send.shape[3]
    table_rows = nodes + 4 * width
    band = lax.axis_index(BAND)
    flags = jnp.stack([band, lax.axis_size(BAND) - 1 - band]).astype(jnp.int32)
    core = lax.axis_index("core").astype(jnp.int32).reshape(1)

    grid_cols = grid_feats.T
    own = call(pick_rim_kernel, [shape((chans, rim), BF16)] * 4, 1, (send_rows, grid_cols))
    arrived = trade(*own)
    outs = [
        shape((chans, keep), BF16), shape((keep, dim), BF16), shape((nodes, dim), BF16),
        shape((grid_rows, LANES), BF16), shape((1, grid_rows), jnp.int32),
    ]
    ins = (send_rows, enc_src, enc_dst, grid_cols, mesh_feats, w_embed, w_send, w_recv)
    keep_rows, keep_sender, node_part, column, row = call(
        keep_kernel, outs, 6, ins, scratch=[pltpu.VMEM((grid_rows, LANES), BF16)]
    )

    outs = [
        shape((chans, grid_rows), BF16), shape((grid_rows, dim), BF16), shape((edges - grid_rows, dim), BF16),
        shape((nodes, dim), BF16), shape((nodes, dim), BF16),
    ] + [shape((width, half), BF16)] * 4
    ins = (
        flags, enc_src, enc_dst, row, halo_send, *arrived, own[0], own[1], w_embed, w_send,
        keep_rows, keep_sender, node_part, column, w_out, mesh_feats,
    )
    all_rows, slope0, slope1, gathered, latent, h00, h01, h10, h11 = call(
        encode_kernel, outs, 12, ins, scalars=1,
        scratch=[pltpu.VMEM((grid_rows + nodes, dim), BF16), pltpu.VMEM((nodes, dim), F32)],
    )

    halos = trade(h00, h01, h10, h11)
    outs = [shape((width, half), BF16)] * 4 + [
        shape((nodes, half), BF16), shape((nodes, half), F32), shape((table_rows, half), BF16),
        shape((table_rows + nodes, dim), BF16), shape((nodes, dim), BF16), shape((nodes, half), BF16),
        shape((nodes, dim), BF16), shape((nodes, dim), BF16),
    ]
    ins = (flags, mesh_src, mesh_dst, latent, cotangent, *halos, u_src, u_dst, u_out, v_in, v_out)
    (g0, g1, g2, g3, coupled_grad, lower_grad, halo_table, ends, summed, coupled, hidden, hidden_grad) = call(
        mesh_kernel, outs, 6, ins, scalars=1,
        scratch=[
            pltpu.VMEM((table_rows + nodes, dim), BF16), pltpu.VMEM((mesh_src.shape[1], dim), BF16),
            pltpu.VMEM((nodes, dim), F32), pltpu.VMEM((table_rows + nodes, dim), F32),
        ],
    )
    returned = trade(g0, g1, g2, g3)
    a_rows = 5 * half
    ins = (core, halo_table, ends, summed, coupled, hidden, hidden_grad, coupled_grad, cotangent)
    a_mine, a_other = call(mesh_weight_kernel, [shape((a_rows // 2, dim), BF16)] * 2, 1, ins, scalars=1)
    a_in = swap_cores(a_other)
    lower_grad, a_mine = lax.optimization_barrier((lower_grad, a_mine))

    b_rows = 3 * dim + half
    outs = [shape((chans, grid_rows), BF16)] + [shape((chans, rim), BF16)] * 4 + [shape((nodes, dim), F32)]
    outs += [shape((b_rows // 2, dim), BF16)] * 2
    ins = (
        core, flags, enc_src, enc_dst, row, halo_send, *returned, lower_grad, coupled_grad, w_out,
        column, slope0, slope1, gathered, w_recv, mesh_feats, w_embed, w_send, all_rows,
    )
    rows_grad, q0, q1, q2, q3, mesh_grad, b_mine, b_other = call(
        encoder_back_kernel, outs, 14, ins, scalars=2, sent=(5,),
        scratch=[
            pltpu.VMEM((edges, dim), BF16), pltpu.VMEM((nodes, dim), BF16), pltpu.VMEM((nodes, dim), F32),
            pltpu.VMEM((dim, dim), F32), pltpu.VMEM((chans, dim), F32),
        ],
    )
    b_in = swap_cores(b_other)
    back = trade(q0, q1, q2, q3)
    patches = lax.axis_size(PATCH)
    packed = (a_rows + b_rows) // 2
    pair = jnp.concatenate([a_mine.astype(F32) + a_in.astype(F32), b_mine.astype(F32) + b_in.astype(F32)], axis=0)
    pair = pair.astype(BF16).reshape(patches, packed // patches, dim)
    parts = lax.all_to_all(pair, PATCH, 0, 0)
    part = jnp.sum(parts.astype(F32), axis=0).astype(BF16)
    part, *back = lax.optimization_barrier((part, *back))
    ins = (flags, send_rows, rows_grad, *back, q0, q1)
    (grid_grad,) = call(
        place_kernel, [shape((chans, grid_rows), BF16)], 5, ins, scalars=1, scratch=[pltpu.VMEM((chans, grid_rows), BF16)]
    )
    away = [part] + [lax.ppermute(part, "z", [(i, (i + k) % 4) for i in range(4)]) for k in (1, 2, 3)]
    away = [piece.astype(F32) for piece in away]
    total = ((away[0] + away[2]) + (away[1] + away[3])).astype(BF16)
    mine = lax.all_to_all(jnp.broadcast_to(total[None], parts.shape), PATCH, 0, 0).reshape(packed, dim)
    mine, grid_grad = lax.optimization_barrier((mine, grid_grad))
    other = swap_cores(mine)
    outs = [shape((chans, dim), F32)] + [shape((dim, dim), F32)] * 3 + [shape((half, dim), F32)] * 2
    outs += [shape((dim, half), F32), shape((half, dim), F32), shape((dim, half), F32)]
    totals = call(functools.partial(unpack_kernel, a_rows), outs, 4, (core, mine, other), scalars=1, sent=tuple(range(9)))
    return (grid_grad.T, mesh_grad, *totals)


def solution(mesh):
    chips = Mesh(mesh.devices.reshape(mesh.shape["band"] // 2, 2, 4, mesh.shape["patch"] // 4), ("z", "core", "y", "x"))
    everywhere = BAND + PATCH
    rows = P(everywhere, None)
    in_specs = (rows,) * 3 + (P(),) * 9 + (rows,) * 3 + (P(everywhere, None, None, None),) + (rows,) * 2
    out_specs = (rows,) * 2 + (P(),) * 9
    return jax.shard_map(body, mesh=chips, in_specs=in_specs, out_specs=out_specs, check_vma=False)
```

```python
import functools

import jax
import jax.numpy as jnp
from jax import lax
from jax.experimental import pallas as pl
from jax.experimental.pallas import tpu as pltpu
from jax.sharding import Mesh
from jax.sharding import PartitionSpec as P

BF16 = jnp.bfloat16
F32 = jnp.float32
LANES = 128
EDGE_TILE = 1024
ROW_TILE = 512
BACK_TILE = 1024
VMEM_LIMIT = 32 * 1024 * 1024
PIECES = 4
BAND = ("z", "core")
PATCH = ("y", "x")


def mm(left, right):
    return lax.dot_general(left, right, (((1,), (0,)), ((), ())), preferred_element_type=F32)


def mm_left(left, right):
    return lax.dot_general(left, right, (((0,), (0,)), ((), ())), preferred_element_type=F32)


def mm_right(left, right):
    return lax.dot_general(left, right, (((1,), (1,)), ((), ())), preferred_element_type=F32)


def table_by_row(index, count):
    n = index.shape[1]
    rows = lax.broadcasted_iota(jnp.int32, (count, n), 0)
    return jnp.where(rows == index, 1.0, 0.0).astype(BF16)


def table_by_column(index, count):
    n = index.shape[1]
    parts = []
    for start in range(0, n, LANES):
        width = min(LANES, n - start)
        piece = jnp.broadcast_to(index[:, start : start + width], (LANES, width))
        column = jnp.transpose(piece)
        wide = jnp.concatenate([column] * (count // LANES), axis=1)
        columns = lax.broadcasted_iota(jnp.int32, (width, count), 1)
        parts.append(jnp.where(wide == columns, 1.0, 0.0).astype(BF16))
    return parts[0] if len(parts) == 1 else jnp.concatenate(parts, axis=0)


def table_by_wide(column, count):
    wide = jnp.concatenate([column.astype(F32)] * (count // LANES), axis=1)
    columns = lax.broadcasted_iota(jnp.int32, wide.shape, 1).astype(F32)
    return jnp.where(wide == columns, 1.0, 0.0).astype(BF16)


def tiles(stop, size, body):
    def step(i, carry):
        body(pl.multiple_of(i * size, size))
        return carry

    lax.fori_loop(0, stop // size, step, 0)


def silu_both(value):
    sigma = 0.5 * jnp.tanh(0.5 * value) + 0.5
    act = value * sigma
    return act, sigma + act * (1.0 - sigma)


class Sent:
    def __init__(self, target, buffer, semaphores):
        self.target, self.buffer, self.semaphores = target, buffer, semaphores
        self.shape = buffer.shape
        self.copies = []

    def __setitem__(self, index, value):
        self.buffer[index] = value

    def __getitem__(self, index):
        return self.buffer[index]

    def send(self, start=0, count=None):
        rows = pl.ds(start, self.shape[0] if count is None else count)
        copy = pltpu.make_async_copy(self.buffer.at[rows], self.target.at[rows], self.semaphores.at[len(self.copies)])
        copy.start()
        self.copies.append(copy)


def call(kernel, out_shape, work, args, scalars=0, sent=(), scratch=()):
    outs = list(out_shape)
    buffers = [pltpu.VMEM(outs[k].shape, outs[k].dtype) for k in sent]
    buffers += [pltpu.SemaphoreType.DMA((PIECES,)) for _ in sent]

    def run(*refs):
        ins, results, rest = refs[: len(args)], list(refs[len(args) : len(args) + len(outs)]), refs[len(args) + len(outs) :]
        for k, place in enumerate(sent):
            results[place] = Sent(results[place], rest[k], rest[len(sent) + k])
        kernel(*ins, *results, *rest[len(buffers) :])
        for place in sent:
            for copy in results[place].copies:
                copy.wait()

    spaces = [pltpu.SMEM] * scalars + [pltpu.VMEM] * (len(args) - scalars)
    return pl.pallas_call(
        run,
        out_shape=outs,
        in_specs=[pl.BlockSpec(memory_space=space) for space in spaces],
        out_specs=[pl.BlockSpec(memory_space=pl.ANY if k in sent else pltpu.VMEM) for k in range(len(outs))],
        scratch_shapes=buffers + list(scratch),
        cost_estimate=pl.CostEstimate(flops=int(work * 1e9), bytes_accessed=int(work * 1e6), transcendentals=0),
        compiler_params=pltpu.CompilerParams(vmem_limit_bytes=VMEM_LIMIT),
    )(*args)


def shape(dims, kind):
    return jax.ShapeDtypeStruct(tuple(dims), kind)


def pick_rim_kernel(order_ref, grid_ref, *out_refs):
    rim = out_refs[0].shape[1]
    keep = order_ref.shape[1] - 4 * rim
    table = table_by_row(order_ref[:, keep:], grid_ref.shape[1])
    picked = mm(grid_ref[...], table).astype(BF16)
    for k in range(4):
        out_refs[k][...] = picked[:, k * rim : (k + 1) * rim]


def keep_kernel(
    order_ref, src_ref, dst_ref, grid_ref, mesh_ref, embed_ref, send_ref, recv_ref,
    rows_ref, sender_ref, node_ref, column_ref, row_ref, dst_s,
):
    keep = rows_ref.shape[1]
    rows = order_ref.shape[1]
    for start in range(0, rows, LANES):
        piece = jnp.broadcast_to(dst_ref[:, start : start + LANES], (LANES, LANES))
        dst_s[start : start + LANES, :] = jnp.transpose(piece).astype(F32).astype(BF16)
    first = src_ref[:, 0:rows]


    def sort(start):
        ids = lax.broadcasted_iota(jnp.int32, (ROW_TILE, rows), 0) + start
        table = jnp.where(ids == first, 1.0, 0.0).astype(BF16)
        column = mm(table, dst_s[...])
        column_ref[pl.ds(start, ROW_TILE), :] = column.astype(BF16)
        for k in range(0, ROW_TILE, LANES):
            turned = jnp.transpose(column[k : k + LANES, :])
            row_ref[:, pl.ds(pl.multiple_of(start + k, LANES), LANES)] = turned[0:1, :].astype(jnp.int32)

    tiles(rows, ROW_TILE, sort)
    for start in range(0, keep, ROW_TILE):
        stop = start + ROW_TILE
        table = table_by_row(order_ref[:, start:stop], grid_ref.shape[1])
        cols = mm(grid_ref[...], table).astype(BF16)
        rows_ref[:, start:stop] = cols
        embedded = silu_both(mm_left(cols, embed_ref[...]))[0].astype(BF16)
        sender_ref[start:stop, :] = mm(embedded, send_ref[...]).astype(BF16)
    node_ref[...] = mm(mesh_ref[...], recv_ref[...]).astype(BF16)


def encode_kernel(
    flag_ref, src_ref, dst_ref, row_ref, halo_ref, in0, in1, in2, in3, own0, own1, embed_ref, send_ref,
    keep_rows_ref, sender_ref, node_ref, column_ref, out_w_ref, mesh_ref,
    rows_ref, slope0, slope1, gathered_ref, latent_ref, h00, h01, h10, h11,
    table, total,
):
    keep = sender_ref.shape[0]
    rim = in0.shape[1]
    rows = keep + 4 * rim
    nodes = node_ref.shape[0]
    rows_ref[:, 0:keep] = keep_rows_ref[...]
    rows_ref[:, keep : keep + rim] = jnp.where(flag_ref[0] > 0, in0[...], own0[...])
    rows_ref[:, keep + rim : keep + 2 * rim] = jnp.where(flag_ref[1] > 0, in1[...], own1[...])
    rows_ref[:, keep + 2 * rim : keep + 3 * rim] = in2[...]
    rows_ref[:, keep + 3 * rim : rows] = in3[...]
    embedded = silu_both(mm_left(rows_ref[:, keep:], embed_ref[...]))[0].astype(BF16)
    table[keep:rows, :] = mm(embedded, send_ref[...]).astype(BF16)
    table[0:keep, :] = sender_ref[...]
    table[rows : rows + nodes, :] = node_ref[...]
    for start in range(0, src_ref.shape[1], EDGE_TILE):
        stop = start + EDGE_TILE
        if start < rows:
            node = mm(table_by_wide(column_ref[start:stop, :], nodes), node_ref[...])
            value = table[start:stop, :].astype(F32) + node
            by_row = table_by_row(row_ref[:, start:stop], nodes)
        else:
            src = src_ref[:, start:stop]
            dst = dst_ref[:, start:stop]
            both = jnp.concatenate([table_by_column(src, rows), table_by_column(dst, nodes)], axis=1)
            value = mm(both, table[...])
            by_row = table_by_row(dst, nodes)
        act, slope = silu_both(value)
        ref, base = (slope0, 0) if start < rows else (slope1, rows)
        ref[start - base : stop - base, :] = slope.astype(BF16)
        part = mm(by_row, act.astype(BF16))
        total[...] = part if start == 0 else total[...] + part
    gathered = total[...].astype(BF16)
    gathered_ref[...] = gathered
    latent = (mesh_ref[...].astype(F32) + mm(gathered, out_w_ref[...])).astype(BF16)
    latent_ref[...] = latent
    lower = latent[:, latent.shape[1] // 2 :]
    for a, b, ref in ((0, 0, h00), (0, 1, h01), (1, 0, h10), (1, 1, h11)):
        pick = table_by_row(halo_ref[0, a, b : b + 1, :], nodes)
        ref[...] = mm_left(pick, lower).astype(BF16)


def mesh_kernel(
    flag_ref, src_ref, dst_ref, latent_ref, cot_ref, b0, b1, b2, b3, u_src_ref, u_dst_ref, u_out_ref, v_in_ref, v_out_ref,
    g0, g1, g2, g3, coupled_grad_ref, lower_grad_ref, halo_table_ref, ends_ref, summed_ref, coupled_ref, hidden_ref, hidden_grad_ref,
    table, slope_s, total, ends,
):
    nodes = latent_ref.shape[0]
    half = latent_ref.shape[1] // 2
    width = b0.shape[0]
    rows = nodes + 4 * width
    upper = latent_ref[:, :half]
    lower = latent_ref[:, half:]
    halo_table_ref[0:nodes, :] = lower
    for k, ref in enumerate((b0, b1, b2, b3)):
        value = ref[...] if k > 1 else jnp.where(flag_ref[k] > 0, ref[...], jnp.zeros_like(ref[...]))
        halo_table_ref[nodes + k * width : nodes + (k + 1) * width, :] = value
    table[0:rows, :] = mm(halo_table_ref[...], u_src_ref[...]).astype(BF16)
    table[rows : rows + nodes, :] = mm(lower, u_dst_ref[...]).astype(BF16)
    for start in range(0, src_ref.shape[1], EDGE_TILE):
        stop = start + EDGE_TILE
        src = src_ref[:, start:stop]
        dst = dst_ref[:, start:stop]
        both = jnp.concatenate([table_by_column(src, rows), table_by_column(dst, nodes)], axis=1)
        act, slope = silu_both(mm(both, table[...]))
        slope_s[start:stop, :] = slope.astype(BF16)
        part = mm(table_by_row(dst, nodes), act.astype(BF16))
        total[...] = part if start == 0 else total[...] + part
    summed = total[...].astype(BF16)
    summed_ref[...] = summed
    coupled = (upper.astype(F32) + mm(summed, u_out_ref[...])).astype(BF16)
    coupled_ref[...] = coupled
    act, slope = silu_both(mm(coupled, v_in_ref[...]))
    hidden_ref[...] = act.astype(BF16)
    upper_cot = cot_ref[:, :half]
    lower_cot = cot_ref[:, half:]
    hidden_grad = (mm_right(lower_cot, v_out_ref[...]) * slope).astype(BF16)
    hidden_grad_ref[...] = hidden_grad
    coupled_grad = (upper_cot.astype(F32) + mm_right(hidden_grad, v_in_ref[...])).astype(BF16)
    coupled_grad_ref[...] = coupled_grad
    summed_grad = mm_right(coupled_grad, u_out_ref[...]).astype(BF16)

    for start in range(0, src_ref.shape[1], EDGE_TILE):
        stop = start + EDGE_TILE
        src = src_ref[:, start:stop]
        dst = dst_ref[:, start:stop]
        grad = mm(table_by_column(dst, nodes), summed_grad) * slope_s[start:stop, :].astype(F32)
        both = jnp.concatenate([table_by_row(src, rows), table_by_row(dst, nodes)], axis=0)
        part = mm(both, grad.astype(BF16))
        ends[...] = part if start == 0 else ends[...] + part
    ends_ref[...] = ends[...].astype(BF16)
    source_grad = ends_ref[0:rows, :]
    target_grad = ends_ref[rows : rows + nodes, :]
    table_grad = mm_right(source_grad, u_src_ref[...])
    lower_grad_ref[...] = lower_cot.astype(F32) + mm_right(target_grad, u_dst_ref[...]) + table_grad[0:nodes, :]
    for k, ref in enumerate((g0, g1, g2, g3)):
        ref[...] = table_grad[nodes + k * width : nodes + (k + 1) * width, :].astype(BF16)


def store_halves(core_ref, mine_ref, other_ref, start, value):
    half = mine_ref.shape[0]
    value = value.astype(BF16)
    done = 0
    while done < value.shape[0]:
        row = start + done
        count = min(value.shape[0] - done, half - row % half)
        piece = value[done : done + count, :]
        here = row % half

        @pl.when(core_ref[0] == row // half)
        def _(piece=piece, here=here, count=count):
            mine_ref[here : here + count, :] = piece

        @pl.when(core_ref[0] != row // half)
        def _(piece=piece, here=here, count=count):
            other_ref[here : here + count, :] = piece

        done += count


def side_by_side(value):
    rows = value.shape[0] // 2
    return jnp.concatenate([value[:rows, :], value[rows:, :]], axis=1)


def mesh_weight_kernel(
    core_ref, halo_table_ref, ends_ref, summed_ref, coupled_ref, hidden_ref, hidden_grad_ref, coupled_grad_ref, cot_ref,
    mine_ref, other_ref,
):
    rows = halo_table_ref.shape[0]
    nodes, half = coupled_ref.shape
    parts = (
        mm_left(halo_table_ref[...], ends_ref[0:rows, :]),
        mm_left(halo_table_ref[0:nodes, :], ends_ref[rows : rows + nodes, :]),
        side_by_side(mm_left(summed_ref[...], coupled_grad_ref[...])),
        mm_left(coupled_ref[...], hidden_grad_ref[...]),
        side_by_side(mm_left(hidden_ref[...], cot_ref[:, half:])),
    )
    start = 0
    for part in parts:
        store_halves(core_ref, mine_ref, other_ref, start, part)
        start += part.shape[0]


def encoder_back_kernel(
    core_ref, flag_ref, src_ref, dst_ref, row_ref, halo_ref, r0, r1, r2, r3, lower_grad_ref, coupled_grad_ref, out_w_ref,
    column_ref, slope0, slope1, gathered_ref, recv_ref, mesh_ref, embed_ref, send_ref, rows_ref,
    rows_grad_ref, g0, g1, g2, g3, mesh_grad_ref, mine_ref, other_ref,
    edge_s, latent_s, nodes_s, sum_send, sum_embed,
):
    nodes, dim = mesh_ref.shape
    rim = g0.shape[1]
    lower_grad = lower_grad_ref[...]
    for a, b, ref in ((0, 0, r0), (0, 1, r1), (1, 0, r2), (1, 1, r3)):
        value = ref[...] if a else jnp.where(flag_ref[b] > 0, ref[...], jnp.zeros_like(ref[...]))
        lower_grad += mm(table_by_row(halo_ref[0, a, b : b + 1, :], nodes), value)
    half = lower_grad.shape[1]
    latent_s[:, :half] = coupled_grad_ref[...]
    latent_s[:, half:] = lower_grad.astype(BF16)
    latent_grad = latent_s[...]
    gathered_grad = mm_right(latent_grad, out_w_ref[...]).astype(BF16)
    rows = column_ref.shape[0]
    for start in range(0, src_ref.shape[1], EDGE_TILE):
        stop = start + EDGE_TILE
        if start < rows:
            by_column = table_by_wide(column_ref[start:stop, :], nodes)
            by_row = table_by_row(row_ref[:, start:stop], nodes)
            slope = slope0[start:stop, :]
        else:
            dst = dst_ref[:, start:stop]
            by_column = table_by_column(dst, nodes)
            by_row = table_by_row(dst, nodes)
            slope = slope1[start - rows : stop - rows, :]
        grad = (mm(by_column, gathered_grad) * slope.astype(F32)).astype(BF16)
        edge_s[start:stop, :] = grad
        part = mm(by_row, grad)
        nodes_s[...] = part if start == 0 else nodes_s[...] + part
    store_halves(core_ref, mine_ref, other_ref, 0, mm_left(gathered_ref[...], latent_grad))
    node_grad = nodes_s[...].astype(BF16)
    store_halves(core_ref, mine_ref, other_ref, dim, mm_left(mesh_ref[...], node_grad))
    mesh_grad_ref[...] = latent_grad.astype(F32) + mm_right(node_grad, recv_ref[...])
    mesh_grad_ref.send()
    extra = src_ref[:, rows:]

    sum_send[...] = jnp.zeros_like(sum_send)
    sum_embed[...] = jnp.zeros_like(sum_embed)

    def back(start):
        here = pl.ds(start, BACK_TILE)
        cols = rows_ref[:, here]
        ids = lax.broadcasted_iota(jnp.int32, (BACK_TILE, extra.shape[1]), 0) + start
        table = jnp.where(ids == extra, 1.0, 0.0).astype(BF16)
        own = edge_s[here, :].astype(F32)
        sender_grad = (own + mm(table, edge_s[rows:, :])).astype(BF16)
        act, slope = silu_both(mm_left(cols, embed_ref[...]))
        embedded_grad = mm_right(sender_grad, send_ref[...]).astype(BF16)
        embed_grad = (embedded_grad.astype(F32) * slope).astype(BF16)
        rows_grad_ref[:, here] = mm_right(embed_ref[...], embed_grad).astype(BF16)
        sum_send[...] += mm_left(act.astype(BF16), sender_grad)
        sum_embed[...] += mm(cols, embed_grad)

    tiles(rows, BACK_TILE, back)
    for k, ref in enumerate((g0, g1, g2, g3)):
        start = rows - (4 - k) * rim
        ref[...] = rows_grad_ref[:, start : start + rim]
    store_halves(core_ref, mine_ref, other_ref, 2 * dim, sum_send[...])
    grad_embed = sum_embed[...]
    pad = jnp.zeros((half - grad_embed.shape[0], dim), F32)
    store_halves(core_ref, mine_ref, other_ref, 3 * dim, jnp.concatenate([grad_embed, pad], axis=0))


def place_kernel(flag_ref, order_ref, rows_ref, in0, in1, in2, in3, own0, own1, grid_grad_ref, all_s):
    rim = in0.shape[1]
    keep = rows_ref.shape[1] - 4 * rim
    all_s[:, 0:keep] = rows_ref[:, 0:keep]
    all_s[:, keep : keep + rim] = jnp.where(flag_ref[0] > 0, in0[...], own0[...])
    all_s[:, keep + rim : keep + 2 * rim] = jnp.where(flag_ref[1] > 0, in1[...], own1[...])
    all_s[:, keep + 2 * rim : keep + 3 * rim] = in2[...]
    all_s[:, keep + 3 * rim : keep + 4 * rim] = in3[...]


    def place(start):
        ids = lax.broadcasted_iota(jnp.int32, (ROW_TILE, order_ref.shape[1]), 0) + start
        table = jnp.where(ids == order_ref[...], 1.0, 0.0).astype(BF16)
        grid_grad_ref[:, pl.ds(start, ROW_TILE)] = mm_right(all_s[...], table).astype(BF16)

    tiles(grid_grad_ref.shape[1], ROW_TILE, place)


def unpack_kernel(a_rows, core_ref, mine_ref, other_ref, embed_ref, send_ref, recv_ref, out_ref, u_src_ref, u_dst_ref, u_out_ref, v_in_ref, v_out_ref):
    first = core_ref[0] == 0

    def read(base, half, start, count):
        pieces = []
        while count > 0:
            here = start % half
            some = min(count, half - here)
            mine = mine_ref[base + here : base + here + some, :]
            other = other_ref[base + here : base + here + some, :]
            pieces.append(jnp.where(first == (start < half), mine, other))
            start += some
            count -= some
        value = pieces[0] if len(pieces) == 1 else jnp.concatenate(pieces, axis=0)
        return value.astype(F32)

    dim, half = v_out_ref.shape
    a_half = a_rows // 2
    b_half = mine_ref.shape[0] - a_half
    for start, ref in ((0, u_src_ref), (half, u_dst_ref), (3 * half, v_in_ref)):
        ref[...] = read(0, a_half, start, half)
        ref.send()
    for start, ref in ((2 * half, u_out_ref), (4 * half, v_out_ref)):
        value = read(0, a_half, start, half)
        ref[0:half, :] = value[:, :half]
        ref[half:, :] = value[:, half:]
        ref.send()
    for start, ref in ((0, out_ref), (dim, recv_ref), (2 * dim, send_ref)):
        ref[...] = read(a_half, b_half, start, dim)
        ref.send()
    ref = embed_ref
    ref[...] = read(a_half, b_half, 3 * dim, half)[0 : ref.shape[0], :]
    ref.send()


def trade(below, above, west, east):
    bands = lax.axis_size(BAND)
    patches = lax.axis_size(PATCH)
    up = [(i, (i + 1) % bands) for i in range(bands)]
    down = [((i + 1) % bands, i) for i in range(bands)]
    right = [(i, (i + 1) % patches) for i in range(patches)]
    left = [((i + 1) % patches, i) for i in range(patches)]
    return (
        lax.ppermute(above, BAND, up),
        lax.ppermute(below, BAND, down),
        lax.ppermute(east, PATCH, right),
        lax.ppermute(west, PATCH, left),
    )


def swap_cores(value):
    return lax.ppermute(value, "core", [(0, 1), (1, 0)])


def body(
    grid_feats, mesh_feats, cotangent, w_embed, w_send, w_recv, w_out, u_src, u_dst, u_out, v_in, v_out,
    send_rows, enc_src, enc_dst, halo_send, mesh_src, mesh_dst,
):
    chans = grid_feats.shape[1]
    grid_rows = grid_feats.shape[0]
    nodes, dim = mesh_feats.shape
    half = dim // 2
    rim = grid_rows // 16
    keep = grid_rows - 4 * rim
    edges = enc_src.shape[1]
    width = halo_send.shape[3]
    table_rows = nodes + 4 * width
    band = lax.axis_index(BAND)
    flags = jnp.stack([band, lax.axis_size(BAND) - 1 - band]).astype(jnp.int32)
    core = lax.axis_index("core").astype(jnp.int32).reshape(1)

    grid_cols = grid_feats.T
    own = call(pick_rim_kernel, [shape((chans, rim), BF16)] * 4, 1, (send_rows, grid_cols))
    arrived = trade(*own)
    outs = [
        shape((chans, keep), BF16), shape((keep, dim), BF16), shape((nodes, dim), BF16),
        shape((grid_rows, LANES), BF16), shape((1, grid_rows), jnp.int32),
    ]
    ins = (send_rows, enc_src, enc_dst, grid_cols, mesh_feats, w_embed, w_send, w_recv)
    keep_rows, keep_sender, node_part, column, row = call(
        keep_kernel, outs, 6, ins, scratch=[pltpu.VMEM((grid_rows, LANES), BF16)]
    )

    outs = [
        shape((chans, grid_rows), BF16), shape((grid_rows, dim), BF16), shape((edges - grid_rows, dim), BF16),
        shape((nodes, dim), BF16), shape((nodes, dim), BF16),
    ] + [shape((width, half), BF16)] * 4
    ins = (
        flags, enc_src, enc_dst, row, halo_send, *arrived, own[0], own[1], w_embed, w_send,
        keep_rows, keep_sender, node_part, column, w_out, mesh_feats,
    )
    all_rows, slope0, slope1, gathered, latent, h00, h01, h10, h11 = call(
        encode_kernel, outs, 12, ins, scalars=1,
        scratch=[pltpu.VMEM((grid_rows + nodes, dim), BF16), pltpu.VMEM((nodes, dim), F32)],
    )

    halos = trade(h00, h01, h10, h11)
    outs = [shape((width, half), BF16)] * 4 + [
        shape((nodes, half), BF16), shape((nodes, half), F32), shape((table_rows, half), BF16),
        shape((table_rows + nodes, dim), BF16), shape((nodes, dim), BF16), shape((nodes, half), BF16),
        shape((nodes, dim), BF16), shape((nodes, dim), BF16),
    ]
    ins = (flags, mesh_src, mesh_dst, latent, cotangent, *halos, u_src, u_dst, u_out, v_in, v_out)
    (g0, g1, g2, g3, coupled_grad, lower_grad, halo_table, ends, summed, coupled, hidden, hidden_grad) = call(
        mesh_kernel, outs, 6, ins, scalars=1,
        scratch=[
            pltpu.VMEM((table_rows + nodes, dim), BF16), pltpu.VMEM((mesh_src.shape[1], dim), BF16),
            pltpu.VMEM((nodes, dim), F32), pltpu.VMEM((table_rows + nodes, dim), F32),
        ],
    )
    returned = trade(g0, g1, g2, g3)
    a_rows = 5 * half
    ins = (core, halo_table, ends, summed, coupled, hidden, hidden_grad, coupled_grad, cotangent)
    a_mine, a_other = call(mesh_weight_kernel, [shape((a_rows // 2, dim), BF16)] * 2, 1, ins, scalars=1)
    a_in = swap_cores(a_other)
    lower_grad, a_mine = lax.optimization_barrier((lower_grad, a_mine))

    b_rows = 3 * dim + half
    outs = [shape((chans, grid_rows), BF16)] + [shape((chans, rim), BF16)] * 4 + [shape((nodes, dim), F32)]
    outs += [shape((b_rows // 2, dim), BF16)] * 2
    ins = (
        core, flags, enc_src, enc_dst, row, halo_send, *returned, lower_grad, coupled_grad, w_out,
        column, slope0, slope1, gathered, w_recv, mesh_feats, w_embed, w_send, all_rows,
    )
    rows_grad, q0, q1, q2, q3, mesh_grad, b_mine, b_other = call(
        encoder_back_kernel, outs, 14, ins, scalars=2, sent=(5,),
        scratch=[
            pltpu.VMEM((edges, dim), BF16), pltpu.VMEM((nodes, dim), BF16), pltpu.VMEM((nodes, dim), F32),
            pltpu.VMEM((dim, dim), F32), pltpu.VMEM((chans, dim), F32),
        ],
    )
    b_in = swap_cores(b_other)
    patches = lax.axis_size(PATCH)
    packed = (a_rows + b_rows) // 2
    pair = jnp.concatenate([a_mine.astype(F32) + a_in.astype(F32), b_mine.astype(F32) + b_in.astype(F32)], axis=0)
    pair = pair.astype(BF16).reshape(patches, packed // patches, dim)
    parts = lax.all_to_all(pair, PATCH, 0, 0)
    part = jnp.sum(parts.astype(F32), axis=0).astype(BF16)
    away = [part] + [lax.ppermute(part, "z", [(i, (i + k) % 4) for i in range(4)]) for k in (1, 2, 3)]
    away = [piece.astype(F32) for piece in away]
    total = ((away[0] + away[2]) + (away[1] + away[3])).astype(BF16)
    total, q0, q1, q2, q3 = lax.optimization_barrier((total, q0, q1, q2, q3))
    back = trade(q0, q1, q2, q3)
    mine = lax.all_to_all(jnp.broadcast_to(total[None], parts.shape), PATCH, 0, 0).reshape(packed, dim)
    mine, *back = lax.optimization_barrier((mine, *back))
    other = swap_cores(mine)
    ins = (flags, send_rows, rows_grad, *back, q0, q1)
    (grid_grad,) = call(
        place_kernel, [shape((chans, grid_rows), BF16)], 5, ins, scalars=1, scratch=[pltpu.VMEM((chans, grid_rows), BF16)]
    )
    outs = [shape((chans, dim), F32)] + [shape((dim, dim), F32)] * 3 + [shape((half, dim), F32)] * 2
    outs += [shape((dim, half), F32), shape((half, dim), F32), shape((dim, half), F32)]
    totals = call(functools.partial(unpack_kernel, a_rows), outs, 4, (core, mine, other), scalars=1, sent=tuple(range(9)))
    return (grid_grad.T, mesh_grad, *totals)


def solution(mesh):
    chips = Mesh(mesh.devices.reshape(mesh.shape["band"] // 2, 2, 4, mesh.shape["patch"] // 4), ("z", "core", "y", "x"))
    everywhere = BAND + PATCH
    rows = P(everywhere, None)
    in_specs = (rows,) * 3 + (P(),) * 9 + (rows,) * 3 + (P(everywhere, None, None, None),) + (rows,) * 2
    out_specs = (rows,) * 2 + (P(),) * 9
    return jax.shard_map(body, mesh=chips, in_specs=in_specs, out_specs=out_specs, check_vma=False)
```
